32 devices in a mesh: dp: 2 (over x), blk: 4 (over y, core), ulysses: 4 (over z).
Axes of the slice: x: 2, y: 2, z: 4, core: 2. Of those that a mesh axis runs over, the one named last changes fastest.
Arguments:
- tokens: bfloat16 [8192, 2304], P(('dp', 'blk', 'ulysses')), may hold values from -6 to 6
- query_weight: bfloat16 [2304, 2048], P(('dp', 'blk')), may hold values from -0.125 to 0.125
- key_projection: bfloat16 [2304, 1024], P(('dp', 'blk')), may hold values from -0.125 to 0.125
- value_projection: bfloat16 [2304, 1024], P(('dp', 'blk')), may hold values from -0.125 to 0.125
- out_weight: bfloat16 [2048, 2304], P(('dp', 'blk')), may hold values from -0.125 to 0.125
- gate_weight: bfloat16 [2304, 9216], P(('dp', 'blk')), may hold values from -0.125 to 0.125
- up_weight: bfloat16 [2304, 9216], P(('dp', 'blk')), may hold values from -0.125 to 0.125
- down_weight: bfloat16 [9216, 2304], P(('dp', 'blk')), may hold values from -0.0625 to 0.0625
- attn_in_gain: float32 [2304], replicated, may hold values from 0.5 to 1.5
- attn_out_gain: float32 [2304], replicated, may hold values from 0.5 to 1.5
- feed_in_gain: float32 [2304], replicated, may hold values from 0.5 to 1.5
- feed_out_gain: float32 [2304], replicated, may hold values from 0.5 to 1.5
- adapt_heads_in: bfloat16 [8, 3, 16, 2304], replicated, may hold values from -0.125 to 0.125
- adapt_query_out: bfloat16 [8, 16, 2048], replicated, may hold values from -0.75 to 0.75
- adapter_key_value_second: bfloat16 [8, 2, 16, 1024], replicated, may hold values from -0.75 to 0.75
- adapt_mix_in: bfloat16 [8, 16, 2048], replicated, may hold values from -0.125 to 0.125
- adapt_mix_out: bfloat16 [8, 16, 2304], replicated, may hold values from -0.75 to 0.75
- adapt_feed_in: bfloat16 [8, 2, 16, 2304], replicated, may hold values from -0.125 to 0.125
- adapt_feed_out: bfloat16 [8, 2, 16, 9216], replicated, may hold values from -0.75 to 0.75
- adapt_down_in: bfloat16 [8, 16, 9216], replicated, may hold values from -0.0625 to 0.0625
- adapt_down_out: bfloat16 [8, 16, 2304], replicated, may hold values from -0.75 to 0.75
- adapter_ids: int32 [2, 9], P('dp'), may hold values from 0 to 7
- cotangent: bfloat16 [8192, 2304], P(('dp', 'blk', 'ulysses')), may hold values from -6 to 6
Outputs:
- layer_out: bfloat16 [8192, 2304], P(('dp', 'blk', 'ulysses'))
- tokens_grad: float32 [8192, 2304], P(('dp', 'blk', 'ulysses'))
- grad_heads_in: float32 [8, 3, 16, 2304], replicated
- grad_query_out: float32 [8, 16, 2048], replicated
- grad_kv_out: float32 [8, 2, 16, 1024], replicated
- grad_mix_in: float32 [8, 16, 2048], replicated
- grad_mix_out: float32 [8, 16, 2304], replicated
- grad_feed_in: float32 [8, 2, 16, 2304], replicated
- grad_feed_out: float32 [8, 2, 16, 9216], replicated
- grad_down_in: float32 [8, 16, 9216], replicated
- grad_down_out: float32 [8, 16, 2304], replicated
The draws below stay inside these ranges and needn't reach their ends.
All inputs are finite; a program needn't handle non-finite values.
Results may differ from the reference program's by a relative error of at most 0.025.
Values may be sent and summed in bfloat16 or wider, within the bound.
A program may use at most 384 MiB of HBM per device.

```python
import math
import jax
import jax.numpy as jnp
from jax import lax

MODEL_WIDTH = 2304
HEADS = 8
KV_HEADS = 4
HEAD = 256
FF = 9216
ADAPTER_RANK = 16
ADAPTER_COUNT = 8
PROMPT = 2048
CONT = 256
CONTS = 8
HQ = 2048
KEY_VALUE_WIDTH = 1024
GROUP = 4096
GROUPS = 2
TOKENS = 8192


def with_ends(array, own_key, least, top_value):
    dims = array.shape
    spot = [jax.random.randint(jax.random.fold_in(own_key, axis), (), 0, dims[axis]) for axis in range(len(dims))]
    array = array.at[tuple(spot)].set(least)
    longest = dims.index(max(dims))
    spot[longest] = (spot[longest] + 1) % dims[longest]
    return array.at[tuple(spot)].set(top_value)


def steps_of(key, dims, cuts, smallest, high):
    def one(axis_at, shards_of):
        draws = jax.random.uniform(jax.random.fold_in(jax.random.fold_in(key, 6), axis_at), (shards_of,), jnp.float32, smallest / len(cuts), high / len(cuts))
        return jnp.repeat(jnp.exp(draws), dims[axis_at] // shards_of).reshape((-1,) + (1,) * (len(dims) - axis_at - 1))

    gain = one(*cuts[0])
    for cut in cuts[1:]:
        gain = gain * one(*cut)
    return gain


def bell_draw(stream_key, dims, spread, limit, pieces=(), held_as=jnp.bfloat16):
    factor_of = steps_of(stream_key, dims, pieces, -0.22, 0.18) if pieces else 1.0
    entries = jax.random.normal(stream_key, dims, jnp.float32) * spread * factor_of
    return jnp.minimum(jnp.maximum(entries, -limit), limit).astype(held_as)


def setup_inputs(seed: int = 0) -> dict:
    streams_of = jax.random.split(jax.random.key(seed), 24)
    return {
        "tokens": bell_draw(streams_of[0], (TOKENS, MODEL_WIDTH), 1.0, 6.0, ((0, 32),)),
        "query_weight": bell_draw(streams_of[1], (MODEL_WIDTH, HQ), MODEL_WIDTH ** -0.5, 0.125, ((0, 8),)),
        "key_projection": bell_draw(streams_of[2], (MODEL_WIDTH, KEY_VALUE_WIDTH), MODEL_WIDTH ** -0.5, 0.125, ((0, 8),)),
        "value_projection": bell_draw(streams_of[3], (MODEL_WIDTH, KEY_VALUE_WIDTH), MODEL_WIDTH ** -0.5, 0.125, ((0, 8),)),
        "out_weight": bell_draw(streams_of[4], (HQ, MODEL_WIDTH), HQ ** -0.5, 0.125, ((0, 8),)),
        "gate_weight": bell_draw(streams_of[5], (MODEL_WIDTH, FF), MODEL_WIDTH ** -0.5, 0.125, ((0, 8),)),
        "up_weight": bell_draw(streams_of[6], (MODEL_WIDTH, FF), MODEL_WIDTH ** -0.5, 0.125, ((0, 8),)),
        "down_weight": bell_draw(streams_of[7], (FF, MODEL_WIDTH), FF ** -0.5, 0.0625, ((0, 8),)),
        "attn_in_gain": jnp.clip(1.0 + 0.1 * jax.random.normal(streams_of[8], (MODEL_WIDTH,), jnp.float32), 0.5, 1.5),
        "attn_out_gain": jnp.clip(1.0 + 0.1 * jax.random.normal(streams_of[9], (MODEL_WIDTH,), jnp.float32), 0.5, 1.5),
        "feed_in_gain": jnp.clip(1.0 + 0.1 * jax.random.normal(streams_of[10], (MODEL_WIDTH,), jnp.float32), 0.5, 1.5),
        "feed_out_gain": jnp.clip(1.0 + 0.1 * jax.random.normal(streams_of[11], (MODEL_WIDTH,), jnp.float32), 0.5, 1.5),
        "adapt_heads_in": bell_draw(streams_of[12], (ADAPTER_COUNT, 3, ADAPTER_RANK, MODEL_WIDTH), MODEL_WIDTH ** -0.5, 0.125),
        "adapt_query_out": bell_draw(streams_of[13], (ADAPTER_COUNT, ADAPTER_RANK, HQ), (4 * ADAPTER_RANK) ** -0.5, 0.75),
        "adapter_key_value_second": bell_draw(streams_of[14], (ADAPTER_COUNT, 2, ADAPTER_RANK, KEY_VALUE_WIDTH), (4 * ADAPTER_RANK) ** -0.5, 0.75),
        "adapt_mix_in": bell_draw(streams_of[15], (ADAPTER_COUNT, ADAPTER_RANK, HQ), HQ ** -0.5, 0.125),
        "adapt_mix_out": bell_draw(streams_of[16], (ADAPTER_COUNT, ADAPTER_RANK, MODEL_WIDTH), (4 * ADAPTER_RANK) ** -0.5, 0.75),
        "adapt_feed_in": bell_draw(streams_of[17], (ADAPTER_COUNT, 2, ADAPTER_RANK, MODEL_WIDTH), MODEL_WIDTH ** -0.5, 0.125),
        "adapt_feed_out": bell_draw(streams_of[18], (ADAPTER_COUNT, 2, ADAPTER_RANK, FF), (4 * ADAPTER_RANK) ** -0.5, 0.75),
        "adapt_down_in": bell_draw(streams_of[19], (ADAPTER_COUNT, ADAPTER_RANK, FF), FF ** -0.5, 0.0625),
        "adapt_down_out": bell_draw(streams_of[20], (ADAPTER_COUNT, ADAPTER_RANK, MODEL_WIDTH), (4 * ADAPTER_RANK) ** -0.5, 0.75),
        "adapter_ids": with_ends(jax.random.randint(streams_of[21], (GROUPS, CONTS + 1), 0, ADAPTER_COUNT), jax.random.fold_in(streams_of[21], 1), 0, ADAPTER_COUNT - 1).astype(jnp.int32),
        "cotangent": bell_draw(streams_of[22], (TOKENS, MODEL_WIDTH), 1.0, 6.0, ((0, 32),)),
    }


@jax.custom_vjp
def low(v):
    return lax.optimization_barrier(v.astype(jnp.bfloat16)).astype(jnp.float32)

@jax.custom_vjp
def low_back(v):
    return v

def low_keep(v):
    return (low(v), None)

def low_pass(kept, grad):
    return (grad,)

def back_keep(v):
    return (v, None)

def back_low(kept, grad):
    return (low(grad),)
low.defvjp(low_keep, low_pass)
low_back.defvjp(back_keep, back_low)
epsilon = 1e-06
soft_cap = 50.0
rope_base = 10000.0
masked_value = -1e+30

def highest(former, latter):
    return jnp.dot(former, latter, precision=lax.Precision.HIGHEST)

def rms_scale(values, gain_row):
    return values * lax.rsqrt(lax.optimization_barrier(jnp.mean(values * values, axis=-1, keepdims=True)) + epsilon) * gain_row

def segment_of(token_index):
    return jnp.where(token_index >= PROMPT, 1 + (token_index - PROMPT) // CONT, 0)

def position_of(token_index):
    return jnp.where(token_index >= PROMPT, PROMPT + (token_index - PROMPT) % CONT, token_index)

def can_see(query_index, query_segment, key_index, key_segment):
    earlier = key_index <= query_index
    return (key_segment == 0) & ((query_segment > 0) | earlier) | (key_segment == query_segment) & earlier

def rotate(head_values, positions):
    half_size = HEAD // 2
    inverse = rope_base ** (-2.0 * jnp.arange(half_size, dtype=jnp.float32) / HEAD)
    angles = positions.astype(jnp.float32)[:, None] * inverse[None, :]
    cosine = jnp.cos(angles)[:, None, :]
    sine_part = jnp.sin(angles)[:, None, :]
    first_half = head_values[..., :half_size]
    second_half = head_values[..., half_size:]
    return jnp.concatenate([first_half * cosine - second_half * sine_part, second_half * cosine + first_half * sine_part], axis=-1)

def adapter_columns(adapters):
    lane_owner = jnp.arange(ADAPTER_COUNT * ADAPTER_RANK, dtype=jnp.int32) // ADAPTER_RANK
    return (adapters[:, None] == lane_owner[None, :]).astype(jnp.float32)

def adapted(inputs, table_in, table_out, columns):
    narrow = highest(inputs, table_in.reshape(ADAPTER_COUNT * ADAPTER_RANK, -1).T) * columns
    narrow = low(low_back(narrow))
    return highest(narrow, table_out.reshape(ADAPTER_COUNT * ADAPTER_RANK, -1))

def group_layer(params, group_tokens, id_row):
    query_weight, key_projection, value_projection, out_weight, gate_weight, up_weight, down_weight, attn_in_gain, attn_out_gain, feed_in_gain, feed_out_gain, adapt_heads_in, adapt_query_out, adapter_key_value_second, adapt_mix_in, adapt_mix_out, adapt_feed_in, adapt_feed_out, adapt_down_in, adapt_down_out = params
    token_index = jnp.arange(GROUP, dtype=jnp.int32)
    segments = segment_of(token_index)
    positions = position_of(token_index)
    columns = adapter_columns(id_row[segments])
    normed = low(rms_scale(group_tokens, attn_in_gain))
    query_pre = low_back(highest(normed, query_weight) + adapted(normed, adapt_heads_in[:, 0], adapt_query_out, columns))
    key_pre = low_back(highest(normed, key_projection) + adapted(normed, adapt_heads_in[:, 1], adapter_key_value_second[:, 0], columns))
    values = low(low_back(highest(normed, value_projection) + adapted(normed, adapt_heads_in[:, 2], adapter_key_value_second[:, 1], columns)))
    queries = low(low_back(rotate(query_pre.reshape(GROUP, HEADS, HEAD), positions) * HEAD ** (-0.5)))
    key_heads = low(low_back(rotate(key_pre.reshape(GROUP, KV_HEADS, HEAD), positions)))
    value_heads = values.reshape(GROUP, KV_HEADS, HEAD)
    query_rows = math.gcd(GROUP, 512)
    blocks = GROUP // query_rows
    grouped = queries.reshape(blocks, query_rows, KV_HEADS, HEADS // KV_HEADS, HEAD)

    def attend(element):
        query_block, query_index = element
        scores = low_back(jnp.einsum('qngd,knd->ngqk', query_block, key_heads, precision=lax.Precision.HIGHEST))
        visible = can_see(query_index[:, None], segment_of(query_index)[:, None], token_index[None, :], segments[None, :])
        capped = jnp.where(visible, soft_cap * jnp.tanh(scores / soft_cap), masked_value)
        shifted = capped - lax.optimization_barrier(jnp.max(capped, axis=-1, keepdims=True))
        exp_scores = jnp.exp(shifted)
        attn_probs = exp_scores / lax.optimization_barrier(jnp.sum(exp_scores, axis=-1, keepdims=True))
        return jnp.einsum('ngqk,knd->qngd', low(attn_probs), value_heads, precision=lax.Precision.HIGHEST)
    attended = lax.map(jax.checkpoint(attend), (grouped, token_index.reshape(blocks, query_rows)))
    mixed_heads = low(low_back(attended.reshape(GROUP, HEADS * HEAD)))
    attn_out = low_back(highest(mixed_heads, out_weight) + adapted(mixed_heads, adapt_mix_in, adapt_mix_out, columns))
    middle = group_tokens + rms_scale(attn_out, attn_out_gain)
    normed_feed = low(rms_scale(middle, feed_in_gain))
    gate_pre = low_back(highest(normed_feed, gate_weight) + adapted(normed_feed, adapt_feed_in[:, 0], adapt_feed_out[:, 0], columns))
    up_pre = low_back(highest(normed_feed, up_weight) + adapted(normed_feed, adapt_feed_in[:, 1], adapt_feed_out[:, 1], columns))
    hidden = low(jax.nn.gelu(gate_pre, approximate=True) * up_pre)
    branch = low_back(highest(hidden, down_weight) + adapted(hidden, adapt_down_in, adapt_down_out, columns))
    return middle + rms_scale(branch, feed_out_gain)

def reference(tokens, query_weight, key_projection, value_projection, out_weight, gate_weight, up_weight, down_weight, attn_in_gain, attn_out_gain, feed_in_gain, feed_out_gain, adapt_heads_in, adapt_query_out, adapter_key_value_second, adapt_mix_in, adapt_mix_out, adapt_feed_in, adapt_feed_out, adapt_down_in, adapt_down_out, adapter_ids, cotangent):
    params = tuple((argument.astype(jnp.float32) for argument in (query_weight, key_projection, value_projection, out_weight, gate_weight, up_weight, down_weight, attn_in_gain, attn_out_gain, feed_in_gain, feed_out_gain, adapt_heads_in, adapt_query_out, adapter_key_value_second, adapt_mix_in, adapt_mix_out, adapt_feed_in, adapt_feed_out, adapt_down_in, adapt_down_out)))
    inputs = tokens.astype(jnp.float32).reshape(GROUPS, GROUP, MODEL_WIDTH)
    layer_step = jax.checkpoint(group_layer)

    def forward(weights_all, layer_inputs):

        def group_step(carried, element):
            group_tokens, id_row = element
            return (carried, layer_step(weights_all, group_tokens, id_row))
        _, outputs = lax.scan(group_step, jnp.zeros((), jnp.float32), (layer_inputs, adapter_ids))
        return outputs
    outputs, pullback = jax.vjp(forward, params, inputs)
    grad_params, grad_inputs = pullback(cotangent.astype(jnp.float32).reshape(GROUPS, GROUP, MODEL_WIDTH))
    return (outputs.reshape(TOKENS, MODEL_WIDTH).astype(jnp.bfloat16), grad_inputs.reshape(TOKENS, MODEL_WIDTH), grad_params[11], grad_params[12], grad_params[13], grad_params[14], grad_params[15], grad_params[16], grad_params[17], grad_params[18], grad_params[19])
```

```python
import jax
import jax.numpy as jnp
from jax import lax
from jax.experimental import pallas as pl
from jax.experimental.pallas import tpu as pltpu
from jax.sharding import PartitionSpec as P

HEADS = 8
KV_HEADS = 4
HEAD = 256
RANK = 16
ADAPTERS = 8
LANES = RANK * ADAPTERS
PROMPT = 2048
CONT = 256
CONTS = 8

epsilon = 1e-06
soft_cap = 50.0
rope_base = 10000.0
PLANE = ("dp", "blk")
EVERY = ("dp", "blk", "ulysses")
f32 = jnp.float32
bf16 = jnp.bfloat16


def dot_nn(a, b):
    return jnp.dot(a, b, preferred_element_type=f32)


def dot_nt(a, b):
    return lax.dot_general(a, b, (((1,), (1,)), ((), ())), preferred_element_type=f32)


def dot_tn(a, b):
    return lax.dot_general(a, b, (((0,), (0,)), ((), ())), preferred_element_type=f32)


def rms_scale(values, gain_row):
    return (
        values * lax.rsqrt(jnp.mean(values * values, axis=-1, keepdims=True) + epsilon) * gain_row
    )


def norm_back(values, gain_row, grad_out):
    scale = lax.rsqrt(jnp.mean(values * values, axis=-1, keepdims=True) + epsilon)
    weighted = grad_out * gain_row
    return scale * weighted - values * (
        scale * scale * scale * jnp.mean(values * weighted, axis=-1, keepdims=True)
    )


def shape(dims, dtype):
    return jax.ShapeDtypeStruct(dims, dtype)


VM = pl.BlockSpec(memory_space=pltpu.VMEM)


MESH = pl.DeviceIdType.MESH


def neighbours():
    dp, b, z = lax.axis_index("dp"), lax.axis_index("blk"), lax.axis_index("ulysses")
    across_x = (dp + 1 - 2 * (dp % 2), b, z)
    across_y = (dp, (b + 2) % 4, z)
    sibling = (dp, b + 1 - 2 * (b % 2), z)
    return across_x, across_y, sibling


def greet(peers):
    barrier = pltpu.get_barrier_semaphore()
    for peer in peers:
        pl.semaphore_signal(barrier, inc=1, device_id=peer, device_id_type=MESH)
    pl.semaphore_wait(barrier, len(peers))


def sender(send, recv):
    def copy(index, src, dst, peer):
        return pltpu.make_async_remote_copy(
            src, dst, send.at[index], recv.at[index], device_id=peer, device_id_type=MESH
        )

    return copy


def add_into(target, source, count, step=32):
    @pl.loop(0, count // step)
    def _(i):
        at = pl.ds(pl.multiple_of(i * step, step), step)
        target[at, :] = (target[at, :].astype(f32) + source[at, :].astype(f32)).astype(target.dtype)


class PlaneGather:
    COUNT = 10

    def __init__(self, copy, own, land, rows):
        px, py, pc = neighbours()
        h = rows // 2
        h0, h1 = pl.ds(0, h), pl.ds(h, h)
        near, far = pl.ds(0, rows), pl.ds(rows, rows)
        self.c = [
            copy(0, own, land.at[0, far], pc),
            copy(1, own.at[h0], land.at[1, h0], px),
            copy(2, own.at[h1], land.at[3, h1], py),
            copy(3, own.at[h1], land.at[1, h1], px),
            copy(4, own.at[h0], land.at[3, h0], py),
            copy(5, land.at[1, h0], land.at[2, h0], py),
            copy(6, land.at[3, h1], land.at[2, h1], px),
            copy(7, land.at[1, near], land.at[1, far], pc),
            copy(8, land.at[3, near], land.at[3, far], pc),
            copy(9, land.at[2, near], land.at[2, far], pc),
        ]

    def begin(self):
        for i in range(5):
            self.c[i].start()

    def before(self, i):
        c = self.c

        @pl.when(i == 0)
        def _():
            c[0].wait_recv()

        @pl.when(i == 1)
        def _():
            c[1].wait_recv()
            c[5].start()
            c[2].wait_recv()
            c[6].start()
            c[3].wait_recv()
            c[7].start()
            c[4].wait_recv()
            c[8].start()
            c[7].wait_recv()

        @pl.when(i == 2)
        def _():
            c[5].wait_recv()
            c[6].wait_recv()
            c[9].start()
            c[9].wait_recv()

        @pl.when(i == 3)
        def _():
            c[8].wait_recv()

    def finish(self):
        for c in self.c:
            c.wait_send()


class PlaneReduce:
    COUNT = 10

    def __init__(self, copy, part, odd, from_core, from_x, from_y, diag, rows, first):
        px, py, pc = neighbours()
        h = rows // 2
        self.h = h
        self.rows = rows
        h0, h1 = pl.ds(0, h), pl.ds(h, h)
        self.part, self.from_core = part, from_core
        self.from_x, self.from_y, self.diag = from_x, from_y, diag
        self.core = [
            copy(first + i, odd.at[i % 2], from_core.at[i], pc) for i in range(4)
        ]
        self.d = [
            copy(first + 4, part.at[2, h0], diag.at[h0], px),
            copy(first + 5, part.at[2, h1], diag.at[h1], py),
        ]
        self.e = [
            copy(first + 6, part.at[1, h0], from_x.at[h0], px),
            copy(first + 7, part.at[3, h1], from_y.at[h1], py),
            copy(first + 8, part.at[1, h1], from_x.at[h1], px),
            copy(first + 9, part.at[3, h0], from_y.at[h0], py),
        ]

    def merge(self, i):
        self.core[i].wait_recv()
        add_into(self.part.at[i], self.from_core.at[i], self.rows)

    def before(self, i):
        for k in (2, 3):

            @pl.when(i == k)
            def _(k=k):
                self.core[k - 2].wait_send()

    def after(self, i):
        for k in range(4):

            @pl.when(i == k)
            def _(k=k):
                self.core[k].start()
                if k == 2:
                    self.merge(1)
                    self.e[0].start()
                    self.merge(2)
                    self.d[0].start()
                    self.d[1].start()

    def finish(self, out):
        h, h0, h1 = self.h, pl.ds(0, self.h), pl.ds(self.h, self.h)
        self.merge(3)
        self.e[1].start()
        self.d[0].wait_recv()
        add_into(self.part.at[3, h0], self.diag.at[h0], h)
        self.e[3].start()
        self.d[1].wait_recv()
        add_into(self.part.at[1, h1], self.diag.at[h1], h)
        self.e[2].start()
        self.merge(0)
        for e in self.e:
            e.wait_recv()

        @pl.loop(0, self.rows // 32)
        def _(i):
            at = pl.ds(pl.multiple_of(i * 32, 32), 32)
            out[at, :] = (
                self.part[0, at, :].astype(f32)
                + self.from_x[at, :].astype(f32)
                + self.from_y[at, :].astype(f32)
            ).astype(out.dtype)

        for c in self.core[2:] + self.d + self.e:
            c.wait_send()


GELU_SLOPE = 0.7978845608028654
GELU_CUBE = 0.044715


def span(i, size):
    return pl.ds(pl.multiple_of(i * size, size), size)


def feed_forward_kernel(
    own, feed_in, gate_out, up_out, down_in, down_out, columns, gate_hbm, up_hbm, down_hbm,
    branch, narrow, feed_all, gate_up,
    gate, up, down, land, hidden, saved, part, odd, from_core, from_x, from_y, diag,
    send, recv, load, store,
):
    rows = own.shape[0]
    share = gate.shape[1]
    width = own.shape[1]
    tile = 384
    loads = [
        pltpu.make_async_copy(s, d, load.at[i])
        for i, (s, d) in enumerate(((gate_hbm, gate), (up_hbm, up), (down_hbm, down)))
    ]
    for c in loads:
        c.start()
    greet(neighbours())
    copy = sender(send, recv)
    gather = PlaneGather(copy, own, land, rows)
    reduce = PlaneReduce(
        copy, part, odd, from_core, from_x, from_y, diag, rows, PlaneGather.COUNT
    )
    gather.begin()
    land[0, :rows, :] = own[...]
    for c in loads:
        c.wait()

    def keep(i):
        slot = i % 2
        return (
            pltpu.make_async_copy(saved.at[slot], gate_up.at[i], store.at[slot]),
            pltpu.make_async_copy(land.at[i], feed_all.at[i], store.at[2 + slot]),
        )

    @pl.loop(0, 4)
    def _(i):
        gather.before(i)
        slot = i % 2

        @pl.when(i >= 2)
        def _():
            for c in keep(i - 2):
                c.wait()

        masks = columns[i].astype(f32)
        low = dot_nt(land[i], feed_in[...])
        low_gate = (low[:, :LANES] * masks).astype(bf16)
        low_up = (low[:, LANES:] * masks).astype(bf16)
        narrow[i, 0] = low_gate
        narrow[i, 1] = low_up

        @pl.loop(0, share // tile)
        def _(n):
            at = span(n, tile)
            g = dot_nn(land[i], gate[:, at]) + dot_nn(narrow[i, 0], gate_out[:, at])
            u = dot_nn(land[i], up[:, at]) + dot_nn(narrow[i, 1], up_out[:, at])
            saved[slot, 0, :, at] = g.astype(bf16)
            saved[slot, 1, :, at] = u.astype(bf16)
            th = jnp.tanh(GELU_SLOPE * (g + GELU_CUBE * g * g * g))
            hidden[:, at] = (0.5 * g * (1.0 + th) * u).astype(bf16)

        for c in keep(i):
            c.start()
        narrow[i, 2] = (dot_nt(hidden[...], down_in[...]) * masks).astype(bf16)
        reduce.before(i)

        @pl.loop(0, width // tile)
        def _(n):
            at = span(n, tile)
            got = dot_nn(hidden[...], down[:, at]) + dot_nn(narrow[i, 2], down_out[:, at])
            got = got.astype(bf16)
            part[i, :, at] = got[:rows]
            odd[i % 2, :, at] = got[rows:]

        reduce.after(i)

    reduce.finish(branch)
    gather.finish()
    for i in (2, 3):
        for c in keep(i):
            c.wait()


def feed_backward_kernel(
    own, feed_in, gate_out, up_out, down_in, down_out, columns, narrow,
    gate_hbm, up_hbm, down_hbm, gate_up,
    grad_feed, both, t_feed_out, t_down_in, t_down_out,
    gate, up, down, land, saved, gg, gu, part, odd, from_core, from_x, from_y, diag,
    send, recv, load, fetch,
):
    rows = own.shape[0]
    share = gate.shape[1]
    width = own.shape[1]
    tile = 384
    loads = [
        pltpu.make_async_copy(s, d, load.at[i])
        for i, (s, d) in enumerate(((down_hbm, down), (gate_hbm, gate), (up_hbm, up)))
    ]

    def bring(i):
        return pltpu.make_async_copy(gate_up.at[i], saved, fetch.at[0])

    for c in loads:
        c.start()
    bring(0).start()
    greet(neighbours())
    copy = sender(send, recv)
    gather = PlaneGather(copy, own, land, rows)
    reduce = PlaneReduce(
        copy, part, odd, from_core, from_x, from_y, diag, rows, PlaneGather.COUNT
    )
    gather.begin()
    land[0, :rows, :] = own[...]
    t_feed_out[...] = jnp.zeros_like(t_feed_out)
    t_down_in[...] = jnp.zeros_like(t_down_in)
    t_down_out[...] = jnp.zeros_like(t_down_out)
    for c in loads:
        c.wait()

    @pl.loop(0, 4)
    def _(i):
        gather.before(i)
        bring(i).wait()
        masks = columns[i].astype(f32)
        back = (dot_nt(land[i], down_out[...]) * masks).astype(bf16)

        @pl.loop(0, share // tile)
        def _(n):
            at = span(n, tile)
            gh = dot_nt(land[i], down[at, :]) + dot_nn(back, down_in[:, at])
            g = saved[0, :, at].astype(f32)
            u = saved[1, :, at].astype(f32)
            th = jnp.tanh(GELU_SLOPE * (g + GELU_CUBE * g * g * g))
            gelu = 0.5 * g * (1.0 + th)
            slope = 0.5 * (1.0 + th) + 0.5 * g * (1.0 - th * th) * GELU_SLOPE * (
                1.0 + 3.0 * GELU_CUBE * g * g
            )
            t_down_in[:, at] += dot_tn(back, (gelu * u).astype(bf16))
            gg[:, at] = (gh * u * slope).astype(bf16)
            gu[:, at] = (gh * gelu).astype(bf16)

        @pl.when(i < 3)
        def _():
            bring(i + 1).start()

        back_gate = (dot_nt(gg[...], gate_out[...]) * masks).astype(bf16)
        back_up = (dot_nt(gu[...], up_out[...]) * masks).astype(bf16)
        both[i] = jnp.concatenate([back_gate, back_up], axis=1)
        reduce.before(i)

        @pl.loop(0, width // tile)
        def _(n):
            at = span(n, tile)
            got = (
                dot_nt(gg[...], gate[at, :])
                + dot_nt(gu[...], up[at, :])
                + dot_nn(both[i], feed_in[:, at])
            ).astype(bf16)
            part[i, :, at] = got[:rows]
            odd[i % 2, :, at] = got[rows:]

        reduce.after(i)
        t_feed_out[0] += dot_tn(narrow[i, 0], gg[...])
        t_feed_out[1] += dot_tn(narrow[i, 1], gu[...])
        t_down_out[...] += dot_tn(narrow[i, 2], land[i])

    reduce.finish(grad_feed)
    gather.finish()


def feed_scratch(rows, width):
    return [
        pltpu.VMEM((4, rows, width), bf16),
        pltpu.VMEM((2, rows, width), bf16),
        pltpu.VMEM((4, rows, width), bf16),
        pltpu.VMEM((rows, width), bf16),
        pltpu.VMEM((rows, width), bf16),
        pltpu.VMEM((rows, width), bf16),
        pltpu.SemaphoreType.DMA((PlaneGather.COUNT + PlaneReduce.COUNT,)),
        pltpu.SemaphoreType.DMA((PlaneGather.COUNT + PlaneReduce.COUNT,)),
    ]


ANY = pl.BlockSpec(memory_space=pl.ANY)


def feed_forward(own, feed_in, gate_out, up_out, down_in, down_out, columns, gate, up, down):
    rows, width = own.shape
    share = gate.shape[1]
    return pl.pallas_call(
        feed_forward_kernel,
        out_shape=(
            shape((rows, width), f32),
            shape((4, 3, 2 * rows, LANES), bf16),
            shape((4, 2 * rows, width), bf16),
            shape((4, 2, 2 * rows, share), bf16),
        ),
        in_specs=[VM] * 7 + [ANY] * 3,
        out_specs=(VM, VM, ANY, ANY),
        scratch_shapes=[
            pltpu.VMEM(gate.shape, bf16),
            pltpu.VMEM(up.shape, bf16),
            pltpu.VMEM(down.shape, bf16),
            pltpu.VMEM((4, 2 * rows, width), bf16),
            pltpu.VMEM((2 * rows, share), bf16),
            pltpu.VMEM((2, 2, 2 * rows, share), bf16),
        ]
        + feed_scratch(rows, width)
        + [pltpu.SemaphoreType.DMA((3,)), pltpu.SemaphoreType.DMA((4,))],
        compiler_params=pltpu.CompilerParams(
            collective_id=1, has_side_effects=True, vmem_limit_bytes=62 << 20
        ),
        name="feed_forward",
    )(own, feed_in, gate_out, up_out, down_in, down_out, columns, gate, up, down)


def feed_backward(
    own, feed_in, gate_out, up_out, down_in, down_out, columns, narrow, gate, up, down, gate_up
):
    rows, width = own.shape
    share = gate.shape[1]
    return pl.pallas_call(
        feed_backward_kernel,
        out_shape=(
            shape((rows, width), bf16),
            shape((4, 2 * rows, 2 * LANES), bf16),
            shape((2, LANES, share), f32),
            shape((LANES, share), f32),
            shape((LANES, width), f32),
        ),
        in_specs=[VM] * 8 + [ANY] * 4,
        out_specs=(VM,) * 5,
        scratch_shapes=[
            pltpu.VMEM(gate.shape, bf16),
            pltpu.VMEM(up.shape, bf16),
            pltpu.VMEM(down.shape, bf16),
            pltpu.VMEM((4, 2 * rows, width), bf16),
            pltpu.VMEM((2, 2 * rows, share), bf16),
            pltpu.VMEM((2 * rows, share), bf16),
            pltpu.VMEM((2 * rows, share), bf16),
        ]
        + feed_scratch(rows, width)
        + [pltpu.SemaphoreType.DMA((3,)), pltpu.SemaphoreType.DMA((1,))],
        compiler_params=pltpu.CompilerParams(
            collective_id=2, has_side_effects=True, vmem_limit_bytes=62 << 20
        ),
        name="feed_backward",
    )(
        own, feed_in, gate_out, up_out, down_in, down_out, columns, narrow, gate, up, down, gate_up
    )


def rms_rows(source, gain, target, rows, add=None, keep=None):
    @pl.loop(0, rows // 32)
    def _(i):
        at = span(i, 32)
        v = source[at, :].astype(f32)
        out = v * lax.rsqrt(jnp.mean(v * v, axis=-1, keepdims=True) + epsilon) * gain[...]
        if add is not None:
            out = out + add[at, :].astype(f32)
        target[at, :] = out.astype(target.dtype)


def attention_forward_kernel(
    tokens, attn_in_gain, attn_out_gain, feed_in_gain, heads_in, query_out, key_out, value_out,
    mix_in, mix_out, columns, own_columns, cosine, sine,
    query_hbm, key_hbm, value_hbm, out_hbm, gate_hbm, up_hbm,
    queries, values_prompt, values_cont, attended, sums, narrow, mixed_out, narrow_mix, attn_out,
    middle, normed_feed, normed_out, wall_out, out_out, gate_share, up_share,
    normed_all, wall, wo, kvp, kvc, acc, total, mixed, send, recv, local,
):
    rows, width = tokens.shape
    dp, b, z = lax.axis_index("dp"), lax.axis_index("blk"), lax.axis_index("ulysses")
    planes = lax.axis_size("ulysses")
    x, y, c = dp % 2, b // 2, b % 2
    base = dp - x
    rank = x * 4 + b
    b_c, b_y = b + 1 - 2 * c, (b + 2) % 4
    b_yc = (b_c + 2) % 4
    pc, py, pyc = (dp, b_c, z), (dp, b_y, z), (dp, b_yc, z)
    other = base + 1 - x
    px, pxc, pxy, pxyc = (other, b, z), (other, b_c, z), (other, b_y, z), (other, b_yc, z)
    pz = (dp, b, z + 1 - 2 * (z % 2))
    left, right = (dp, b, z - 1), (dp, b, z + 1)
    depth = query_hbm.shape[0]
    share = gate_share.shape[1]
    part = out_hbm.shape[0]
    copy = sender(send, recv)

    def block(i):
        return span(i, rows)

    def weight_rows(i):
        return pl.ds(pl.multiple_of(i * depth, 16), depth)

    def out_rows(i):
        return span(i, part)

    heads = ((query_hbm, 2 * HEAD, 0), (key_hbm, HEAD, 2 * HEAD), (value_hbm, HEAD, 3 * HEAD))

    def columns_of(ref, target, size):
        return ref.at[:, pl.ds(pl.multiple_of(target * size, 128), size)]

    own_loads = [
        pltpu.make_async_copy(
            columns_of(ref, b, size), wall.at[weight_rows(rank), pl.ds(to, size)], local.at[i]
        )
        for i, (ref, size, to) in enumerate(heads)
    ]
    own_loads.append(pltpu.make_async_copy(out_hbm, wo.at[out_rows(rank)], local.at[3]))
    own_rows = [
        pltpu.make_async_copy(
            columns_of(ref, rank, share), out.at[weight_rows(rank)], local.at[4 + i]
        )
        for i, (ref, out) in enumerate(((gate_hbm, gate_share), (up_hbm, up_share)))
    ]
    for cp in own_loads:
        cp.start()

    barrier = pltpu.get_barrier_semaphore()
    for peer in (pc, py, pyc, px, pxc, pxy, pxyc) + tuple(
        (dp, b, (z + d) % planes) for d in range(1, planes)
    ):
        pl.semaphore_signal(barrier, inc=1, device_id=peer, device_id_type=MESH)

    rms_rows(tokens, attn_in_gain, normed_all.at[block(b)], rows)
    pl.semaphore_wait(barrier, 6 + planes)

    stage = []
    for j, (peer, pb) in enumerate(((py, b_y), (pyc, b_yc), (pc, b_c))):
        for i, (ref, size, to) in enumerate(heads):
            stage.append(
                copy(
                    3 + 3 * j + i,
                    columns_of(ref, pb, size),
                    wall.at[weight_rows(rank), pl.ds(to, size)],
                    peer,
                )
            )
    token_copies = [
        copy(0, normed_all.at[block(b)], normed_all.at[block(b)], py),
        copy(1, normed_all.at[block(b)], normed_all.at[block(b)], pc),
        copy(2, normed_all.at[block(b_y)], normed_all.at[block(b_y)], pc),
    ]
    across = [
        copy(12 + i, wall.at[weight_rows(x * 4 + o)], wall.at[weight_rows(x * 4 + o)], px)
        for i, o in enumerate((b, b_c, b_y, b_yc))
    ]
    for cp in stage[:3]:
        cp.start()
    token_copies[0].start()
    for cp in stage[3:]:
        cp.start()
    token_copies[1].start()
    for cp in own_loads[:3]:
        cp.wait()
    across[0].start()
    for cp in stage[6:]:
        cp.wait_recv()
    across[1].start()
    for cp in stage[:3]:
        cp.wait_recv()
    across[2].start()
    for cp in stage[3:6]:
        cp.wait_recv()
    across[3].start()
    token_copies[0].wait_recv()
    token_copies[2].start()

    half = part // 2
    rx, ry, rxy = (1 - x) * 4 + b, x * 4 + b_y, (1 - x) * 4 + b_y

    def wo_part(r, h):
        return wo.at[pl.ds(pl.multiple_of(r * part + h * half, 16), half)]

    wo_first = [
        (16, wo_part(rank, 0), px),
        (17, wo_part(rank, 1), py),
        (18, wo_part(rank, 1), px),
        (19, wo_part(rank, 0), py),
        (20, wo.at[out_rows(rank)], pc),
    ]
    wo_next = [
        (21, wo_part(rx, 0), py),
        (22, wo_part(ry, 1), px),
        (23, wo.at[out_rows(rx)], pc),
        (24, wo.at[out_rows(ry)], pc),
        (25, wo.at[out_rows(rxy)], pc),
    ]
    wo_first = [copy(i, ref, ref, peer) for i, ref, peer in wo_first]
    wo_next = [copy(i, ref, ref, peer) for i, ref, peer in wo_next]
    own_loads[3].wait()
    for cp in across:
        cp.wait_recv()
    for cp in wo_first:
        cp.start()
    token_copies[1].wait_recv()
    token_copies[2].wait_recv()

    outs = [
        pltpu.make_async_copy(normed_all, normed_out, local.at[6]),
        pltpu.make_async_copy(wall, wall_out, local.at[7]),
        pltpu.make_async_copy(wo, out_out, local.at[8]),
        pltpu.make_async_copy(kvp, values_prompt, local.at[9]),
        pltpu.make_async_copy(kvc, values_cont, local.at[10]),
        pltpu.make_async_copy(mixed, mixed_out, local.at[11]),
    ]
    outs[0].start()
    outs[1].start()

    half_head = HEAD // 2

    @pl.loop(0, 4)
    def _(t):
        at = block(t)
        masks = columns[at, :].astype(f32)
        cos, sin = cosine[at, :], sine[at, :]
        a = normed_all[at, :]
        for i in range(3):
            lanes = slice(i * LANES, (i + 1) * LANES)
            narrow[at, lanes] = (dot_nt(a, heads_in[lanes, :]) * masks).astype(bf16)

        def turned(pre, scale):
            first, second = pre[:, :half_head], pre[:, half_head:]
            one, two = first * cos - second * sin, second * cos + first * sin
            if scale != 1.0:
                one, two = one * scale, two * scale
            return jnp.concatenate([one, two], axis=1).astype(bf16)

        for h in range(2):
            lanes = slice(h * HEAD, (h + 1) * HEAD)
            pre = dot_nn(a, wall[:, lanes]) + dot_nn(narrow[at, :LANES], query_out[:, lanes])
            queries[t, h * rows : (h + 1) * rows, :] = turned(pre, HEAD ** (-0.5))
        pre = dot_nn(a, wall[:, 2 * HEAD : 3 * HEAD]) + dot_nn(
            narrow[at, LANES : 2 * LANES], key_out[...]
        )
        key = turned(pre, 1.0)
        value = (
            dot_nn(a, wall[:, 3 * HEAD :]) + dot_nn(narrow[at, 2 * LANES :], value_out[...])
        ).astype(bf16)

        @pl.when(t < 2)
        def _():
            kvp[z, 0, t] = key
            kvp[z, 1, t] = value

        @pl.when(t >= 2)
        def _():
            kvc[0, t - 2] = key
            kvc[1, t - 2] = value

    def hop(direction, d):
        index = 42 + d if direction > 0 else 45 + d
        zz = z - d * direction
        return copy(index, kvp.at[zz], kvp.at[zz], right if direction > 0 else left)

    def pass_on(direction, d):
        reach = z < planes - 1 if direction > 0 else z > 0

        @pl.when(reach)
        def _():
            hop(direction, d).start()

    pass_on(1, 0)
    pass_on(-1, 0)

    acc[...] = jnp.zeros_like(acc)
    total[...] = jnp.zeros_like(total)
    row = lax.broadcasted_iota(jnp.int32, (2 * rows, rows), 0) % rows
    causal = lax.broadcasted_iota(jnp.int32, (2 * rows, rows), 1) <= row

    def step(t, k, v, masked):
        e = jnp.exp(soft_cap * jnp.tanh(dot_nt(queries[t], k) * (1.0 / soft_cap)))
        if masked:
            e = jnp.where(causal, e, 0.0)
        some = e[:, :128]
        for n in range(128, rows, 128):
            some = some + e[:, n : n + 128]
        total[t] += some
        acc[t] += dot_nn(e.astype(bf16), v)

    step(0, kvp[z, 0, 0], kvp[z, 1, 0], True)
    step(1, kvp[z, 0, 0], kvp[z, 1, 0], False)
    step(1, kvp[z, 0, 1], kvp[z, 1, 1], True)

    @pl.loop(2, 4)
    def _(t):
        step(t, kvc[0, t - 2], kvc[1, t - 2], True)
        step(t, kvp[z, 0, 0], kvp[z, 1, 0], False)
        step(t, kvp[z, 0, 1], kvp[z, 1, 1], False)

    wo_first[0].wait_recv()
    wo_next[0].start()
    wo_first[1].wait_recv()
    wo_next[1].start()

    swaps = []
    at = 26
    for peer, pr in (
        (px, rx), (py, ry), (pxc, (1 - x) * 4 + b_c), (pyc, x * 4 + b_yc), (pc, x * 4 + b_c),
    ):
        for ref, out in ((gate_hbm, gate_share), (up_hbm, up_share)):
            swaps.append(
                copy(at, columns_of(ref, pr, share), out.at[weight_rows(rank)], peer)
            )
            at += 1
    far = []
    for i, (ref, out) in enumerate(((gate_hbm, gate_share), (up_hbm, up_share))):
        for j, (peer, pr) in enumerate(((pxy, rxy), (pxyc, (1 - x) * 4 + b_yc))):
            far.append(
                pltpu.make_async_remote_copy(
                    columns_of(ref, pr, share),
                    out.at[weight_rows(rank)],
                    send.at[36 + 2 * j + i],
                    recv.at[36 + i],
                    device_id=peer,
                    device_id_type=MESH,
                )
            )
    got_rank = (1 - x) * 4 + (1 - y) * 2 + z % 2
    relay = [
        copy(40 + i, out.at[weight_rows(got_rank)], out.at[weight_rows(got_rank)], pz)
        for i, out in enumerate((gate_share, up_share))
    ]

    @pl.when(c == z % 2)
    def _():
        for cp in far:
            cp.start()

    for cp in swaps:
        cp.start()
    for cp in own_rows:
        cp.start()

    @pl.loop(0, 2 * (planes - 1))
    def _(i):
        d = i // 2 + 1
        direction = 1 - 2 * (i % 2)
        zz = z - d * direction

        @pl.when((zz >= 0) & (zz < planes))
        def _():
            index = 42 + 3 * (i % 2) + d - 1
            here = pltpu.make_async_remote_copy(
                kvp.at[zz], kvp.at[zz], send.at[index], recv.at[index], device_id=left,
                device_id_type=MESH,
            )
            here.wait_recv()

            @pl.when((i % 2 == 0) & (z < planes - 1))
            def _():
                pltpu.make_async_remote_copy(
                    kvp.at[zz], kvp.at[zz], send.at[index + 1], recv.at[index + 1],
                    device_id=right, device_id_type=MESH,
                ).start()

            @pl.when((i % 2 == 1) & (z > 0))
            def _():
                pltpu.make_async_remote_copy(
                    kvp.at[zz], kvp.at[zz], send.at[index + 1], recv.at[index + 1],
                    device_id=left, device_id_type=MESH,
                ).start()

            step(1, kvp[zz, 0, 0], kvp[zz, 1, 0], False)

            @pl.when(zz < z)
            def _():
                step(0, kvp[zz, 0, 0], kvp[zz, 1, 0], False)
                step(1, kvp[zz, 0, 1], kvp[zz, 1, 1], False)

            @pl.loop(2, 4)
            def _(t):
                step(t, kvp[zz, 0, 0], kvp[zz, 1, 0], False)
                step(t, kvp[zz, 0, 1], kvp[zz, 1, 1], False)

    outs[3].start()
    outs[4].start()
    ones = jnp.ones((8, 128), f32)

    @pl.loop(0, 4)
    def _(t):
        whole = jnp.sum(total[t], axis=1, keepdims=True)
        got = (acc[t] / whole).astype(bf16)
        attended[t, :, :HEAD] = got[:rows]
        attended[t, :, HEAD:] = got[rows:]
        sums[t] = lax.dot_general(
            ones, total[t], (((1,), (1,)), ((), ())), precision=lax.Precision.HIGHEST,
            preferred_element_type=f32,
        )

    lanes = pl.ds(pl.multiple_of(b * 2 * HEAD, 128), 2 * HEAD)
    mixes = [
        copy(48 + i, attended.at[o], mixed.at[:, lanes], peer)
        for i, (peer, o) in enumerate(((py, b_y), (pyc, b_yc), (pc, b_c)))
    ]
    for cp in mixes:
        cp.start()
    mixed[:, lanes] = attended[b]
    wo_first[2].wait_recv()
    wo_next[2].start()
    wo_first[3].wait_recv()
    wo_next[3].start()
    wo_next[0].wait_recv()
    wo_next[1].wait_recv()
    wo_next[4].start()
    wo_first[4].wait_recv()
    for cp in wo_next[2:]:
        cp.wait_recv()
    for cp in mixes:
        cp.wait_recv()
    outs[2].start()
    outs[5].start()
    narrow_mix[...] = (dot_nt(mixed[...], mix_in[...]) * own_columns[...].astype(f32)).astype(bf16)

    @pl.loop(0, width // 384)
    def _(n):
        at = span(n, 384)
        attn_out[:, at] = dot_nn(mixed[...], wo[:, at]) + dot_nn(narrow_mix[...], mix_out[:, at])

    rms_rows(attn_out, attn_out_gain, middle, rows, add=tokens)
    rms_rows(middle, feed_in_gain, normed_feed, rows)

    for cp in far[:1] + far[2:3]:
        cp.wait_recv()
    for cp in relay:
        cp.start()
    for cp in swaps:
        cp.wait()
    for cp in relay:
        cp.wait()

    @pl.when(c == z % 2)
    def _():
        for cp in far:
            cp.wait_send()

    for cp in own_rows + outs:
        cp.wait()
    for cp in stage + token_copies + across + wo_first + wo_next + mixes:
        cp.wait_send()

    @pl.loop(0, 2 * (planes - 1))
    def _(i):
        d = i // 2
        direction = 1 - 2 * (i % 2)
        zz = z - d * direction
        onward = z + direction

        @pl.when((zz >= 0) & (zz < planes) & (onward >= 0) & (onward < planes))
        def _():
            index = 42 + 3 * (i % 2) + d
            pltpu.make_async_remote_copy(
                kvp.at[zz], kvp.at[zz], send.at[index], recv.at[index], device_id=left,
                device_id_type=MESH,
            ).wait_send()


def attention_forward(
    tokens, gains, tables, columns, own_columns, cosine, sine, weights, share
):
    rows, width = tokens.shape
    planes = lax.axis_size("ulysses")
    return pl.pallas_call(
        attention_forward_kernel,
        out_shape=(
            shape((4, 2 * rows, HEAD), bf16),
            shape((planes, 2, 2, rows, HEAD), bf16),
            shape((2, 2, rows, HEAD), bf16),
            shape((4, rows, 2 * HEAD), bf16),
            shape((4, 8, 2 * rows), f32),
            shape((4 * rows, 3 * LANES), bf16),
            shape((rows, 8 * HEAD), bf16),
            shape((rows, LANES), bf16),
            shape((rows, width), f32),
            shape((rows, width), f32),
            shape((rows, width), bf16),
            shape((4 * rows, width), bf16),
            shape((width, 4 * HEAD), bf16),
            shape((8 * HEAD, width), bf16),
            shape((width, share), bf16),
            shape((width, share), bf16),
        ),
        in_specs=[VM] * 14 + [ANY] * 6,
        out_specs=(VM, ANY, ANY, VM, VM, VM, ANY, VM, VM, VM, VM, ANY, ANY, ANY, ANY, ANY),
        scratch_shapes=[
            pltpu.VMEM((4 * rows, width), bf16),
            pltpu.VMEM((width, 4 * HEAD), bf16),
            pltpu.VMEM((8 * HEAD, width), bf16),
            pltpu.VMEM((planes, 2, 2, rows, HEAD), bf16),
            pltpu.VMEM((2, 2, rows, HEAD), bf16),
            pltpu.VMEM((4, 2 * rows, HEAD), f32),
            pltpu.VMEM((4, 2 * rows, 128), f32),
            pltpu.VMEM((rows, 8 * HEAD), bf16),
            pltpu.SemaphoreType.DMA((51,)),
            pltpu.SemaphoreType.DMA((51,)),
            pltpu.SemaphoreType.DMA((12,)),
        ],
        compiler_params=pltpu.CompilerParams(
            collective_id=3, has_side_effects=True, vmem_limit_bytes=62 << 20
        ),
        name="attention_forward",
    )(tokens, *gains, *tables, columns, own_columns, cosine, sine, *weights)


class Places:
    def __init__(self):
        dp, b, z = lax.axis_index("dp"), lax.axis_index("blk"), lax.axis_index("ulysses")
        self.b, self.z, self.planes = b, z, lax.axis_size("ulysses")
        x, c = dp % 2, b % 2
        self.x, self.y, self.c = x, b // 2, c
        self.b_c, self.b_y = b + 1 - 2 * c, (b + 2) % 4
        self.b_yc = (self.b_c + 2) % 4
        other = dp + 1 - 2 * x
        self.dp, self.other = dp, other
        self.pc, self.py, self.pyc = (dp, self.b_c, z), (dp, self.b_y, z), (dp, self.b_yc, z)
        self.px = (other, b, z)
        self.plane = (
            self.pc, self.py, self.pyc, self.px,
            (other, self.b_c, z), (other, self.b_y, z), (other, self.b_yc, z),
        )
        self.rank = x * 4 + b
        self.near = (x * 4 + b, (1 - x) * 4 + b, (1 - x) * 4 + self.b_y, x * 4 + self.b_y)
        self.far = (x * 4 + self.b_c, (1 - x) * 4 + self.b_c, (1 - x) * 4 + self.b_yc, x * 4 + self.b_yc)

    def along(self, d):
        return (self.z + d) % self.planes

    def up(self, d):
        return (self.dp, self.b, self.along(d))


class TableSpread:
    COUNT = 16

    def __init__(self, place, copy, first, source, arrived, piece, gathered, local):
        self.place, self.source, self.arrived, self.piece = place, source, arrived, piece
        self.gathered = gathered
        n = place.planes
        self.q = piece.shape[0]
        half = n // 2

        def region(rank, h):
            return gathered.at[rank, pl.ds(h * half, half)]

        self.out = [
            copy(first + d - 1, source.at[span(place.along(d), self.q)], arrived.at[d - 1], place.up(d))
            for d in range(1, n)
        ]
        self.own = pltpu.make_async_copy(piece, gathered.at[place.rank, place.z], local)
        self.back = [
            copy(first + 2 + d, piece, gathered.at[place.rank, place.z], place.up(d))
            for d in range(1, n)
        ]
        own, rx, rxy, ry = place.near
        at = first + 6

        def same(i, ref, peer):
            return copy(at + i, ref, ref, peer)

        px, py, pc = place.px, place.py, place.pc
        self.first = [
            same(0, region(own, 0), px),
            same(1, region(own, 1), py),
            same(2, region(own, 1), px),
            same(3, region(own, 0), py),
            same(4, gathered.at[own], pc),
        ]
        self.next = [
            same(5, region(rx, 0), py),
            same(6, region(ry, 1), px),
            same(7, gathered.at[rx], pc),
            same(8, gathered.at[ry], pc),
            same(9, gathered.at[rxy], pc),
        ]

    def scatter(self):
        for c in self.out:
            c.start()

    def gather(self):
        for c in self.out:
            c.wait_recv()
        got = self.source[span(self.place.z, self.q), :].astype(f32)
        for i in range(self.place.planes - 1):
            got = got + self.arrived[i].astype(f32)
        self.piece[...] = got.astype(bf16)
        self.own.start()
        for c in self.back:
            c.start()

    def plane(self):
        for c in self.back:
            c.wait_recv()
        self.own.wait()
        for c in self.first:
            c.start()

    def forward(self):
        self.first[0].wait_recv()
        self.next[0].start()
        self.first[1].wait_recv()
        self.next[1].start()
        self.first[2].wait_recv()
        self.next[2].start()
        self.first[3].wait_recv()
        self.next[3].start()

    def corner(self):
        self.next[0].wait_recv()
        self.next[1].wait_recv()
        self.next[4].start()

    def finish(self):
        self.first[4].wait_recv()
        for c in self.next[2:]:
            c.wait_recv()
        for c in self.out + self.back + self.first + self.next:
            c.wait_send()


class TableReduce:
    COUNT = 10

    def __init__(self, place, copy, first, table, part, from_core, from_x, from_y, diag, total, local):
        self.part, self.from_core, self.from_x, self.from_y = part, from_core, from_x, from_y
        self.diag, self.total = diag, total
        m = total.shape[0]
        self.m, self.h = m, m // 2
        h0, h1 = pl.ds(0, self.h), pl.ds(self.h, self.h)
        self.h0, self.h1 = h0, h1
        self.core = [
            copy(first + i, table.at[place.far[i]], from_core.at[i], place.pc) for i in range(4)
        ]
        self.load = [
            pltpu.make_async_copy(table.at[place.near[i]], part.at[i], local(i)) for i in range(4)
        ]
        self.d = [
            copy(first + 4, part.at[2, h0], diag.at[h0], place.px),
            copy(first + 5, part.at[2, h1], diag.at[h1], place.py),
        ]
        self.e = [
            copy(first + 6, part.at[1, h0], from_x.at[h0], place.px),
            copy(first + 7, part.at[3, h1], from_y.at[h1], place.py),
            copy(first + 8, part.at[1, h1], from_x.at[h1], place.px),
            copy(first + 9, part.at[3, h0], from_y.at[h0], place.py),
        ]

    def begin(self):
        for c in self.core + self.load:
            c.start()

    def merge(self):
        for i in (2, 1, 3, 0):
            self.load[i].wait()
            self.core[i].wait_recv()
            add_into(self.part.at[i], self.from_core.at[i], self.m, 16)
            if i == 2:
                self.d[0].start()
                self.d[1].start()
        self.e[0].start()
        self.e[1].start()

    def corner(self):
        self.d[0].wait_recv()
        add_into(self.part.at[3, self.h0], self.diag.at[self.h0], self.h, 16)
        self.e[3].start()
        self.d[1].wait_recv()
        add_into(self.part.at[1, self.h1], self.diag.at[self.h1], self.h, 16)
        self.e[2].start()

    def finish(self):
        for e in self.e:
            e.wait_recv()

        @pl.loop(0, self.m // 16)
        def _(i):
            at = span(i, 16)
            self.total[at, :] = (
                self.part[0, at, :].astype(f32)
                + self.from_x[at, :].astype(f32)
                + self.from_y[at, :].astype(f32)
            ).astype(bf16)

        for c in self.core + self.d + self.e:
            c.wait_send()


def attention_backward_kernel(
    grad_mixed, queries, kvp, kvc, attended, sums, narrow, heads_in, query_out, key_out, value_out,
    columns, cosine, sine, mix_table,
    normed_hbm, wall_hbm, feed_table, feed_share,
    grad_normed, g_feed_table, g_feed_share, g_head_table, g_head_share,
    normed_all, wall, g, delta, inv, dq, kv_own, kv_far, kv_send, kv_got, grad_pre, back, part,
    from_core, from_y,
    a_part, a_core, a_x, a_y, a_diag, a_total, a_in, a_piece,
    s_in, s_piece,
    h_table, h_part, h_core, h_x, h_y, h_diag, h_total, h_in, h_piece,
    o_table, o_got, o_total, o_in, o_piece,
    send, recv, local,
):
    rows, width = grad_normed.shape
    place = Places()
    b, z, planes = place.b, place.z, place.planes
    copy = sender(send, recv)
    loads = [
        pltpu.make_async_copy(normed_hbm, normed_all, local.at[0]),
        pltpu.make_async_copy(wall_hbm, wall, local.at[1]),
    ]
    for c in loads:
        c.start()
    barrier = pltpu.get_barrier_semaphore()
    peers = list(place.plane) + [place.up(d) for d in range(1, planes)]
    for peer in peers:
        pl.semaphore_signal(barrier, inc=1, device_id=peer, device_id_type=MESH)
    pl.semaphore_wait(barrier, len(peers))

    swaps = []
    for j, (peer, pb) in enumerate(
        ((place.py, place.b_y), (place.pyc, place.b_yc), (place.pc, place.b_c))
    ):
        for h in range(2):
            lanes = pl.ds(pl.multiple_of(pb * 2 * HEAD + h * HEAD, 128), HEAD)
            swaps.append(
                copy(
                    2 * j + h,
                    grad_mixed.at[:, lanes],
                    g.at[b, pl.ds(h * rows, rows)],
                    peer,
                )
            )
    for c in swaps:
        c.start()
    at = 12
    feed_reduce = TableReduce(
        place, copy, at, feed_table, a_part, a_core, a_x, a_y, a_diag, a_total,
        lambda i: local.at[2 + i],
    )
    at += TableReduce.COUNT
    feed_spread = TableSpread(place, copy, at, a_total, a_in, a_piece, g_feed_table, local.at[6])
    at += TableSpread.COUNT
    share_spread = TableSpread(
        place, copy, at, feed_share, s_in, s_piece, g_feed_share, local.at[7]
    )
    at += TableSpread.COUNT
    head_reduce = TableReduce(
        place, copy, at, h_table, h_part, h_core, h_x, h_y, h_diag, h_total,
        lambda i: local.at[8 + i],
    )
    at += TableReduce.COUNT
    head_spread = TableSpread(place, copy, at, h_total, h_in, h_piece, g_head_table, local.at[12])
    at += TableSpread.COUNT
    out_spread = TableSpread(place, copy, at, o_total, o_in, o_piece, g_head_share, local.at[13])
    at += TableSpread.COUNT
    lanes_half = o_total.shape[0]
    out_swap = copy(
        at, o_table.at[span(1 - place.x, lanes_half)], o_got, place.px
    )

    share_spread.scatter()
    feed_reduce.begin()
    for h in range(2):
        lanes = pl.ds(pl.multiple_of(b * 2 * HEAD + h * HEAD, 128), HEAD)
        g[b, h * rows : (h + 1) * rows, :] = grad_mixed[:, lanes]
    for c in swaps:
        c.wait()

    ones = jnp.ones((8, HEAD), f32)

    @pl.loop(0, 4)
    def _(t):
        for h in range(2):
            at_h = slice(h * rows, (h + 1) * rows)
            lanes = slice(h * HEAD, (h + 1) * HEAD)
            product = g[t, at_h, :].astype(f32) * attended[t, :, lanes].astype(f32)
            delta[t, :, at_h] = lax.dot_general(
                ones, product, (((1,), (1,)), ((), ())), precision=lax.Precision.HIGHEST,
                preferred_element_type=f32,
            )
        inv[t] = 1.0 / sums[t]

    query = lax.broadcasted_iota(jnp.int32, (rows, 2 * rows), 1) % rows
    causal = lax.broadcasted_iota(jnp.int32, (rows, 2 * rows), 0) <= query

    def step(t, k, v, total, slot, masked):
        q, gt = queries[t], g[t]
        th = jnp.tanh(dot_nt(k, q) * (1.0 / soft_cap))
        p = jnp.exp(soft_cap * th) * inv[t, 0:1, :]
        if masked:
            p = jnp.where(causal, p, 0.0)
        total[1, slot] += dot_nn(p.astype(bf16), gt)
        ds = (p * (dot_nt(v, gt) - delta[t, 0:1, :]) * (1.0 - th * th)).astype(bf16)
        total[0, slot] += dot_nn(ds, q)
        dq[t] += dot_tn(ds, k)

    dq[...] = jnp.zeros_like(dq)
    kv_own[...] = jnp.zeros_like(kv_own)

    def kv_copy(d):
        return copy(6 + d - 1, kv_send.at[d - 1], kv_got.at[d - 1], place.up(d))

    for d in range(1, planes):
        pass

    @pl.loop(1, planes)
    def _(d):
        zz = (z + d) % planes
        kv_far[...] = jnp.zeros_like(kv_far)
        step(1, kvp[zz, 0, 0], kvp[zz, 1, 0], kv_far, 0, False)

        @pl.when(zz < z)
        def _():
            step(0, kvp[zz, 0, 0], kvp[zz, 1, 0], kv_far, 0, False)
            step(1, kvp[zz, 0, 1], kvp[zz, 1, 1], kv_far, 1, False)

        @pl.loop(2, 4)
        def _(t):
            step(t, kvp[zz, 0, 0], kvp[zz, 1, 0], kv_far, 0, False)
            step(t, kvp[zz, 0, 1], kvp[zz, 1, 1], kv_far, 1, False)

        kv_send[d - 1] = kv_far[...].astype(bf16)
        for k in range(1, planes):

            @pl.when(d == k)
            def _(k=k):
                kv_copy(k).start()
                if k == 1:
                    feed_reduce.merge()
                    share_spread.gather()
                if k == 2:
                    feed_reduce.corner()
                    share_spread.plane()

    feed_reduce.finish()
    feed_spread.scatter()
    step(0, kvp[z, 0, 0], kvp[z, 1, 0], kv_own, 0, True)
    step(1, kvp[z, 0, 0], kvp[z, 1, 0], kv_own, 0, False)
    step(1, kvp[z, 0, 1], kvp[z, 1, 1], kv_own, 1, True)

    @pl.loop(2, 4)
    def _(t):
        step(t, kvc[0, t - 2], kvc[1, t - 2], kv_own, t, True)
        step(t, kvp[z, 0, 0], kvp[z, 1, 0], kv_own, 0, False)
        step(t, kvp[z, 0, 1], kvp[z, 1, 1], kv_own, 1, False)

    for c in loads:
        c.wait()
    feed_spread.gather()
    for d in range(1, planes):
        kv_copy(d).wait_recv()
        kv_own[:, 0:2] += kv_got[d - 1].astype(f32)
    half_head = HEAD // 2

    @pl.loop(0, 4)
    def _(t):
        at = span(t, rows)
        cos, sin = cosine[at, :], sine[at, :]
        masks = columns[at, :].astype(f32)

        def turned(pre, scale):
            first, second = pre[:, :half_head], pre[:, half_head:]
            one, two = first * cos + second * sin, second * cos - first * sin
            if scale != 1.0:
                one, two = one * scale, two * scale
            return jnp.concatenate([one, two], axis=1).astype(bf16)

        for h in range(2):
            grad_pre[at, h * HEAD : (h + 1) * HEAD] = turned(
                dq[t, h * rows : (h + 1) * rows, :], HEAD ** (-0.5)
            )
        grad_pre[at, 2 * HEAD : 3 * HEAD] = turned(kv_own[0, t], 1.0)
        grad_pre[at, 3 * HEAD :] = kv_own[1, t].astype(bf16)
        for i, (lanes, table) in enumerate(
            (
                (slice(0, 2 * HEAD), query_out),
                (slice(2 * HEAD, 3 * HEAD), key_out),
                (slice(3 * HEAD, 4 * HEAD), value_out),
            )
        ):
            back[at, i * LANES : (i + 1) * LANES] = (
                dot_nt(grad_pre[at, lanes], table[...]) * masks
            ).astype(bf16)

    share_spread.forward()
    for i, lanes in enumerate(
        (slice(0, 2 * HEAD), slice(2 * HEAD, 3 * HEAD), slice(3 * HEAD, 4 * HEAD))
    ):
        o_table[:, lanes] = dot_tn(
            narrow[:, i * LANES : (i + 1) * LANES], grad_pre[:, lanes]
        ).astype(bf16)
    out_swap.start()
    h_table[:, 3 * RANK :, :] = mix_table[...]

    @pl.loop(0, width // 384)
    def _(n):
        at = span(n, 384)
        got = dot_tn(back[...], normed_all[:, at]).astype(bf16)
        for i in range(3):
            for a in range(ADAPTERS):
                first = i * LANES + a * RANK
                h_table[a, i * RANK : (i + 1) * RANK, at] = got[first : first + RANK]

    head_reduce.begin()
    feed_spread.plane()

    def project(slot, target):
        at_rows = span(target, rows)

        @pl.loop(0, width // 384)
        def _(n):
            at = span(n, 384)
            part[slot, :, at] = (
                dot_nt(grad_pre[at_rows, :], wall[at, :])
                + dot_nn(back[at_rows, :], heads_in[:, at])
            ).astype(bf16)

    to_core = [copy(9 + i, part.at[i], from_core.at[i], place.pc) for i in range(2)]
    to_y = copy(11, part.at[2], from_y, place.py)
    project(0, place.b_yc)
    to_core[0].start()
    share_spread.corner()
    project(2, place.b_y)
    to_core[0].wait_recv()
    add_into(part.at[2], from_core.at[0], rows)
    to_y.start()
    head_reduce.merge()
    feed_spread.forward()
    out_swap.wait_recv()

    @pl.loop(0, lanes_half // 16)
    def _(i):
        at = span(i, 16)
        mine = pl.ds(pl.multiple_of(place.x * lanes_half + i * 16, 16), 16)
        o_total[at, :] = (o_table[mine, :].astype(f32) + o_got[at, :].astype(f32)).astype(bf16)

    out_spread.scatter()
    project(1, place.b_c)
    to_core[1].start()
    head_reduce.corner()
    feed_spread.corner()
    out_spread.gather()
    project(3, b)
    head_reduce.finish()
    head_spread.scatter()
    out_spread.plane()
    head_spread.gather()
    to_core[1].wait_recv()
    out_spread.forward()
    head_spread.plane()
    out_spread.corner()
    head_spread.forward()
    to_y.wait_recv()

    @pl.loop(0, rows // 32)
    def _(i):
        at = span(i, 32)
        grad_normed[at, :] = (
            part[3, at, :].astype(f32)
            + from_core[1, at, :].astype(f32)
            + from_y[at, :].astype(f32)
        ).astype(grad_normed.dtype)

    head_spread.corner()
    for spread in (share_spread, feed_spread, out_spread, head_spread):
        spread.finish()
    out_swap.wait_send()
    to_y.wait_send()
    for c in to_core:
        c.wait_send()
    for d in range(1, planes):
        kv_copy(d).wait_send()


def attention_backward(
    grad_mixed, kept, tables, columns, cosine, sine, mix_table, normed_all, wall, feed_table,
    feed_share,
):
    rows = grad_mixed.shape[0]
    width = wall.shape[0]
    planes = lax.axis_size("ulysses")
    m = feed_table.shape[1]
    fs, fw = feed_share.shape
    hm = 4 * RANK
    ow = 4 * HEAD
    om = LANES // 2
    count = 12 + 2 * TableReduce.COUNT + 4 * TableSpread.COUNT + 1

    def reduce_scratch(m):
        return [
            pltpu.VMEM((4, m, width), bf16),
            pltpu.VMEM((4, m, width), bf16),
            pltpu.VMEM((m, width), bf16),
            pltpu.VMEM((m, width), bf16),
            pltpu.VMEM((m, width), bf16),
            pltpu.VMEM((m, width), bf16),
        ]

    def spread_scratch(m, w):
        return [
            pltpu.VMEM((planes - 1, m // planes, w), bf16),
            pltpu.VMEM((m // planes, w), bf16),
        ]

    return pl.pallas_call(
        attention_backward_kernel,
        out_shape=(
            shape((rows, width), f32),
            shape((8, planes, m // planes, width), bf16),
            shape((8, planes, fs // planes, fw), bf16),
            shape((8, planes, hm // planes, width), bf16),
            shape((8, planes, om // planes, ow), bf16),
        ),
        in_specs=[VM] * 15 + [ANY] * 3 + [VM],
        out_specs=(VM, ANY, ANY, ANY, ANY),
        scratch_shapes=[
            pltpu.VMEM((4 * rows, width), bf16),
            pltpu.VMEM((width, 4 * HEAD), bf16),
            pltpu.VMEM((4, 2 * rows, HEAD), bf16),
            pltpu.VMEM((4, 8, 2 * rows), f32),
            pltpu.VMEM((4, 8, 2 * rows), f32),
            pltpu.VMEM((4, 2 * rows, HEAD), f32),
            pltpu.VMEM((2, 4, rows, HEAD), f32),
            pltpu.VMEM((2, 2, rows, HEAD), f32),
            pltpu.VMEM((planes - 1, 2, 2, rows, HEAD), bf16),
            pltpu.VMEM((planes - 1, 2, 2, rows, HEAD), bf16),
            pltpu.VMEM((4 * rows, 4 * HEAD), bf16),
            pltpu.VMEM((4 * rows, 3 * LANES), bf16),
            pltpu.VMEM((4, rows, width), bf16),
            pltpu.VMEM((2, rows, width), bf16),
            pltpu.VMEM((rows, width), bf16),
        ]
        + reduce_scratch(m)
        + spread_scratch(m, width)
        + spread_scratch(fs, fw)
        + [pltpu.VMEM((ADAPTERS, hm, width), bf16)]
        + reduce_scratch(hm)
        + spread_scratch(hm, width)
        + [
            pltpu.VMEM((LANES, ow), bf16),
            pltpu.VMEM((om, ow), bf16),
            pltpu.VMEM((om, ow), bf16),
        ]
        + spread_scratch(om, ow)
        + [
            pltpu.SemaphoreType.DMA((count,)),
            pltpu.SemaphoreType.DMA((count,)),
            pltpu.SemaphoreType.DMA((14,)),
        ],
        compiler_params=pltpu.CompilerParams(
            collective_id=4, has_side_effects=True, vmem_limit_bytes=62 << 20
        ),
        name="attention_backward",
    )(
        grad_mixed, *kept, *tables, columns, cosine, sine, mix_table, normed_all, wall, feed_table,
        feed_share,
    )


def take_columns(table, index, width):
    return lax.dynamic_slice_in_dim(table, index * width, width, axis=1)


def shards(
    tokens,
    query_weight,
    key_projection,
    value_projection,
    out_weight,
    gate_weight,
    up_weight,
    down_weight,
    attn_in_gain,
    attn_out_gain,
    feed_in_gain,
    feed_out_gain,
    adapt_heads_in,
    adapt_query_out,
    adapter_key_value_second,
    adapt_mix_in,
    adapt_mix_out,
    adapt_feed_in,
    adapt_feed_out,
    adapt_down_in,
    adapt_down_out,
    adapter_ids,
    cotangent,
):
    rows, width = tokens.shape
    blk_n = lax.axis_size("blk")
    z_n = lax.axis_size("ulysses")
    dp_n = lax.axis_size("dp")
    b = lax.axis_index("blk")
    z = lax.axis_index("ulysses")
    rank = lax.axis_index("dp") % 2 * blk_n + b
    ff = gate_weight.shape[1]
    share = ff // (2 * blk_n)
    weights = (
        query_weight, key_projection, value_projection, out_weight, gate_weight, up_weight,
        down_weight,
    )
    if dp_n > 2:
        weights = tuple(
            lax.dynamic_slice_in_dim(
                lax.all_gather(weight, PLANE, axis=0, tiled=True),
                rank * (weight.shape[0] * dp_n // 2),
                weight.shape[0] * dp_n // 2,
            )
            for weight in weights
        )
    down_rows = weights[6]

    block_first = (jnp.arange(blk_n, dtype=jnp.int32) * z_n + z) * rows
    sequence = jnp.where(block_first >= PROMPT, 1 + (block_first - PROMPT) // CONT, 0)
    all_ids = lax.all_gather(adapter_ids.astype(f32), "dp", axis=0, tiled=True).astype(jnp.int32)
    seq_ids = jnp.arange(CONTS + 1, dtype=jnp.int32)
    block_ids = jnp.sum(
        jnp.where(sequence[None, :, None] == seq_ids[None, None, :], all_ids[:, None, :], 0), axis=2
    )
    owner = jnp.arange(LANES, dtype=jnp.int32) // RANK
    block_masks = (block_ids[:, :, None] == owner).astype(f32)
    group_masks = lax.dynamic_index_in_dim(block_masks, lax.axis_index("dp"), 0, keepdims=False)
    own_mask = lax.dynamic_index_in_dim(group_masks, b, 0, keepdims=True)[0]
    group_columns = jnp.repeat(group_masks, rows, axis=0).astype(bf16)

    heads_in = jnp.transpose(adapt_heads_in, (1, 0, 2, 3)).reshape(3, LANES, width)
    query_out = take_columns(adapt_query_out.reshape(LANES, -1), b, 2 * HEAD)
    kv_out = jnp.transpose(adapter_key_value_second, (1, 0, 2, 3)).reshape(2, LANES, -1)
    key_out = take_columns(kv_out[0], b, HEAD)
    value_out = take_columns(kv_out[1], b, HEAD)
    mix_in = adapt_mix_in.reshape(LANES, -1)
    mix_out = adapt_mix_out.reshape(LANES, -1)
    feed_in = jnp.transpose(adapt_feed_in, (1, 0, 2, 3)).reshape(2, LANES, width)
    feed_out = jnp.transpose(adapt_feed_out, (1, 0, 2, 3)).reshape(2, LANES, ff)
    gate_out = take_columns(feed_out[0], rank, share)
    up_out = take_columns(feed_out[1], rank, share)
    down_in = take_columns(adapt_down_in.reshape(LANES, ff), rank, share)
    down_out = adapt_down_out.reshape(LANES, width)

    token_index = (block_first[:, None] + jnp.arange(rows, dtype=jnp.int32)).reshape(-1)
    positions = jnp.where(token_index >= PROMPT, PROMPT + (token_index - PROMPT) % CONT, token_index)
    half = HEAD // 2
    inverse = rope_base ** (-2.0 * jnp.arange(half, dtype=f32) / HEAD)
    angles = positions.astype(f32)[:, None] * inverse[None, :]
    cosine, sine = jnp.cos(angles), jnp.sin(angles)
    residual = tokens.astype(f32)
    (
        queries, kvp, kvc, attended, exp_sum, narrow_heads, mixed, narrow_mix, attn_out, middle,
        normed_feed, normed_all, head_weight, out_full, gate_share, up_share,
    ) = attention_forward(
        tokens,
        (attn_in_gain[None], attn_out_gain[None], feed_in_gain[None]),
        (heads_in.reshape(3 * LANES, width), query_out, key_out, value_out, mix_in, mix_out),
        group_columns,
        jnp.broadcast_to(own_mask, (rows, LANES)).astype(bf16),
        cosine,
        sine,
        weights[:6],
        share,
    )
    order = jnp.array([[0, 1], [4, 5], [6, 7], [2, 3]], dtype=jnp.int32)
    pair_masks = lax.dynamic_slice_in_dim(
        block_masks, lax.axis_index("dp") // 2 * 2, 2, axis=0
    ).reshape(8, LANES)
    plane_columns = jnp.repeat(
        jnp.take(pair_masks, (rank % 8) ^ order, axis=0), rows, axis=1
    ).reshape(4, 2 * rows, LANES).astype(bf16)
    feed_in2 = feed_in.reshape(2 * LANES, width)
    tables = (feed_in2, gate_out, up_out, down_in, down_out, plane_columns)
    branch, narrow_feed, feed_all, gate_up = feed_forward(
        normed_feed, *tables, gate_share, up_share, down_rows
    )
    layer_out = (middle + rms_scale(branch, feed_out_gain)).astype(bf16)
    grad_top = cotangent.astype(f32)
    grad_branch = norm_back(branch, feed_out_gain, grad_top).astype(bf16)
    grad_feed, back_feed, grad_feed_out, grad_down_in, grad_down_out = feed_backward(
        grad_branch, *tables, narrow_feed, gate_share, up_share, down_rows, gate_up
    )
    grad_feed = grad_feed.astype(f32)
    grad_feed_in = dot_tn(back_feed.reshape(-1, 2 * LANES), feed_all.reshape(-1, width))
    grad_middle = grad_top + norm_back(middle, feed_in_gain, grad_feed)
    grad_attn = norm_back(attn_out, attn_out_gain, grad_middle).astype(bf16)

    back_mix = (dot_nt(grad_attn, mix_out) * own_mask).astype(bf16)
    grad_mix_in, grad_mix_out = dot_tn(back_mix, mixed), dot_tn(narrow_mix, grad_attn)
    grad_mixed = (dot_nt(grad_attn, out_full) + dot_nn(back_mix, mix_in)).astype(bf16)
    def by_rank(table):
        return table.astype(bf16).reshape(-1, ADAPTERS, RANK, width).transpose(1, 0, 2, 3).reshape(
            ADAPTERS, -1, width
        )

    feed_table = by_rank(jnp.concatenate([grad_feed_in, grad_down_out, grad_mix_out]))
    feed_share = jnp.concatenate(
        [grad_feed_out.reshape(2 * LANES, share), grad_down_in]
    ).astype(bf16)
    mix_table = jnp.pad(
        grad_mix_in.astype(bf16).reshape(ADAPTERS, RANK, -1), ((0, 0), (0, 0), (0, width - mixed.shape[1]))
    )
    grad_normed, feed_rows, feed_columns, head_rows, head_columns = attention_backward(
        grad_mixed,
        (queries, kvp, kvc, attended, exp_sum, narrow_heads),
        (heads_in.reshape(3 * LANES, width), query_out, key_out, value_out),
        group_columns,
        cosine,
        sine,
        mix_table,
        normed_all,
        head_weight,
        feed_table,
        feed_share,
    )
    tokens_grad = grad_middle + norm_back(residual, attn_in_gain, grad_normed)

    feed_rows = feed_rows.reshape(ADAPTERS, 4, RANK, width)
    feed_columns = (
        feed_columns.reshape(8, 3, ADAPTERS, RANK, share)
        .transpose(2, 1, 3, 0, 4)
        .reshape(ADAPTERS, 3, RANK, ff)
    )
    head_rows = head_rows.reshape(ADAPTERS, 4, RANK, width)
    head_columns = (
        head_columns.reshape(2, 4, LANES // 2, 4 * HEAD)
        .transpose(0, 2, 1, 3)
        .reshape(ADAPTERS, RANK, 4, 4 * HEAD)
    )

    def joined(first, last):
        return head_columns[..., first:last].reshape(ADAPTERS, RANK, -1)

    summed = (
        head_rows[:, :3],
        joined(0, 2 * HEAD),
        jnp.stack([joined(2 * HEAD, 3 * HEAD), joined(3 * HEAD, 4 * HEAD)], axis=1),
        head_rows[:, 3, :, : mixed.shape[1]],
        feed_rows[:, 3],
        feed_rows[:, :2],
        feed_columns[:, :2],
        feed_columns[:, 2],
        feed_rows[:, 2],
    )
    summed = tuple(table.astype(f32) for table in summed)
    if dp_n > 2:
        summed = tuple(lax.psum(table * 0.5, "dp") for table in summed)
    return (layer_out, tokens_grad) + summed


def solution(mesh):
    sharded = P(EVERY, None)
    rowwise = P(PLANE, None)
    placed = (
        (sharded,) + (rowwise,) * 7 + (P(),) * 13 + (P("dp", None), sharded)
    )
    return jax.shard_map(
        shards,
        mesh=mesh,
        in_specs=placed,
        out_specs=(sharded, sharded) + (P(),) * 9,
        check_vma=False,
    )
```

```python
import math

import jax
import jax.numpy as jnp
from jax import lax
from jax.experimental import pallas as pl
from jax.experimental.pallas import tpu as pltpu
from jax.sharding import PartitionSpec as P

HEADS = 8
KV_HEADS = 4
HEAD = 256
RANK = 16
ADAPTERS = 8
LANES = RANK * ADAPTERS
PROMPT = 2048
CONT = 256
CONTS = 8

epsilon = 1e-06
soft_cap = 50.0
rope_base = 10000.0
PLANE = ("dp", "blk")
EVERY = ("dp", "blk", "ulysses")
f32 = jnp.float32
bf16 = jnp.bfloat16


def dot_nn(a, b):
    return jnp.dot(a, b, preferred_element_type=f32)


def dot_nt(a, b):
    return lax.dot_general(a, b, (((1,), (1,)), ((), ())), preferred_element_type=f32)


def dot_tn(a, b):
    return lax.dot_general(a, b, (((0,), (0,)), ((), ())), preferred_element_type=f32)


def norm_grad(values, gain_row, grad_out):
    scale = lax.rsqrt(jnp.mean(values * values, axis=-1, keepdims=True) + epsilon)
    weighted = grad_out * gain_row
    return scale * weighted - values * (
        scale * scale * scale * jnp.mean(values * weighted, axis=-1, keepdims=True)
    )


def shape(dims, dtype):
    return jax.ShapeDtypeStruct(dims, dtype)


VM = pl.BlockSpec(memory_space=pltpu.VMEM)


MESH = pl.DeviceIdType.MESH


def neighbours():
    dp, b, z = lax.axis_index("dp"), lax.axis_index("blk"), lax.axis_index("ulysses")
    across_x = (dp + 1 - 2 * (dp % 2), b, z)
    across_y = (dp, (b + 2) % 4, z)
    sibling = (dp, b + 1 - 2 * (b % 2), z)
    return across_x, across_y, sibling


def greet(peers):
    barrier = pltpu.get_barrier_semaphore()
    for peer in peers:
        pl.semaphore_signal(barrier, inc=1, device_id=peer, device_id_type=MESH)
    pl.semaphore_wait(barrier, len(peers))


def sender(send, recv):
    def copy(index, src, dst, peer):
        return pltpu.make_async_remote_copy(
            src, dst, send.at[index], recv.at[index], device_id=peer, device_id_type=MESH
        )

    return copy


def add_into(target, source, count, step=32):
    @pl.loop(0, count // step)
    def _(i):
        at = pl.ds(pl.multiple_of(i * step, step), step)
        target[at, :] = (target[at, :].astype(f32) + source[at, :].astype(f32)).astype(target.dtype)


class PlaneGather:
    COUNT = 10

    def __init__(self, copy, own, land, rows):
        px, py, pc = neighbours()
        h = rows // 2
        h0, h1 = pl.ds(0, h), pl.ds(h, h)
        near, far = pl.ds(0, rows), pl.ds(rows, rows)
        self.c = [
            copy(0, own, land.at[0, far], pc),
            copy(1, own.at[h0], land.at[1, h0], px),
            copy(2, own.at[h1], land.at[3, h1], py),
            copy(3, own.at[h1], land.at[1, h1], px),
            copy(4, own.at[h0], land.at[3, h0], py),
            copy(5, land.at[1, h0], land.at[2, h0], py),
            copy(6, land.at[3, h1], land.at[2, h1], px),
            copy(7, land.at[1, near], land.at[1, far], pc),
            copy(8, land.at[3, near], land.at[3, far], pc),
            copy(9, land.at[2, near], land.at[2, far], pc),
        ]

    def begin(self):
        for i in range(5):
            self.c[i].start()

    def before(self, i):
        c = self.c

        @pl.when(i == 0)
        def _():
            c[0].wait_recv()

        @pl.when(i == 1)
        def _():
            c[1].wait_recv()
            c[5].start()
            c[2].wait_recv()
            c[6].start()
            c[3].wait_recv()
            c[7].start()
            c[4].wait_recv()
            c[8].start()
            c[7].wait_recv()

        @pl.when(i == 2)
        def _():
            c[5].wait_recv()
            c[6].wait_recv()
            c[9].start()
            c[9].wait_recv()

        @pl.when(i == 3)
        def _():
            c[8].wait_recv()

    def finish(self):
        for c in self.c:
            c.wait_send()


def plane_masks(masks, i, rows):
    group = (i + 1) // 2 % 2
    near = (lax.axis_index("blk") + 2 * (i // 2)) % 4
    far = near + 1 - 2 * (near % 2)
    first = masks[group, pl.ds(near, 1), :]
    second = masks[group, pl.ds(far, 1), :]
    return jnp.where(
        lax.broadcasted_iota(jnp.int32, (2 * rows, LANES), 0) < rows, first, second
    )


def feed_table_copies(rank, share, feed_in_hbm, feed_out_hbm, down_in_hbm, feed_in, feed_out, down_in):
    lanes = pl.ds(pl.multiple_of(rank * share, 128), share)
    return [
        (feed_in_hbm.at[:, 0], feed_in.at[0]),
        (feed_in_hbm.at[:, 1], feed_in.at[1]),
        (feed_out_hbm.at[:, 0, :, lanes], feed_out.at[0]),
        (feed_out_hbm.at[:, 1, :, lanes], feed_out.at[1]),
        (down_in_hbm.at[:, :, lanes], down_in),
    ]


def feed_table_scratch(width, share):
    return [
        pltpu.VMEM((2, ADAPTERS, RANK, width), bf16),
        pltpu.VMEM((2, ADAPTERS, RANK, share), bf16),
        pltpu.VMEM((ADAPTERS, RANK, share), bf16),
    ]


class PlaneReduce:
    COUNT = 10

    def __init__(self, copy, part, odd, from_core, from_x, from_y, diag, rows, first):
        px, py, pc = neighbours()
        h = rows // 2
        self.h = h
        self.rows = rows
        h0, h1 = pl.ds(0, h), pl.ds(h, h)
        self.part, self.from_core = part, from_core
        self.from_x, self.from_y, self.diag = from_x, from_y, diag
        self.core = [
            copy(first + i, odd.at[i % 2], from_core.at[i], pc) for i in range(4)
        ]
        self.d = [
            copy(first + 4, part.at[2, h0], diag.at[h0], px),
            copy(first + 5, part.at[2, h1], diag.at[h1], py),
        ]
        self.e = [
            copy(first + 6, part.at[1, h0], from_x.at[h0], px),
            copy(first + 7, part.at[3, h1], from_y.at[h1], py),
            copy(first + 8, part.at[1, h1], from_x.at[h1], px),
            copy(first + 9, part.at[3, h0], from_y.at[h0], py),
        ]

    def merge(self, i):
        self.core[i].wait_recv()
        add_into(self.part.at[i], self.from_core.at[i], self.rows)

    def before(self, i):
        for k in (2, 3):

            @pl.when(i == k)
            def _(k=k):
                self.core[k - 2].wait_send()

    def after(self, i):
        for k in range(4):

            @pl.when(i == k)
            def _(k=k):
                self.core[k].start()
                if k == 2:
                    self.merge(1)
                    self.e[0].start()
                    self.merge(2)
                    self.d[0].start()
                    self.d[1].start()

    def finish(self, write, between=None):
        h, h0, h1 = self.h, pl.ds(0, self.h), pl.ds(self.h, self.h)
        self.merge(3)
        self.e[1].start()
        self.d[0].wait_recv()
        add_into(self.part.at[3, h0], self.diag.at[h0], h)
        self.e[3].start()
        self.d[1].wait_recv()
        add_into(self.part.at[1, h1], self.diag.at[h1], h)
        self.e[2].start()
        if between is not None:
            between()
        self.merge(0)
        for e in self.e:
            e.wait_recv()

        @pl.loop(0, self.rows // 32)
        def _(i):
            at = pl.ds(pl.multiple_of(i * 32, 32), 32)
            write(
                at,
                self.part[0, at, :].astype(f32)
                + self.from_x[at, :].astype(f32)
                + self.from_y[at, :].astype(f32),
            )

        for c in self.core[2:] + self.d + self.e:
            c.wait_send()


GELU_SLOPE = 0.7978845608028654
GELU_CUBE = 0.044715


def plane_rank():
    return lax.axis_index("dp") % 2 * 4 + lax.axis_index("blk")


def span(i, size):
    return pl.ds(pl.multiple_of(i * size, size), size)


def feed_forward_kernel(
    own, middle, cotangent, gains, masks, down_out, feed_in_hbm, feed_out_hbm, down_in_hbm,
    gate_hbm, up_hbm, down_hbm,
    layer_out, grad_branch, narrow, feed_all, gate_up,
    feed_in, feed_out, down_in, gate, up, down, land, hidden, saved, part, odd, from_core, from_x, from_y, diag,
    send, recv, load, store,
):
    rows = own.shape[0]
    share = gate.shape[1]
    width = own.shape[1]
    tile = 384
    loads = [
        pltpu.make_async_copy(s, d, load.at[i])
        for i, (s, d) in enumerate(
            [(gate_hbm, gate), (up_hbm, up), (down_hbm, down)]
            + feed_table_copies(
                plane_rank(), share, feed_in_hbm, feed_out_hbm, down_in_hbm, feed_in, feed_out,
                down_in,
            )
        )
    ]
    for c in loads:
        c.start()
    greet(neighbours())
    copy = sender(send, recv)
    gather = PlaneGather(copy, own, land, rows)
    reduce = PlaneReduce(
        copy, part, odd, from_core, from_x, from_y, diag, rows, PlaneGather.COUNT
    )
    gather.begin()
    land[0, :rows, :] = own[...]
    for c in loads:
        c.wait()

    def keep(i):
        slot = i % 2
        return (
            pltpu.make_async_copy(saved.at[slot], gate_up.at[i], store.at[slot]),
            pltpu.make_async_copy(land.at[i], feed_all.at[i], store.at[2 + slot]),
        )

    @pl.loop(0, 4)
    def _(i):
        gather.before(i)
        slot = i % 2

        @pl.when(i >= 2)
        def _():
            for c in keep(i - 2):
                c.wait()

        mask = plane_masks(masks, i, rows)
        for k in range(2):
            narrow[i, k] = (dot_nt(land[i], flat(feed_in[k])) * mask).astype(bf16)

        @pl.loop(0, share // tile)
        def _(n):
            at = span(n, tile)
            g = dot_nn(land[i], gate[:, at]) + dot_nn(narrow[i, 0], flat(feed_out[0, :, :, at]))
            u = dot_nn(land[i], up[:, at]) + dot_nn(narrow[i, 1], flat(feed_out[1, :, :, at]))
            saved[slot, 0, :, at] = g.astype(bf16)
            saved[slot, 1, :, at] = u.astype(bf16)
            th = jnp.tanh(GELU_SLOPE * (g + GELU_CUBE * g * g * g))
            hidden[:, at] = (0.5 * g * (1.0 + th) * u).astype(bf16)

        for c in keep(i):
            c.start()
        narrow[i, 2] = (dot_nt(hidden[...], flat(down_in[...])) * mask).astype(bf16)
        reduce.before(i)

        @pl.loop(0, width // tile)
        def _(n):
            at = span(n, tile)
            got = dot_nn(hidden[...], down[:, at]) + dot_nn(narrow[i, 2], down_out[:, at])
            got = got.astype(bf16)
            part[i, :, at] = got[:rows]
            odd[i % 2, :, at] = got[rows:]

        reduce.after(i)

    def write(at, branch):
        scale = lax.rsqrt(jnp.mean(branch * branch, axis=-1, keepdims=True) + epsilon)
        gain = gains[3:4, :]
        layer_out[at, :] = (middle[at, :].astype(f32) + branch * scale * gain).astype(bf16)
        grad_branch[at, :] = norm_grad(branch, gain, cotangent[at, :].astype(f32)).astype(bf16)

    reduce.finish(write)
    gather.finish()
    for i in (2, 3):
        for c in keep(i):
            c.wait()


def feed_backward_kernel(
    own, masks, down_out, narrow, feed_in_hbm, feed_out_hbm, down_in_hbm,
    gate_hbm, up_hbm, down_hbm, gate_up, feed_all,
    grad_feed, feed_table, share_sum,
    both, t_feed_out, t_down_in, t_down_out, share_table, share_in, share_piece,
    feed_in, feed_out, down_in, gate, up, down, land, saved, gg, gu, part, odd, from_core, from_x, from_y, diag,
    send, recv, load, fetch,
):
    rows = own.shape[0]
    share = gate.shape[1]
    width = own.shape[1]
    tile = 384
    loads = [
        pltpu.make_async_copy(s, d, load.at[i])
        for i, (s, d) in enumerate(
            [(down_hbm, down), (gate_hbm, gate), (up_hbm, up)]
            + feed_table_copies(
                plane_rank(), share, feed_in_hbm, feed_out_hbm, down_in_hbm, feed_in, feed_out,
                down_in,
            )
        )
    ]

    def bring(i):
        return pltpu.make_async_copy(gate_up.at[i], saved, fetch.at[0])

    for c in loads:
        c.start()
    bring(0).start()
    place = Places()
    greet(list(neighbours()) + [place.up(d) for d in range(1, place.planes)])
    copy = sender(send, recv)
    spread = TableSum(
        place, copy, PlaneGather.COUNT + PlaneReduce.COUNT, share_table, share_in, share_piece,
        lambda z: share_sum.at[z], fetch.at[1],
    )
    gather = PlaneGather(copy, own, land, rows)
    reduce = PlaneReduce(
        copy, part, odd, from_core, from_x, from_y, diag, rows, PlaneGather.COUNT
    )
    gather.begin()
    land[0, :rows, :] = own[...]
    t_feed_out[...] = jnp.zeros_like(t_feed_out)
    t_down_in[...] = jnp.zeros_like(t_down_in)
    t_down_out[...] = jnp.zeros_like(t_down_out)
    for c in loads:
        c.wait()

    @pl.loop(0, 4)
    def _(i):
        gather.before(i)
        bring(i).wait()
        mask = plane_masks(masks, i, rows)
        back = (dot_nt(land[i], down_out[...]) * mask).astype(bf16)

        @pl.loop(0, share // tile)
        def _(n):
            at = span(n, tile)
            gh = dot_nt(land[i], down[at, :]) + dot_nn(back, flat(down_in[:, :, at]))
            g = saved[0, :, at].astype(f32)
            u = saved[1, :, at].astype(f32)
            th = jnp.tanh(GELU_SLOPE * (g + GELU_CUBE * g * g * g))
            gelu = 0.5 * g * (1.0 + th)
            slope = 0.5 * (1.0 + th) + 0.5 * g * (1.0 - th * th) * GELU_SLOPE * (
                1.0 + 3.0 * GELU_CUBE * g * g
            )
            t_down_in[:, at] += dot_tn(back, (gelu * u).astype(bf16))
            gg[:, at] = (gh * u * slope).astype(bf16)
            gu[:, at] = (gh * gelu).astype(bf16)

        @pl.when(i < 3)
        def _():
            bring(i + 1).start()

        both[i, :, :LANES] = (dot_nt(gg[...], flat(feed_out[0])) * mask).astype(bf16)
        both[i, :, LANES:] = (dot_nt(gu[...], flat(feed_out[1])) * mask).astype(bf16)
        reduce.before(i)

        @pl.loop(0, width // tile)
        def _(n):
            at = span(n, tile)
            got = (
                dot_nt(gg[...], gate[at, :])
                + dot_nt(gu[...], up[at, :])
                + dot_nn(both[i, :, :LANES], flat(feed_in[0, :, :, at]))
                + dot_nn(both[i, :, LANES:], flat(feed_in[1, :, :, at]))
            ).astype(bf16)
            part[i, :, at] = got[:rows]
            odd[i % 2, :, at] = got[rows:]

        reduce.after(i)
        t_feed_out[0] += dot_tn(narrow[i, 0], gg[...])
        t_feed_out[1] += dot_tn(narrow[i, 1], gu[...])
        t_down_out[...] += dot_tn(narrow[i, 2], land[i])

    share_table[: 2 * LANES] = t_feed_out[...].reshape(2 * LANES, share).astype(bf16)
    share_table[2 * LANES :] = t_down_in[...].astype(bf16)
    spread.scatter()
    gather.finish()
    reload = [pltpu.make_async_copy(feed_all.at[i], land.at[i], fetch.at[2 + i]) for i in range(4)]
    for c in reload:
        c.start()

    def tables():
        spread.gather()
        for c in reload:
            c.wait()
        backs = both[...].reshape(8 * rows, 2 * LANES)

        @pl.loop(0, width // 256)
        def _(n):
            at = span(n, 256)
            got = dot_tn(backs, land[:, :, at].reshape(8 * rows, 256)).astype(bf16)
            last = t_down_out[:, at].astype(bf16)
            for a in range(ADAPTERS):
                first = slice(a * RANK, (a + 1) * RANK)
                second = slice(LANES + a * RANK, LANES + (a + 1) * RANK)
                feed_table[a, :RANK, at] = got[first]
                feed_table[a, RANK : 2 * RANK, at] = got[second]
                feed_table[a, 2 * RANK :, at] = last[first]

    def write(at, total):
        grad_feed[at, :] = total.astype(grad_feed.dtype)

    reduce.finish(write, tables)
    spread.finish()


def feed_scratch(rows, width, extra=0):
    count = PlaneGather.COUNT + PlaneReduce.COUNT + extra
    return [
        pltpu.VMEM((4, rows, width), bf16),
        pltpu.VMEM((2, rows, width), bf16),
        pltpu.VMEM((4, rows, width), bf16),
        pltpu.VMEM((rows, width), bf16),
        pltpu.VMEM((rows, width), bf16),
        pltpu.VMEM((rows, width), bf16),
        pltpu.SemaphoreType.DMA((count,)),
        pltpu.SemaphoreType.DMA((count,)),
    ]


ANY = pl.BlockSpec(memory_space=pl.ANY)


def feed_forward(own, middle, cotangent, gains, masks, down_out, tables, gate, up, down):
    rows, width = own.shape
    share = gate.shape[1]
    return pl.pallas_call(
        feed_forward_kernel,
        out_shape=(
            shape((rows, width), bf16),
            shape((rows, width), bf16),
            shape((4, 3, 2 * rows, LANES), bf16),
            shape((4, 2 * rows, width), bf16),
            shape((4, 2, 2 * rows, share), bf16),
        ),
        in_specs=[VM] * 6 + [ANY] * 6,
        out_specs=(VM, VM, VM, ANY, ANY),
        scratch_shapes=feed_table_scratch(width, share)
        + [
            pltpu.VMEM(gate.shape, bf16),
            pltpu.VMEM(up.shape, bf16),
            pltpu.VMEM(down.shape, bf16),
            pltpu.VMEM((4, 2 * rows, width), bf16),
            pltpu.VMEM((2 * rows, share), bf16),
            pltpu.VMEM((2, 2, 2 * rows, share), bf16),
        ]
        + feed_scratch(rows, width)
        + [pltpu.SemaphoreType.DMA((8,)), pltpu.SemaphoreType.DMA((4,))],
        compiler_params=pltpu.CompilerParams(
            collective_id=1, has_side_effects=True, vmem_limit_bytes=62 << 20
        ),
        name="feed_forward",
    )(own, middle, cotangent, gains, masks, down_out, *tables, gate, up, down)


def feed_backward(own, masks, down_out, narrow, tables, gate, up, down, gate_up, feed_all):
    rows, width = own.shape
    share = gate.shape[1]
    planes = lax.axis_size("ulysses")
    piece = 3 * LANES // planes
    return pl.pallas_call(
        feed_backward_kernel,
        out_shape=(
            shape((rows, width), bf16),
            shape((ADAPTERS, 3 * RANK, width), bf16),
            shape((planes, piece, share), bf16),
        ),
        in_specs=[VM] * 4 + [ANY] * 8,
        out_specs=(VM, VM, ANY),
        scratch_shapes=[
            pltpu.VMEM((4, 2 * rows, 2 * LANES), bf16),
            pltpu.VMEM((2, LANES, share), f32),
            pltpu.VMEM((LANES, share), f32),
            pltpu.VMEM((LANES, width), f32),
            pltpu.VMEM((3 * LANES, share), bf16),
            pltpu.VMEM((planes - 1, piece, share), bf16),
            pltpu.VMEM((piece, share), bf16),
        ]
        + feed_table_scratch(width, share)
        + [
            pltpu.VMEM(gate.shape, bf16),
            pltpu.VMEM(up.shape, bf16),
            pltpu.VMEM(down.shape, bf16),
            pltpu.VMEM((4, 2 * rows, width), bf16),
            pltpu.VMEM((2, 2 * rows, share), bf16),
            pltpu.VMEM((2 * rows, share), bf16),
            pltpu.VMEM((2 * rows, share), bf16),
        ]
        + feed_scratch(rows, width, TableSum.COUNT)
        + [pltpu.SemaphoreType.DMA((8,)), pltpu.SemaphoreType.DMA((6,))],
        compiler_params=pltpu.CompilerParams(
            collective_id=2, has_side_effects=True, vmem_limit_bytes=62 << 20
        ),
        name="feed_backward",
    )(own, masks, down_out, narrow, *tables, gate, up, down, gate_up, feed_all)


def flat(table):
    return table.reshape(LANES, table.shape[-1])


def head_table_copies(
    b, heads_hbm, query_out_hbm, kv_out_hbm, heads_in, query_out, key_out, value_out
):
    lanes = pl.ds(pl.multiple_of(b * 2 * HEAD, 128), 2 * HEAD)
    lane = pl.ds(pl.multiple_of(b * HEAD, 128), HEAD)
    return [(heads_hbm.at[:, i], heads_in.at[i]) for i in range(3)] + [
        (query_out_hbm.at[:, :, lanes], query_out),
        (kv_out_hbm.at[:, 0, :, lane], key_out),
        (kv_out_hbm.at[:, 1, :, lane], value_out),
    ]


def head_table_scratch(width):
    return [
        pltpu.VMEM((3, ADAPTERS, RANK, width), bf16),
        pltpu.VMEM((ADAPTERS, RANK, 2 * HEAD), bf16),
        pltpu.VMEM((ADAPTERS, RANK, HEAD), bf16),
        pltpu.VMEM((ADAPTERS, RANK, HEAD), bf16),
    ]


def adapter_mask(ids, t, z, planes, rows):
    sequence = 0 if t * planes * rows < PROMPT else 1 + ((t * planes + z) * rows - PROMPT) // CONT
    owner = lax.broadcasted_iota(jnp.int32, (1, LANES), 1) // RANK
    return jnp.where(owner == ids[0, sequence], 1.0, 0.0)


def rms_rows(source, gains, which, target, rows, add=None):
    gain = gains.at[pl.ds(which, 1)]

    @pl.loop(0, rows // 32)
    def _(i):
        at = span(i, 32)
        v = source[at, :].astype(f32)
        out = v * lax.rsqrt(jnp.mean(v * v, axis=-1, keepdims=True) + epsilon) * gain[...]
        if add is not None:
            out = out + add[at, :].astype(f32)
        target[at, :] = out.astype(target.dtype)


def attention_forward_kernel(
    tokens, gains, ids, mix_in, mix_out, heads_hbm, query_out_hbm, kv_out_hbm,
    query_hbm, key_hbm, value_hbm, out_hbm, gate_hbm, up_hbm,
    queries, values_prompt, values_cont, attended, sums, narrow, mixed_out, narrow_mix,
    attn_out_out, middle_out, normed_feed, cosine, sine, masks_out, normed_out, wall_out, out_out, gate_share,
    up_share,
    heads_in, query_out, key_out, value_out, masks, masks_got, attn_out, middle,
    normed_all, wall, wo, kvp, kvc, acc, total, mixed, send, recv, local,
):
    rows, width = tokens.shape
    dp, b, z = lax.axis_index("dp"), lax.axis_index("blk"), lax.axis_index("ulysses")
    planes = lax.axis_size("ulysses")
    x, y, c = dp % 2, b // 2, b % 2
    base = dp - x
    rank = x * 4 + b
    b_c, b_y = b + 1 - 2 * c, (b + 2) % 4
    b_yc = (b_c + 2) % 4
    pc, py, pyc = (dp, b_c, z), (dp, b_y, z), (dp, b_yc, z)
    other = base + 1 - x
    px, pxc, pxy, pxyc = (other, b, z), (other, b_c, z), (other, b_y, z), (other, b_yc, z)
    pz = (dp, b, z + 1 - 2 * (z % 2))
    left, right = (dp, b, z - 1), (dp, b, z + 1)
    depth = query_hbm.shape[0]
    share = gate_share.shape[1]
    part = out_hbm.shape[0]
    copy = sender(send, recv)

    def block(i):
        return span(i, rows)

    def weight_rows(i):
        return pl.ds(pl.multiple_of(i * depth, 16), depth)

    def out_rows(i):
        return span(i, part)

    heads = ((query_hbm, 2 * HEAD, 0), (key_hbm, HEAD, 2 * HEAD), (value_hbm, HEAD, 3 * HEAD))

    def columns_of(ref, target, size):
        return ref.at[:, pl.ds(pl.multiple_of(target * size, 128), size)]

    own_loads = [
        pltpu.make_async_copy(
            columns_of(ref, b, size), wall.at[weight_rows(rank), pl.ds(to, size)], local.at[i]
        )
        for i, (ref, size, to) in enumerate(heads)
    ]
    own_loads.append(pltpu.make_async_copy(out_hbm, wo.at[out_rows(rank)], local.at[3]))
    table_loads = [
        pltpu.make_async_copy(src, dst, local.at[12 + i])
        for i, (src, dst) in enumerate(
            head_table_copies(
                b, heads_hbm, query_out_hbm, kv_out_hbm, heads_in, query_out, key_out, value_out
            )
        )
    ]
    own_rows = [
        pltpu.make_async_copy(
            columns_of(ref, rank, share), out.at[weight_rows(rank)], local.at[4 + i]
        )
        for i, (ref, out) in enumerate(((gate_hbm, gate_share), (up_hbm, up_share)))
    ]
    for cp in own_loads + table_loads:
        cp.start()

    barrier = pltpu.get_barrier_semaphore()
    for peer in (pc, py, pyc, px, pxc, pxy, pxyc) + tuple(
        (dp, b, (z + d) % planes) for d in range(1, planes)
    ):
        pl.semaphore_signal(barrier, inc=1, device_id=peer, device_id_type=MESH)

    rms_rows(tokens, gains, 0, normed_all.at[block(b)], rows)
    masks[...] = jnp.zeros_like(masks)
    for t in range(4):
        masks[t : t + 1, :] = adapter_mask(ids, t, z, planes, rows)
    masks_out[0] = masks[...]
    pl.semaphore_wait(barrier, 6 + planes)

    stage = []
    for j, (peer, pb) in enumerate(((py, b_y), (pyc, b_yc), (pc, b_c))):
        for i, (ref, size, to) in enumerate(heads):
            stage.append(
                copy(
                    3 + 3 * j + i,
                    columns_of(ref, pb, size),
                    wall.at[weight_rows(rank), pl.ds(to, size)],
                    peer,
                )
            )
    token_copies = [
        copy(0, normed_all.at[block(b)], normed_all.at[block(b)], py),
        copy(1, normed_all.at[block(b)], normed_all.at[block(b)], pc),
        copy(2, normed_all.at[block(b_y)], normed_all.at[block(b_y)], pc),
    ]
    across = [
        copy(12 + i, wall.at[weight_rows(x * 4 + o)], wall.at[weight_rows(x * 4 + o)], px)
        for i, o in enumerate((b, b_c, b_y, b_yc))
    ]
    for cp in stage[:3]:
        cp.start()
    token_copies[0].start()
    for cp in stage[3:]:
        cp.start()
    token_copies[1].start()
    mask_copy = copy(34, masks, masks_got, px)
    mask_copy.start()
    for cp in own_loads[:3]:
        cp.wait()
    across[0].start()
    for cp in stage[6:]:
        cp.wait_recv()
    across[1].start()
    for cp in stage[:3]:
        cp.wait_recv()
    across[2].start()
    for cp in stage[3:6]:
        cp.wait_recv()
    across[3].start()
    token_copies[0].wait_recv()
    token_copies[2].start()
    lane = lax.broadcasted_iota(jnp.int32, (rows, HEAD // 2), 1).astype(f32)
    inverse = jnp.exp(lane * (-2.0 / HEAD * math.log(rope_base)))

    @pl.loop(0, 4)
    def _(t):
        at = block(t)
        token = (t * planes + z) * rows + lax.broadcasted_iota(jnp.int32, (rows, HEAD // 2), 0)
        position = jnp.where(token >= PROMPT, PROMPT + (token - PROMPT) % CONT, token)
        angle = position.astype(f32) * inverse
        cosine[at, :] = jnp.cos(angle)
        sine[at, :] = jnp.sin(angle)

    for cp in table_loads:
        cp.wait()
    mask_copy.wait()
    masks_out[1] = masks_got[...]

    half = part // 2
    rx, ry, rxy = (1 - x) * 4 + b, x * 4 + b_y, (1 - x) * 4 + b_y

    def wo_part(r, h):
        return wo.at[pl.ds(pl.multiple_of(r * part + h * half, 16), half)]

    wo_first = [
        (16, wo_part(rank, 0), px),
        (17, wo_part(rank, 1), py),
        (18, wo_part(rank, 1), px),
        (19, wo_part(rank, 0), py),
        (20, wo.at[out_rows(rank)], pc),
    ]
    wo_next = [
        (21, wo_part(rx, 0), py),
        (22, wo_part(ry, 1), px),
        (23, wo.at[out_rows(rx)], pc),
        (24, wo.at[out_rows(ry)], pc),
        (25, wo.at[out_rows(rxy)], pc),
    ]
    wo_first = [copy(i, ref, ref, peer) for i, ref, peer in wo_first]
    wo_next = [copy(i, ref, ref, peer) for i, ref, peer in wo_next]
    swaps = [
        copy(26 + i, columns_of(ref, x * 4 + b_c, share), out.at[weight_rows(rank)], pc)
        for i, (ref, out) in enumerate(((gate_hbm, gate_share), (up_hbm, up_share)))
    ]
    chips = (
        ((px, rx), (pxc, (1 - x) * 4 + b_c)),
        ((py, ry), (pyc, x * 4 + b_yc)),
        ((pxy, rxy), (pxyc, (1 - x) * 4 + b_yc)),
    )
    got_ranks = (
        (1 - x) * 4 + y * 2 + z % 2, x * 4 + (1 - y) * 2 + z % 2, (1 - x) * 4 + (1 - y) * 2 + z % 2,
    )
    direct, relay, whole = {}, {}, []
    for n, targets in enumerate(chips):
        for i, (ref, out) in enumerate(((gate_hbm, gate_share), (up_hbm, up_share))):
            kind = 2 * n + i
            if kind in (0, 2):
                whole += [
                    copy(63 + kind + j, columns_of(ref, pr, share), out.at[weight_rows(rank)], peer)
                    for j, (peer, pr) in enumerate(targets)
                ]
                continue
            direct[kind] = [
                pltpu.make_async_remote_copy(
                    columns_of(ref, pr, share),
                    out.at[weight_rows(rank)],
                    send.at[51 + 2 * kind + j],
                    recv.at[51 + kind],
                    device_id=peer,
                    device_id_type=MESH,
                )
                for j, (peer, pr) in enumerate(targets)
            ]
            got = out.at[weight_rows(got_ranks[n])]
            relay[kind] = copy(28 + kind, got, got, pz)

    def send_direct(kinds):
        @pl.when(c == z % 2)
        def _():
            for kind in kinds:
                for cp in direct[kind]:
                    cp.start()

    def pass_along(kinds):
        for kind in kinds:
            direct[kind][0].wait_recv()
            relay[kind].start()

    own_loads[3].wait()
    for cp in across:
        cp.wait_recv()
    for cp in wo_first:
        cp.start()
    send_direct((4, 5))
    for cp in swaps + own_rows:
        cp.start()
    token_copies[1].wait_recv()
    token_copies[2].wait_recv()

    outs = [
        pltpu.make_async_copy(normed_all, normed_out, local.at[6]),
        pltpu.make_async_copy(wall, wall_out, local.at[7]),
        pltpu.make_async_copy(wo, out_out, local.at[8]),
        pltpu.make_async_copy(kvp, values_prompt, local.at[9]),
        pltpu.make_async_copy(kvc, values_cont, local.at[10]),
        pltpu.make_async_copy(mixed, mixed_out, local.at[11]),
    ]
    outs[0].start()
    outs[1].start()

    half_head = HEAD // 2

    @pl.loop(0, 4)
    def _(t):
        at = block(t)
        mask = masks[pl.ds(t, 1), :]
        cos, sin = cosine[at, :], sine[at, :]
        a = normed_all[at, :]
        for i in range(3):
            lanes = slice(i * LANES, (i + 1) * LANES)
            narrow[at, lanes] = (dot_nt(a, flat(heads_in[i])) * mask).astype(bf16)

        def turned(pre, scale):
            first, second = pre[:, :half_head], pre[:, half_head:]
            one, two = first * cos - second * sin, second * cos + first * sin
            if scale != 1.0:
                one, two = one * scale, two * scale
            return jnp.concatenate([one, two], axis=1).astype(bf16)

        for h in range(2):
            lanes = slice(h * HEAD, (h + 1) * HEAD)
            pre = dot_nn(a, wall[:, lanes]) + dot_nn(
                narrow[at, :LANES], flat(query_out[:, :, lanes])
            )
            queries[t, h * rows : (h + 1) * rows, :] = turned(pre, HEAD ** (-0.5))
        pre = dot_nn(a, wall[:, 2 * HEAD : 3 * HEAD]) + dot_nn(
            narrow[at, LANES : 2 * LANES], flat(key_out[...])
        )
        key = turned(pre, 1.0)
        value = (
            dot_nn(a, wall[:, 3 * HEAD :]) + dot_nn(
                narrow[at, 2 * LANES :], flat(value_out[...])
            )
        ).astype(bf16)

        @pl.when(t < 2)
        def _():
            kvp[z, 0, t] = key
            kvp[z, 1, t] = value

        @pl.when(t >= 2)
        def _():
            kvc[0, t - 2] = key
            kvc[1, t - 2] = value

    def hop(direction, d):
        index = 42 + d if direction > 0 else 45 + d
        zz = z - d * direction
        return copy(index, kvp.at[zz], kvp.at[zz], right if direction > 0 else left)

    def pass_on(direction, d):
        reach = z < planes - 1 if direction > 0 else z > 0

        @pl.when(reach)
        def _():
            hop(direction, d).start()

    pass_on(1, 0)
    pass_on(-1, 0)

    send_direct((1, 3))
    acc[...] = jnp.zeros_like(acc)
    total[...] = jnp.zeros_like(total)
    row = lax.broadcasted_iota(jnp.int32, (2 * rows, rows), 0) % rows
    causal = lax.broadcasted_iota(jnp.int32, (2 * rows, rows), 1) <= row

    def step(t, k, v, masked):
        e = jnp.exp(soft_cap * jnp.tanh(dot_nt(queries[t], k) * (1.0 / soft_cap)))
        if masked:
            e = jnp.where(causal, e, 0.0)
        some = e[:, :128]
        for n in range(128, rows, 128):
            some = some + e[:, n : n + 128]
        total[t] += some
        acc[t] += dot_nn(e.astype(bf16), v)

    step(0, kvp[z, 0, 0], kvp[z, 1, 0], True)
    step(1, kvp[z, 0, 0], kvp[z, 1, 0], False)
    step(1, kvp[z, 0, 1], kvp[z, 1, 1], True)

    @pl.loop(2, 4)
    def _(t):
        step(t, kvc[0, t - 2], kvc[1, t - 2], True)
        step(t, kvp[z, 0, 0], kvp[z, 1, 0], False)
        step(t, kvp[z, 0, 1], kvp[z, 1, 1], False)

    for cp in whole:
        cp.start()
    wo_first[0].wait_recv()
    wo_next[0].start()
    wo_first[1].wait_recv()
    wo_next[1].start()

    @pl.loop(0, 2 * (planes - 1))
    def _(i):
        d = i // 2 + 1
        direction = 1 - 2 * (i % 2)
        zz = z - d * direction

        @pl.when(i == 2)
        def _():
            pass_along((4, 5))

        @pl.when((zz >= 0) & (zz < planes))
        def _():
            index = 42 + 3 * (i % 2) + d - 1
            here = pltpu.make_async_remote_copy(
                kvp.at[zz], kvp.at[zz], send.at[index], recv.at[index], device_id=left,
                device_id_type=MESH,
            )
            here.wait_recv()

            @pl.when((i % 2 == 0) & (z < planes - 1))
            def _():
                pltpu.make_async_remote_copy(
                    kvp.at[zz], kvp.at[zz], send.at[index + 1], recv.at[index + 1],
                    device_id=right, device_id_type=MESH,
                ).start()

            @pl.when((i % 2 == 1) & (z > 0))
            def _():
                pltpu.make_async_remote_copy(
                    kvp.at[zz], kvp.at[zz], send.at[index + 1], recv.at[index + 1],
                    device_id=left, device_id_type=MESH,
                ).start()

            step(1, kvp[zz, 0, 0], kvp[zz, 1, 0], False)

            @pl.when(zz < z)
            def _():
                step(0, kvp[zz, 0, 0], kvp[zz, 1, 0], False)
                step(1, kvp[zz, 0, 1], kvp[zz, 1, 1], False)

            @pl.loop(2, 4)
            def _(t):
                step(t, kvp[zz, 0, 0], kvp[zz, 1, 0], False)
                step(t, kvp[zz, 0, 1], kvp[zz, 1, 1], False)

    outs[3].start()
    outs[4].start()
    ones = jnp.ones((8, 128), f32)

    @pl.loop(0, 4)
    def _(t):
        whole = jnp.sum(total[t], axis=1, keepdims=True)
        got = (acc[t] / whole).astype(bf16)
        attended[t, :, :HEAD] = got[:rows]
        attended[t, :, HEAD:] = got[rows:]
        sums[t] = lax.dot_general(
            ones, total[t], (((1,), (1,)), ((), ())), precision=lax.Precision.HIGHEST,
            preferred_element_type=f32,
        )

    lanes = pl.ds(pl.multiple_of(b * 2 * HEAD, 128), 2 * HEAD)
    mixes = [
        copy(48 + i, attended.at[o], mixed.at[:, lanes], peer)
        for i, (peer, o) in enumerate(((py, b_y), (pyc, b_yc), (pc, b_c)))
    ]
    for cp in mixes:
        cp.start()
    mixed[:, lanes] = attended[b]
    pass_along((1, 3))
    wo_first[2].wait_recv()
    wo_next[2].start()
    wo_first[3].wait_recv()
    wo_next[3].start()
    wo_next[0].wait_recv()
    wo_next[1].wait_recv()
    wo_next[4].start()
    wo_first[4].wait_recv()
    for cp in wo_next[2:]:
        cp.wait_recv()
    for cp in mixes:
        cp.wait_recv()
    outs[2].start()
    outs[5].start()
    narrow_mix[...] = (dot_nt(mixed[...], mix_in[...]) * masks[pl.ds(b, 1), :]).astype(bf16)

    @pl.loop(0, width // 384)
    def _(n):
        at = span(n, 384)
        attn_out[:, at] = dot_nn(mixed[...], wo[:, at]) + dot_nn(narrow_mix[...], mix_out[:, at])

    rms_rows(attn_out, gains, 1, middle, rows, add=tokens)
    rms_rows(middle, gains, 2, normed_feed, rows)
    attn_out_out[...] = attn_out[...].astype(bf16)
    middle_out[...] = middle[...].astype(bf16)

    for cp in swaps + whole:
        cp.wait()
    for cp in relay.values():
        cp.wait()

    @pl.when(c == z % 2)
    def _():
        for pair in direct.values():
            for cp in pair:
                cp.wait_send()

    for cp in own_rows + outs:
        cp.wait()
    for cp in stage + token_copies + across + wo_first + wo_next + mixes:
        cp.wait_send()

    @pl.loop(0, 2 * (planes - 1))
    def _(i):
        d = i // 2
        direction = 1 - 2 * (i % 2)
        zz = z - d * direction
        onward = z + direction

        @pl.when((zz >= 0) & (zz < planes) & (onward >= 0) & (onward < planes))
        def _():
            index = 42 + 3 * (i % 2) + d
            pltpu.make_async_remote_copy(
                kvp.at[zz], kvp.at[zz], send.at[index], recv.at[index], device_id=left,
                device_id_type=MESH,
            ).wait_send()


def attention_forward(tokens, gains, ids, mix_in, mix_out, tables, weights, share):
    rows, width = tokens.shape
    planes = lax.axis_size("ulysses")
    return pl.pallas_call(
        attention_forward_kernel,
        out_shape=(
            shape((4, 2 * rows, HEAD), bf16),
            shape((planes, 2, 2, rows, HEAD), bf16),
            shape((2, 2, rows, HEAD), bf16),
            shape((4, rows, 2 * HEAD), bf16),
            shape((4, 8, 2 * rows), f32),
            shape((4 * rows, 3 * LANES), bf16),
            shape((rows, 8 * HEAD), bf16),
            shape((rows, LANES), bf16),
            shape((rows, width), bf16),
            shape((rows, width), bf16),
            shape((rows, width), bf16),
            shape((4 * rows, HEAD // 2), f32),
            shape((4 * rows, HEAD // 2), f32),
            shape((2, 16, LANES), f32),
            shape((4 * rows, width), bf16),
            shape((width, 4 * HEAD), bf16),
            shape((8 * HEAD, width), bf16),
            shape((width, share), bf16),
            shape((width, share), bf16),
        ),
        in_specs=[VM, VM, pl.BlockSpec(memory_space=pltpu.SMEM), VM, VM] + [ANY] * 9,
        out_specs=(VM, ANY, ANY, VM, VM, VM, ANY) + (VM,) * 7 + (ANY,) * 5,
        scratch_shapes=head_table_scratch(width)
        + [
            pltpu.VMEM((16, LANES), f32),
            pltpu.VMEM((16, LANES), f32),
            pltpu.VMEM((rows, width), f32),
            pltpu.VMEM((rows, width), f32),
            pltpu.VMEM((4 * rows, width), bf16),
            pltpu.VMEM((width, 4 * HEAD), bf16),
            pltpu.VMEM((8 * HEAD, width), bf16),
            pltpu.VMEM((planes, 2, 2, rows, HEAD), bf16),
            pltpu.VMEM((2, 2, rows, HEAD), bf16),
            pltpu.VMEM((4, 2 * rows, HEAD), f32),
            pltpu.VMEM((4, 2 * rows, 128), f32),
            pltpu.VMEM((rows, 8 * HEAD), bf16),
            pltpu.SemaphoreType.DMA((67,)),
            pltpu.SemaphoreType.DMA((67,)),
            pltpu.SemaphoreType.DMA((18,)),
        ],
        compiler_params=pltpu.CompilerParams(
            collective_id=3, has_side_effects=True, vmem_limit_bytes=62 << 20
        ),
        name="attention_forward",
    )(tokens, gains, ids, mix_in, mix_out, *tables, *weights)


class Places:
    def __init__(self):
        dp, b, z = lax.axis_index("dp"), lax.axis_index("blk"), lax.axis_index("ulysses")
        self.b, self.z, self.planes = b, z, lax.axis_size("ulysses")
        x, c = dp % 2, b % 2
        self.x, self.y, self.c = x, b // 2, c
        self.b_c, self.b_y = b + 1 - 2 * c, (b + 2) % 4
        self.b_yc = (self.b_c + 2) % 4
        other = dp + 1 - 2 * x
        self.dp, self.other = dp, other
        self.pc, self.py, self.pyc = (dp, self.b_c, z), (dp, self.b_y, z), (dp, self.b_yc, z)
        self.px = (other, b, z)
        self.plane = (
            self.pc, self.py, self.pyc, self.px,
            (other, self.b_c, z), (other, self.b_y, z), (other, self.b_yc, z),
        )
        self.rank = x * 4 + b
        self.near = (x * 4 + b, (1 - x) * 4 + b, (1 - x) * 4 + self.b_y, x * 4 + self.b_y)
        self.far = (x * 4 + self.b_c, (1 - x) * 4 + self.b_c, (1 - x) * 4 + self.b_yc, x * 4 + self.b_yc)

    def along(self, d):
        return (self.z + d) % self.planes

    def up(self, d):
        return (self.dp, self.b, self.along(d))


class TableSum:
    COUNT = 6

    def __init__(self, place, copy, first, source, arrived, piece, target, local):
        self.place, self.source, self.arrived, self.piece = place, source, arrived, piece
        n = place.planes
        self.q = piece.shape[0]
        self.out = [
            copy(first + d - 1, source.at[span(place.along(d), self.q)], arrived.at[d - 1], place.up(d))
            for d in range(1, n)
        ]
        self.own = pltpu.make_async_copy(piece, target(place.z), local)
        self.back = [
            copy(first + 2 + d, piece, target(place.z), place.up(d)) for d in range(1, n)
        ]

    def scatter(self):
        for c in self.out:
            c.start()

    def gather(self):
        for c in self.out:
            c.wait_recv()
        got = self.source[span(self.place.z, self.q), :].astype(f32)
        for i in range(self.place.planes - 1):
            got = got + self.arrived[i].astype(f32)
        self.piece[...] = got.astype(bf16)
        self.own.start()
        for c in self.back:
            c.start()

    def ready(self):
        for c in self.back:
            c.wait_recv()
        self.own.wait()

    def finish(self):
        self.ready()
        self.close()

    def close(self):
        for c in self.out + self.back:
            c.wait_send()


class PlaneSpread:
    COUNT = 10

    def __init__(self, place, copy, first, own, gathered):
        half = place.planes // 2
        parts = (pl.ds(0, half), pl.ds(half, half))
        mine, rx, rxy, ry = place.near
        px, py, pc = place.px, place.py, place.pc

        def same(i, ref, peer):
            return copy(first + i, ref, ref, peer)

        def send(i, part, peer):
            return copy(first + i, own.at[part], gathered.at[mine, part], peer)

        self.first = [
            send(0, parts[0], px),
            send(1, parts[1], py),
            send(2, parts[1], px),
            send(3, parts[0], py),
            copy(first + 4, own, gathered.at[mine], pc),
        ]
        self.next = [
            same(5, gathered.at[rx, parts[0]], py),
            same(6, gathered.at[ry, parts[1]], px),
            same(7, gathered.at[rx], pc),
            same(8, gathered.at[ry], pc),
            same(9, gathered.at[rxy], pc),
        ]

    def plane(self):
        for c in self.first:
            c.start()

    def forward(self):
        for i in range(4):
            self.first[i].wait_recv()
            self.next[i].start()

    def corner(self):
        self.next[0].wait_recv()
        self.next[1].wait_recv()
        self.next[4].start()

    def finish(self):
        self.first[4].wait_recv()
        for c in self.next[2:]:
            c.wait_recv()
        for c in self.first + self.next:
            c.wait_send()


class TableSpread:
    COUNT = TableSum.COUNT + PlaneSpread.COUNT

    def __init__(self, place, copy, first, source, arrived, piece, gathered, local):
        own = gathered.at[place.rank]
        self.sum = TableSum(
            place, copy, first, source, arrived, piece, lambda z: gathered.at[place.rank, z], local
        )
        self.spread = PlaneSpread(place, copy, first + TableSum.COUNT, own, gathered)
        self.scatter, self.gather = self.sum.scatter, self.sum.gather
        self.forward, self.corner = self.spread.forward, self.spread.corner

    def plane(self):
        self.sum.ready()
        self.spread.plane()

    def finish(self):
        self.sum.close()
        self.spread.finish()


class TableReduce:
    COUNT = 10

    def __init__(self, place, copy, first, table, part, from_core, from_x, from_y, diag, total, local):
        self.part, self.from_core, self.from_x, self.from_y = part, from_core, from_x, from_y
        self.diag, self.total = diag, total
        m = total.shape[0]
        self.m, self.h = m, m // 2
        h0, h1 = pl.ds(0, self.h), pl.ds(self.h, self.h)
        self.h0, self.h1 = h0, h1
        self.core = [
            copy(first + i, table.at[place.far[i]], from_core.at[i], place.pc) for i in range(4)
        ]
        self.load = [
            pltpu.make_async_copy(table.at[place.near[i]], part.at[i], local(i)) for i in range(4)
        ]
        self.d = [
            copy(first + 4, part.at[2, h0], diag.at[h0], place.px),
            copy(first + 5, part.at[2, h1], diag.at[h1], place.py),
        ]
        self.e = [
            copy(first + 6, part.at[1, h0], from_x.at[h0], place.px),
            copy(first + 7, part.at[3, h1], from_y.at[h1], place.py),
            copy(first + 8, part.at[1, h1], from_x.at[h1], place.px),
            copy(first + 9, part.at[3, h0], from_y.at[h0], place.py),
        ]

    def begin(self):
        for c in self.core + self.load:
            c.start()

    def merge(self):
        for i in (2, 1, 3, 0):
            self.load[i].wait()
            self.core[i].wait_recv()
            add_into(self.part.at[i], self.from_core.at[i], self.m, 16)
            if i == 2:
                self.d[0].start()
                self.d[1].start()
        self.e[0].start()
        self.e[1].start()

    def corner(self):
        self.d[0].wait_recv()
        add_into(self.part.at[3, self.h0], self.diag.at[self.h0], self.h, 16)
        self.e[3].start()
        self.d[1].wait_recv()
        add_into(self.part.at[1, self.h1], self.diag.at[self.h1], self.h, 16)
        self.e[2].start()

    def finish(self):
        for e in self.e:
            e.wait_recv()

        @pl.loop(0, self.m // 16)
        def _(i):
            at = span(i, 16)
            self.total[at, :] = (
                self.part[0, at, :].astype(f32)
                + self.from_x[at, :].astype(f32)
                + self.from_y[at, :].astype(f32)
            ).astype(bf16)

        for c in self.core + self.d + self.e:
            c.wait_send()


def attention_backward_kernel(
    middle, attn_out, cotangent, gains, masks, mixed, narrow_mix, mix_in, mix_out,
    queries, kvp, kvc, attended, sums, narrow, cosine, sine,
    grad_feed_hbm, tokens_hbm, heads_hbm, query_out_hbm, kv_out_hbm, out_hbm, normed_hbm, wall_hbm, feed_hbm, feed_share,
    tokens_grad, g_feed_table, g_feed_share, g_head_table, g_head_share,
    heads_in, query_out, key_out, value_out, wo, wall, grad_attn, grad_mixed,
    g, delta, inv, dq, kv_own, kv_far, kv_send, kv_got, grad_pre, back,
    from_core, from_y,
    feed_table, a_part, a_core, a_x, a_y, a_diag, a_total, a_in, a_piece,
    h_table, h_part, h_core, h_x, h_y, h_diag, h_total, h_in, h_piece,
    o_table, o_got, o_total, o_in, o_piece,
    send, recv, local,
):
    rows, width = tokens_grad.shape
    place = Places()
    b, z, planes = place.b, place.z, place.planes
    copy = sender(send, recv)
    normed_all = wo.at[pl.ds(0, 4 * rows)]
    part = [wo.at[pl.ds((4 + i) * rows, rows)] for i in range(4)]
    own_share = pltpu.make_async_copy(feed_share, g_feed_share.at[place.rank], local.at[0])
    loads = [
        pltpu.make_async_copy(src, dst, local.at[14 + i])
        for i, (src, dst) in enumerate(
            [(out_hbm, wo)]
            + head_table_copies(
                b, heads_hbm, query_out_hbm, kv_out_hbm, heads_in, query_out, key_out, value_out
            )
            + [(wall_hbm, wall), (feed_hbm, feed_table.at[:, pl.ds(0, 3 * RANK)])]
        )
    ]
    grad_feed = from_y
    bring_feed = pltpu.make_async_copy(grad_feed_hbm, grad_feed, local.at[24])
    bring_feed.start()
    late = pltpu.make_async_copy(normed_hbm, normed_all, local.at[1])
    for c in loads:
        c.start()
    own_share.start()
    barrier = pltpu.get_barrier_semaphore()
    peers = list(place.plane) + [place.up(d) for d in range(1, planes)]
    for peer in peers:
        pl.semaphore_signal(barrier, inc=1, device_id=peer, device_id_type=MESH)
    pl.semaphore_wait(barrier, len(peers))

    swaps = []
    for j, (peer, pb) in enumerate(
        ((place.py, place.b_y), (place.pyc, place.b_yc), (place.pc, place.b_c))
    ):
        for h in range(2):
            lanes = pl.ds(pl.multiple_of(pb * 2 * HEAD + h * HEAD, 128), HEAD)
            swaps.append(
                copy(
                    2 * j + h,
                    grad_mixed.at[:, lanes],
                    g.at[b, pl.ds(h * rows, rows)],
                    peer,
                )
            )
    at = 12
    feed_reduce = TableReduce(
        place, copy, at, feed_table, a_part, a_core, a_x, a_y, a_diag, a_total,
        lambda i: local.at[2 + i],
    )
    at += TableReduce.COUNT
    feed_spread = TableSpread(place, copy, at, a_total, a_in, a_piece, g_feed_table, local.at[6])
    at += TableSpread.COUNT
    share_spread = PlaneSpread(place, copy, at, feed_share, g_feed_share)
    at += PlaneSpread.COUNT
    head_reduce = TableReduce(
        place, copy, at, h_table, h_part, h_core, h_x, h_y, h_diag, h_total,
        lambda i: local.at[8 + i],
    )
    at += TableReduce.COUNT
    head_spread = TableSpread(place, copy, at, h_total, h_in, h_piece, g_head_table, local.at[12])
    at += TableSpread.COUNT
    out_spread = TableSpread(place, copy, at, o_total, o_in, o_piece, g_head_share, local.at[13])
    at += TableSpread.COUNT
    lanes_half = o_total.shape[0]
    out_swap = copy(
        at, o_table.at[span(1 - place.x, lanes_half)], o_got, place.px
    )

    share_spread.plane()

    bring_feed.wait()

    @pl.loop(0, rows // 32)
    def _(i):
        at = span(i, 32)
        grad = cotangent[at, :].astype(f32) + norm_grad(
            middle[at, :].astype(f32), gains[2:3, :], grad_feed[at, :].astype(f32)
        )
        tokens_grad[at, :] = grad
        grad_attn[at, :] = norm_grad(attn_out[at, :].astype(f32), gains[1:2, :], grad).astype(bf16)

    back_mix = (dot_nt(grad_attn[...], mix_out[...]) * masks[0, pl.ds(b, 1), :]).astype(bf16)
    loads[0].wait()
    for j, pb in enumerate((place.b_y, place.b_yc, place.b_c, b)):

        @pl.loop(0, 2)
        def _(h):
            at = span(pb * 2 + h, HEAD)
            grad_mixed[:, at] = (
                dot_nt(grad_attn[...], wo[at, :]) + dot_nn(back_mix, mix_in[:, at])
            ).astype(bf16)

        if j < 3:
            for c in swaps[2 * j : 2 * j + 2]:
                c.start()
    late.start()
    for c in loads[1:]:
        c.wait()
    for n in range(8):
        lanes = slice(n * HEAD, (n + 1) * HEAD)
        got = dot_tn(back_mix, mixed[:, lanes]).astype(bf16)
        for a in range(ADAPTERS):
            h_table[a, 3 * RANK :, lanes] = got[a * RANK : (a + 1) * RANK]
    h_table[:, 3 * RANK :, 8 * HEAD :] = jnp.zeros((ADAPTERS, RANK, width - 8 * HEAD), bf16)

    @pl.loop(0, width // 256)
    def _(n):
        at = span(n, 256)
        got = dot_tn(narrow_mix[...], grad_attn[:, at]).astype(bf16)
        for a in range(ADAPTERS):
            feed_table[a, 3 * RANK :, at] = got[a * RANK : (a + 1) * RANK]

    tokens = grad_attn
    bring_tokens = pltpu.make_async_copy(tokens_hbm, tokens, local.at[23])
    bring_tokens.start()
    feed_reduce.begin()
    for h in range(2):
        lanes = pl.ds(pl.multiple_of(b * 2 * HEAD + h * HEAD, 128), HEAD)
        g[b, h * rows : (h + 1) * rows, :] = grad_mixed[:, lanes]
    share_spread.forward()
    for c in swaps:
        c.wait()

    ones = jnp.ones((8, HEAD), f32)

    @pl.loop(0, 4)
    def _(t):
        for h in range(2):
            at_h = slice(h * rows, (h + 1) * rows)
            lanes = slice(h * HEAD, (h + 1) * HEAD)
            product = g[t, at_h, :].astype(f32) * attended[t, :, lanes].astype(f32)
            delta[t, :, at_h] = lax.dot_general(
                ones, product, (((1,), (1,)), ((), ())), precision=lax.Precision.HIGHEST,
                preferred_element_type=f32,
            )
        inv[t] = 1.0 / sums[t]

    query = lax.broadcasted_iota(jnp.int32, (rows, 2 * rows), 1) % rows
    causal = lax.broadcasted_iota(jnp.int32, (rows, 2 * rows), 0) <= query

    def step(t, k, v, total, slot, masked):
        q, gt = queries[t], g[t]
        th = jnp.tanh(dot_nt(k, q) * (1.0 / soft_cap))
        p = jnp.exp(soft_cap * th) * inv[t, 0:1, :]
        if masked:
            p = jnp.where(causal, p, 0.0)
        total[1, slot] += dot_nn(p.astype(bf16), gt)
        ds = (p * (dot_nt(v, gt) - delta[t, 0:1, :]) * (1.0 - th * th)).astype(bf16)
        total[0, slot] += dot_nn(ds, q)
        dq[t] += dot_tn(ds, k)

    dq[...] = jnp.zeros_like(dq)
    kv_own[...] = jnp.zeros_like(kv_own)

    def kv_copy(d):
        return copy(6 + d - 1, kv_send.at[d - 1], kv_got.at[d - 1], place.up(d))

    @pl.loop(1, planes)
    def _(d):
        zz = (z + d) % planes
        kv_far[...] = jnp.zeros_like(kv_far)
        step(1, kvp[zz, 0, 0], kvp[zz, 1, 0], kv_far, 0, False)

        @pl.when(zz < z)
        def _():
            step(0, kvp[zz, 0, 0], kvp[zz, 1, 0], kv_far, 0, False)
            step(1, kvp[zz, 0, 1], kvp[zz, 1, 1], kv_far, 1, False)

        @pl.loop(2, 4)
        def _(t):
            step(t, kvp[zz, 0, 0], kvp[zz, 1, 0], kv_far, 0, False)
            step(t, kvp[zz, 0, 1], kvp[zz, 1, 1], kv_far, 1, False)

        kv_send[d - 1] = kv_far[...].astype(bf16)
        for k in range(1, planes):

            @pl.when(d == k)
            def _(k=k):
                kv_copy(k).start()
                if k == 1:
                    feed_reduce.merge()
                    share_spread.corner()
                if k == 2:
                    feed_reduce.corner()

    feed_reduce.finish()
    feed_spread.scatter()
    step(0, kvp[z, 0, 0], kvp[z, 1, 0], kv_own, 0, True)
    step(1, kvp[z, 0, 0], kvp[z, 1, 0], kv_own, 0, False)
    step(1, kvp[z, 0, 1], kvp[z, 1, 1], kv_own, 1, True)

    @pl.loop(2, 4)
    def _(t):
        step(t, kvc[0, t - 2], kvc[1, t - 2], kv_own, t, True)
        step(t, kvp[z, 0, 0], kvp[z, 1, 0], kv_own, 0, False)
        step(t, kvp[z, 0, 1], kvp[z, 1, 1], kv_own, 1, False)

    late.wait()
    feed_spread.gather()
    for d in range(1, planes):
        kv_copy(d).wait_recv()
        kv_own[:, 0:2] += kv_got[d - 1].astype(f32)
    half_head = HEAD // 2

    @pl.loop(0, 4)
    def _(t):
        at = span(t, rows)
        cos, sin = cosine[at, :], sine[at, :]
        mask = masks[0, pl.ds(t, 1), :]

        def turned(pre, scale):
            first, second = pre[:, :half_head], pre[:, half_head:]
            one, two = first * cos + second * sin, second * cos - first * sin
            if scale != 1.0:
                one, two = one * scale, two * scale
            return jnp.concatenate([one, two], axis=1).astype(bf16)

        for h in range(2):
            grad_pre[at, h * HEAD : (h + 1) * HEAD] = turned(
                dq[t, h * rows : (h + 1) * rows, :], HEAD ** (-0.5)
            )
        grad_pre[at, 2 * HEAD : 3 * HEAD] = turned(kv_own[0, t], 1.0)
        grad_pre[at, 3 * HEAD :] = kv_own[1, t].astype(bf16)
        for i, (lanes, table) in enumerate(
            (
                (slice(0, 2 * HEAD), query_out),
                (slice(2 * HEAD, 3 * HEAD), key_out),
                (slice(3 * HEAD, 4 * HEAD), value_out),
            )
        ):
            back[at, i * LANES : (i + 1) * LANES] = (
                dot_nt(grad_pre[at, lanes], flat(table[...])) * mask
            ).astype(bf16)

    for i, lanes in enumerate(
        (slice(0, 2 * HEAD), slice(2 * HEAD, 3 * HEAD), slice(3 * HEAD, 4 * HEAD))
    ):
        o_table[:, lanes] = dot_tn(
            narrow[:, i * LANES : (i + 1) * LANES], grad_pre[:, lanes]
        ).astype(bf16)
    out_swap.start()

    @pl.loop(0, width // 256)
    def _(n):
        at = span(n, 256)
        got = dot_tn(back[...], normed_all[:, at]).astype(bf16)
        for i in range(3):
            for a in range(ADAPTERS):
                first = i * LANES + a * RANK
                h_table[a, i * RANK : (i + 1) * RANK, at] = got[first : first + RANK]

    head_reduce.begin()
    feed_spread.plane()

    def project(slot, target):
        at_rows = span(target, rows)

        @pl.loop(0, width // 256)
        def _(n):
            at = span(n, 256)
            part[slot][:, at] = (
                dot_nt(grad_pre[at_rows, :], wall[at, :])
                + dot_nn(back[at_rows, :], heads_in[:, :, :, at].reshape(3 * LANES, 256))
            ).astype(bf16)

    to_core = [copy(9 + i, part[i], from_core.at[i], place.pc) for i in range(2)]
    to_y = copy(11, part[2], from_y, place.py)
    project(0, place.b_yc)
    to_core[0].start()
    project(2, place.b_y)
    to_core[0].wait_recv()
    add_into(part[2], from_core.at[0], rows)
    to_y.start()
    head_reduce.merge()
    feed_spread.forward()
    out_swap.wait_recv()

    @pl.loop(0, lanes_half // 16)
    def _(i):
        at = span(i, 16)
        mine = pl.ds(pl.multiple_of(place.x * lanes_half + i * 16, 16), 16)
        o_total[at, :] = (o_table[mine, :].astype(f32) + o_got[at, :].astype(f32)).astype(bf16)

    out_spread.scatter()
    project(1, place.b_c)
    to_core[1].start()
    head_reduce.corner()
    feed_spread.corner()
    out_spread.gather()
    project(3, b)
    head_reduce.finish()
    head_spread.scatter()
    out_spread.plane()
    head_spread.gather()
    to_core[1].wait_recv()
    out_spread.forward()
    head_spread.plane()
    out_spread.corner()
    head_spread.forward()
    to_y.wait_recv()
    bring_tokens.wait()

    @pl.loop(0, rows // 32)
    def _(i):
        at = span(i, 32)
        grad = (
            part[3][at, :].astype(f32)
            + from_core[1, at, :].astype(f32)
            + from_y[at, :].astype(f32)
        )
        tokens_grad[at, :] += norm_grad(tokens[at, :].astype(f32), gains[0:1, :], grad)

    head_spread.corner()
    for spread in (share_spread, feed_spread, out_spread, head_spread):
        spread.finish()
    own_share.wait()
    out_swap.wait_send()
    to_y.wait_send()
    for c in to_core:
        c.wait_send()
    for d in range(1, planes):
        kv_copy(d).wait_send()


def attention_backward(rows_in, kept, grad_feed, tokens, tables, weights, feed_table, feed_share):
    rows, width = rows_in[0].shape
    planes = lax.axis_size("ulysses")
    m = 4 * RANK
    hm = 4 * RANK
    ow = 4 * HEAD
    om = LANES // 2
    count = 12 + 2 * TableReduce.COUNT + 3 * TableSpread.COUNT + PlaneSpread.COUNT + 1

    def reduce_scratch(m):
        return [
            pltpu.VMEM((ADAPTERS, m, width), bf16),
            pltpu.VMEM((4, m, width), bf16),
            pltpu.VMEM((4, m, width), bf16),
            pltpu.VMEM((m, width), bf16),
            pltpu.VMEM((m, width), bf16),
            pltpu.VMEM((m, width), bf16),
            pltpu.VMEM((m, width), bf16),
        ]

    def spread_scratch(m, w):
        return [
            pltpu.VMEM((planes - 1, m // planes, w), bf16),
            pltpu.VMEM((m // planes, w), bf16),
        ]

    return pl.pallas_call(
        attention_backward_kernel,
        out_shape=(
            shape((rows, width), f32),
            shape((8, planes, m // planes, width), bf16),
            shape((8,) + feed_share.shape, bf16),
            shape((8, planes, hm // planes, width), bf16),
            shape((8, planes, om // planes, ow), bf16),
        ),
        in_specs=[VM] * 17 + [ANY] * 10,
        out_specs=(VM, ANY, ANY, ANY, ANY),
        scratch_shapes=head_table_scratch(width)
        + [
            pltpu.VMEM((8 * HEAD, width), bf16),
            pltpu.VMEM((width, 4 * HEAD), bf16),
            pltpu.VMEM((rows, width), bf16),
            pltpu.VMEM((rows, 8 * HEAD), bf16),
            pltpu.VMEM((4, 2 * rows, HEAD), bf16),
            pltpu.VMEM((4, 8, 2 * rows), f32),
            pltpu.VMEM((4, 8, 2 * rows), f32),
            pltpu.VMEM((4, 2 * rows, HEAD), f32),
            pltpu.VMEM((2, 4, rows, HEAD), f32),
            pltpu.VMEM((2, 2, rows, HEAD), f32),
            pltpu.VMEM((planes - 1, 2, 2, rows, HEAD), bf16),
            pltpu.VMEM((planes - 1, 2, 2, rows, HEAD), bf16),
            pltpu.VMEM((4 * rows, 4 * HEAD), bf16),
            pltpu.VMEM((4 * rows, 3 * LANES), bf16),
            pltpu.VMEM((2, rows, width), bf16),
            pltpu.VMEM((rows, width), bf16),
        ]
        + reduce_scratch(m)
        + spread_scratch(m, width)
        + reduce_scratch(hm)
        + spread_scratch(hm, width)
        + [
            pltpu.VMEM((LANES, ow), bf16),
            pltpu.VMEM((om, ow), bf16),
            pltpu.VMEM((om, ow), bf16),
        ]
        + spread_scratch(om, ow)
        + [
            pltpu.SemaphoreType.DMA((count,)),
            pltpu.SemaphoreType.DMA((count,)),
            pltpu.SemaphoreType.DMA((25,)),
        ],
        compiler_params=pltpu.CompilerParams(
            collective_id=4, has_side_effects=True, vmem_limit_bytes=63 << 20
        ),
        name="attention_backward",
    )(*rows_in, *kept, grad_feed, tokens, *tables, *weights, feed_table, feed_share)


def shards(
    tokens,
    query_weight,
    key_projection,
    value_projection,
    out_weight,
    gate_weight,
    up_weight,
    down_weight,
    attn_in_gain,
    attn_out_gain,
    feed_in_gain,
    feed_out_gain,
    adapt_heads_in,
    adapt_query_out,
    adapter_key_value_second,
    adapt_mix_in,
    adapt_mix_out,
    adapt_feed_in,
    adapt_feed_out,
    adapt_down_in,
    adapt_down_out,
    adapter_ids,
    cotangent,
):
    width = tokens.shape[1]
    blk_n = lax.axis_size("blk")
    dp_n = lax.axis_size("dp")
    rank = lax.axis_index("dp") % 2 * blk_n + lax.axis_index("blk")
    ff = gate_weight.shape[1]
    share = ff // (2 * blk_n)
    weights = (
        query_weight, key_projection, value_projection, out_weight, gate_weight, up_weight,
        down_weight,
    )
    if dp_n > 2:
        weights = tuple(
            lax.dynamic_slice_in_dim(
                lax.all_gather(weight, PLANE, axis=0, tiled=True),
                rank * (weight.shape[0] * dp_n // 2),
                weight.shape[0] * dp_n // 2,
            )
            for weight in weights
        )
    down_rows = weights[6]
    gains = jnp.stack([attn_in_gain, attn_out_gain, feed_in_gain, feed_out_gain])
    mix_in, mix_out, down_out = flat(adapt_mix_in), flat(adapt_mix_out), flat(adapt_down_out)
    head_tables = (adapt_heads_in, adapt_query_out, adapter_key_value_second)
    feed_tables = (adapt_feed_in, adapt_feed_out, adapt_down_in)
    (
        queries, kvp, kvc, attended, exp_sum, narrow_heads, mixed, narrow_mix, attn_out, middle,
        normed_feed, cosine, sine, masks, normed_all, head_weight, out_full, gate_share, up_share,
    ) = attention_forward(
        tokens, gains, adapter_ids, mix_in, mix_out, head_tables, weights[:6], share
    )
    layer_out, grad_branch, narrow_feed, feed_all, gate_up = feed_forward(
        normed_feed, middle, cotangent, gains, masks, down_out, feed_tables, gate_share, up_share,
        down_rows,
    )
    grad_feed, feed_table, share_sum = feed_backward(
        grad_branch, masks, down_out, narrow_feed, feed_tables, gate_share, up_share, down_rows,
        gate_up, feed_all,
    )
    tokens_grad, feed_rows, feed_columns, head_rows, head_columns = attention_backward(
        (
            middle, attn_out, cotangent, gains, masks, mixed, narrow_mix, mix_in, mix_out,
        ),
        (queries, kvp, kvc, attended, exp_sum, narrow_heads, cosine, sine),
        grad_feed,
        tokens,
        head_tables,
        (out_full, normed_all, head_weight),
        feed_table,
        share_sum,
    )

    feed_rows = feed_rows.reshape(ADAPTERS, 4, RANK, width)
    feed_columns = (
        feed_columns.reshape(8, 3, ADAPTERS, RANK, share)
        .transpose(2, 1, 3, 0, 4)
        .reshape(ADAPTERS, 3, RANK, ff)
    )
    head_rows = head_rows.reshape(ADAPTERS, 4, RANK, width)
    head_columns = (
        head_columns.reshape(2, 4, LANES // 2, 4 * HEAD)
        .transpose(0, 2, 1, 3)
        .reshape(ADAPTERS, RANK, 4, 4 * HEAD)
    )

    def joined(first, last):
        return head_columns[..., first:last].reshape(ADAPTERS, RANK, -1)

    summed = (
        head_rows[:, :3],
        joined(0, 2 * HEAD),
        jnp.stack([joined(2 * HEAD, 3 * HEAD), joined(3 * HEAD, 4 * HEAD)], axis=1),
        head_rows[:, 3, :, : mixed.shape[1]],
        feed_rows[:, 3],
        feed_rows[:, :2],
        feed_columns[:, :2],
        feed_columns[:, 2],
        feed_rows[:, 2],
    )
    summed = tuple(table.astype(f32) for table in summed)
    if dp_n > 2:
        summed = tuple(lax.psum(table * 0.5, "dp") for table in summed)
    return (layer_out, tokens_grad) + summed


def solution(mesh):
    sharded = P(EVERY, None)
    rowwise = P(PLANE, None)
    placed = (
        (sharded,) + (rowwise,) * 7 + (P(),) * 13 + (P("dp", None), sharded)
    )
    return jax.shard_map(
        shards,
        mesh=mesh,
        in_specs=placed,
        out_specs=(sharded, sharded) + (P(),) * 9,
        check_vma=False,
    )
```

```python
import math

import jax
import jax.numpy as jnp
from jax import lax
from jax.experimental import pallas as pl
from jax.experimental.pallas import tpu as pltpu
from jax.sharding import PartitionSpec as P

HEADS = 8
KV_HEADS = 4
HEAD = 256
RANK = 16
ADAPTERS = 8
LANES = RANK * ADAPTERS
PROMPT = 2048
CONT = 256
CONTS = 8

epsilon = 1e-06
soft_cap = 50.0
rope_base = 10000.0
PLANE = ("dp", "blk")
EVERY = ("dp", "blk", "ulysses")
f32 = jnp.float32
bf16 = jnp.bfloat16


def dot_nn(a, b):
    return jnp.dot(a, b, preferred_element_type=f32)


def dot_nt(a, b):
    return lax.dot_general(a, b, (((1,), (1,)), ((), ())), preferred_element_type=f32)


def dot_tn(a, b):
    return lax.dot_general(a, b, (((0,), (0,)), ((), ())), preferred_element_type=f32)


def norm_grad(values, gain_row, grad_out):
    scale = lax.rsqrt(jnp.mean(values * values, axis=-1, keepdims=True) + epsilon)
    weighted = grad_out * gain_row
    return scale * weighted - values * (
        scale * scale * scale * jnp.mean(values * weighted, axis=-1, keepdims=True)
    )


def shape(dims, dtype):
    return jax.ShapeDtypeStruct(dims, dtype)


VM = pl.BlockSpec(memory_space=pltpu.VMEM)


MESH = pl.DeviceIdType.MESH


def neighbours():
    dp, b, z = lax.axis_index("dp"), lax.axis_index("blk"), lax.axis_index("ulysses")
    across_x = (dp + 1 - 2 * (dp % 2), b, z)
    across_y = (dp, (b + 2) % 4, z)
    sibling = (dp, b + 1 - 2 * (b % 2), z)
    return across_x, across_y, sibling


def greet(peers):
    barrier = pltpu.get_barrier_semaphore()
    for peer in peers:
        pl.semaphore_signal(barrier, inc=1, device_id=peer, device_id_type=MESH)
    pl.semaphore_wait(barrier, len(peers))


def sender(send, recv):
    def copy(index, src, dst, peer):
        return pltpu.make_async_remote_copy(
            src, dst, send.at[index], recv.at[index], device_id=peer, device_id_type=MESH
        )

    return copy


def add_into(target, source, count, step=32):
    @pl.loop(0, count // step)
    def _(i):
        at = pl.ds(pl.multiple_of(i * step, step), step)
        target[at, :] = (target[at, :].astype(f32) + source[at, :].astype(f32)).astype(target.dtype)


class PlaneGather:
    COUNT = 10

    def __init__(self, copy, own, land, rows):
        px, py, pc = neighbours()
        h = rows // 2
        h0, h1 = pl.ds(0, h), pl.ds(h, h)
        near, far = pl.ds(0, rows), pl.ds(rows, rows)
        self.c = [
            copy(0, own, land.at[0, far], pc),
            copy(1, own.at[h0], land.at[1, h0], px),
            copy(2, own.at[h1], land.at[1, h1], py),
            copy(3, own.at[h1], land.at[3, h0], px),
            copy(4, own.at[h0], land.at[3, h1], py),
            copy(5, land.at[1, h0], land.at[2, h0], py),
            copy(6, land.at[1, h1], land.at[2, h1], px),
            copy(7, land.at[1, near], land.at[1, far], pc),
            copy(8, land.at[3, near], land.at[3, far], pc),
            copy(9, land.at[2, near], land.at[2, far], pc),
        ]

    def begin(self):
        for i in range(3):
            self.c[i].start()

    def before(self, i):
        c = self.c

        @pl.when(i == 0)
        def _():
            c[0].wait_recv()

        @pl.when(i == 1)
        def _():
            c[1].wait_recv()
            c[5].start()
            c[2].wait_recv()
            c[6].start()
            c[7].start()
            for k in (3, 4):
                c[k].start()
            c[7].wait_recv()

        @pl.when(i == 2)
        def _():
            c[5].wait_recv()
            c[6].wait_recv()
            c[9].start()
            c[9].wait_recv()

        @pl.when(i == 3)
        def _():
            c[3].wait_recv()
            c[4].wait_recv()
            c[8].start()
            c[8].wait_recv()

    def finish(self):
        for c in self.c:
            c.wait_send()


def plane_masks(masks, i, rows):
    b = lax.axis_index("blk")
    diagonal = i // 2 * (1 - i % 2)
    away = (i + 2) // 3
    out = jnp.zeros((2 * rows, LANES), f32)
    place = lax.broadcasted_iota(jnp.int32, (2 * rows, LANES), 0) // (rows // 2)
    for half, (group, shift) in enumerate(((away, diagonal), (diagonal, away))):
        near = (b + 2 * shift) % 4
        far = near + 1 - 2 * (near % 2)
        out = jnp.where(place == half, masks[group, pl.ds(near, 1), :], out)
        out = jnp.where(place == 2 + half, masks[group, pl.ds(far, 1), :], out)
    return out


def feed_table_copies(rank, share, feed_in_hbm, feed_out_hbm, down_in_hbm, feed_in, feed_out, down_in):
    lanes = pl.ds(pl.multiple_of(rank * share, 128), share)
    return [
        (feed_in_hbm.at[:, 0], feed_in.at[0]),
        (feed_in_hbm.at[:, 1], feed_in.at[1]),
        (feed_out_hbm.at[:, 0, :, lanes], feed_out.at[0]),
        (feed_out_hbm.at[:, 1, :, lanes], feed_out.at[1]),
        (down_in_hbm.at[:, :, lanes], down_in),
    ]


def feed_table_scratch(width, share):
    return [
        pltpu.VMEM((2, ADAPTERS, RANK, width), bf16),
        pltpu.VMEM((2, ADAPTERS, RANK, share), bf16),
        pltpu.VMEM((ADAPTERS, RANK, share), bf16),
    ]


class PlaneReduce:
    COUNT = 10

    def __init__(self, copy, part, odd, from_core, from_x, from_y, diag, rows, first):
        px, py, pc = neighbours()
        h = rows // 2
        self.h = h
        self.rows = rows
        h0, h1 = pl.ds(0, h), pl.ds(h, h)
        self.part, self.from_core = part, from_core
        self.from_x, self.from_y, self.diag = from_x, from_y, diag
        self.core = [
            copy(first + i, odd.at[i % 2], from_core.at[i], pc) for i in range(4)
        ]
        self.d = [
            copy(first + 4, part.at[2, h0], diag.at[h0], px),
            copy(first + 5, part.at[2, h1], diag.at[h1], py),
        ]
        self.e = [
            copy(first + 6, part.at[1, h0], from_x.at[h0], px),
            copy(first + 7, part.at[1, h1], from_y.at[h1], py),
            copy(first + 8, part.at[3, h0], from_x.at[h1], px),
            copy(first + 9, part.at[3, h1], from_y.at[h0], py),
        ]

    def merge(self, i):
        self.core[i].wait_recv()
        add_into(self.part.at[i], self.from_core.at[i], self.rows)

    def before(self, i):
        for k in (2, 3):

            @pl.when(i == k)
            def _(k=k):
                self.core[k - 2].wait_send()

    def after(self, i):
        for k in range(4):

            @pl.when(i == k)
            def _(k=k):
                self.core[k].start()
                if k == 2:
                    self.merge(1)
                    self.e[0].start()
                    self.e[1].start()
                    self.merge(2)
                    self.d[0].start()
                    self.d[1].start()

    def finish(self, write, between=None):
        h, h0, h1 = self.h, pl.ds(0, self.h), pl.ds(self.h, self.h)
        self.merge(3)
        self.d[0].wait_recv()
        add_into(self.part.at[3, h1], self.diag.at[h0], h)
        self.e[3].start()
        self.d[1].wait_recv()
        add_into(self.part.at[3, h0], self.diag.at[h1], h)
        self.e[2].start()
        if between is not None:
            between()
        self.merge(0)
        for e in self.e:
            e.wait_recv()

        @pl.loop(0, self.rows // 32)
        def _(i):
            at = pl.ds(pl.multiple_of(i * 32, 32), 32)
            write(
                at,
                self.part[0, at, :].astype(f32)
                + self.from_x[at, :].astype(f32)
                + self.from_y[at, :].astype(f32),
            )

        for c in self.core[2:] + self.d + self.e:
            c.wait_send()


GELU_SLOPE = 0.7978845608028654
GELU_CUBE = 0.044715


def plane_rank():
    return lax.axis_index("dp") % 2 * 4 + lax.axis_index("blk")


def span(i, size):
    return pl.ds(pl.multiple_of(i * size, size), size)


def woven(gate_hbm, up_hbm, both):
    out = []
    for j in range(gate_hbm.shape[1] // 128):
        for k, ref in enumerate((gate_hbm, up_hbm)):
            out.append(
                (ref.at[:, pl.ds(j * 128, 128)], both.at[:, pl.ds(j * 256 + k * 128, 128)])
            )
    return out


def feed_forward_kernel(
    own, middle, cotangent, gains, masks, down_out, feed_in_hbm, feed_out_hbm, down_in_hbm,
    gate_hbm, up_hbm, down_hbm,
    layer_out, grad_branch, narrow, feed_all, gate_up,
    feed_in, feed_out, down_in, weave, down, land, hidden, saved, part, odd, from_core, from_x, from_y, diag,
    send, recv, load, store,
):
    rows = own.shape[0]
    share = gate_hbm.shape[1]
    width = own.shape[1]
    tile = 256
    loads = [
        pltpu.make_async_copy(s, d, load.at[i])
        for i, (s, d) in enumerate(
            woven(gate_hbm, up_hbm, weave)
            + [(down_hbm, down)]
            + feed_table_copies(
                plane_rank(), share, feed_in_hbm, feed_out_hbm, down_in_hbm, feed_in, feed_out,
                down_in,
            )
        )
    ]
    for c in loads:
        c.start()
    greet(neighbours())
    copy = sender(send, recv)
    gather = PlaneGather(copy, own, land, rows)
    reduce = PlaneReduce(
        copy, part, odd, from_core, from_x, from_y, diag, rows, PlaneGather.COUNT
    )
    gather.begin()
    land[0, :rows, :] = own[...]
    for c in loads:
        c.wait()

    def keep(i):
        slot = i % 2
        return (
            pltpu.make_async_copy(saved.at[slot], gate_up.at[i], store.at[slot]),
            pltpu.make_async_copy(land.at[i], feed_all.at[i], store.at[2 + slot]),
        )

    @pl.loop(0, 4)
    def _(i):
        gather.before(i)
        slot = i % 2

        @pl.when(i >= 2)
        def _():
            for c in keep(i - 2):
                c.wait()

        mask = plane_masks(masks, i, rows)
        for k in range(2):
            narrow[i, k] = (dot_nt(land[i], flat(feed_in[k])) * mask).astype(bf16)

        @pl.loop(0, share // 128)
        def _(n):
            at = span(n, 128)
            pre = dot_nn(land[i], weave[:, span(n, 256)])
            g = pre[:, :128] + dot_nn(narrow[i, 0], flat(feed_out[0, :, :, at]))
            u = pre[:, 128:] + dot_nn(narrow[i, 1], flat(feed_out[1, :, :, at]))
            saved[slot, 0, :, at] = g.astype(bf16)
            saved[slot, 1, :, at] = u.astype(bf16)
            th = jnp.tanh(GELU_SLOPE * (g + GELU_CUBE * g * g * g))
            hidden[:, at] = (0.5 * g * (1.0 + th) * u).astype(bf16)

        for c in keep(i):
            c.start()
        narrow[i, 2] = (dot_nt(hidden[...], flat(down_in[...])) * mask).astype(bf16)
        reduce.before(i)

        @pl.loop(0, width // tile)
        def _(n):
            at = span(n, tile)
            got = dot_nn(hidden[...], down[:, at]) + dot_nn(narrow[i, 2], down_out[:, at])
            got = got.astype(bf16)
            part[i, :, at] = got[:rows]
            odd[i % 2, :, at] = got[rows:]

        reduce.after(i)

    def write(at, branch):
        scale = lax.rsqrt(jnp.mean(branch * branch, axis=-1, keepdims=True) + epsilon)
        gain = gains[3:4, :]
        layer_out[at, :] = (middle[at, :].astype(f32) + branch * scale * gain).astype(bf16)
        grad_branch[at, :] = norm_grad(branch, gain, cotangent[at, :].astype(f32)).astype(bf16)

    reduce.finish(write)
    gather.finish()
    for i in (2, 3):
        for c in keep(i):
            c.wait()


def feed_backward_kernel(
    own, masks, down_out, narrow, feed_in_hbm, feed_out_hbm, down_in_hbm,
    gate_hbm, up_hbm, down_hbm, gate_up, feed_all,
    grad_feed, feed_table, share_sum,
    back, both, t_feed_out, t_down_in, t_down_out, share_table, share_in, share_piece,
    feed_in, feed_out, down_in, weave, down, land, saved, gg, part, odd, from_core, from_x, from_y, diag,
    send, recv, load, fetch,
):
    rows = own.shape[0]
    share = gate_hbm.shape[1]
    width = own.shape[1]
    tile = 256
    loads = [
        pltpu.make_async_copy(s, d, load.at[i])
        for i, (s, d) in enumerate(
            woven(gate_hbm, up_hbm, weave)
            + [(down_hbm, down)]
            + feed_table_copies(
                plane_rank(), share, feed_in_hbm, feed_out_hbm, down_in_hbm, feed_in, feed_out,
                down_in,
            )
        )
    ]

    def bring(i):
        return pltpu.make_async_copy(gate_up.at[i], saved, fetch.at[0])

    for c in loads:
        c.start()
    bring(0).start()
    place = Places()
    greet(list(neighbours()) + [place.up(d) for d in range(1, place.planes)])
    copy = sender(send, recv)
    spread = TableSum(
        place, copy, PlaneGather.COUNT + PlaneReduce.COUNT, share_table, share_in, share_piece,
        lambda z: share_sum.at[z], fetch.at[1],
    )
    gather = PlaneGather(copy, own, land, rows)
    reduce = PlaneReduce(
        copy, part, odd, from_core, from_x, from_y, diag, rows, PlaneGather.COUNT
    )
    gather.begin()
    land[0, :rows, :] = own[...]
    t_feed_out[...] = jnp.zeros_like(t_feed_out)
    t_down_in[...] = jnp.zeros_like(t_down_in)
    t_down_out[...] = jnp.zeros_like(t_down_out)
    for c in loads:
        c.wait()

    @pl.loop(0, 4)
    def _(i):
        gather.before(i)
        bring(i).wait()
        mask = plane_masks(masks, i, rows)
        back[...] = (dot_nt(land[i], down_out[...]) * mask).astype(bf16)

        @pl.loop(0, 2)
        def _(n):
            at = span(n, rows)
            gh = dot_nt(land[i, at, :], down[...]) + dot_nn(back[at, :], flat(down_in[...]))
            g = saved[0, at, :].astype(f32)
            u = saved[1, at, :].astype(f32)
            th = jnp.tanh(GELU_SLOPE * (g + GELU_CUBE * g * g * g))
            gelu = 0.5 * g * (1.0 + th)
            slope = 0.5 * (1.0 + th) + 0.5 * g * (1.0 - th * th) * GELU_SLOPE * (
                1.0 + 3.0 * GELU_CUBE * g * g
            )
            saved[0, at, :] = (gelu * u).astype(bf16)
            left = (gh * u * slope).astype(bf16)
            right = (gh * gelu).astype(bf16)
            for j in range(share // 128):
                lanes = slice(j * 128, (j + 1) * 128)
                gg[at, j * 256 : j * 256 + 128] = left[:, lanes]
                gg[at, j * 256 + 128 : (j + 1) * 256] = right[:, lanes]

        t_down_in[...] += dot_tn(back[...], saved[0])

        @pl.when(i < 3)
        def _():
            bring(i + 1).start()

        for k in range(2):
            low = jnp.zeros((2 * rows, LANES), f32)
            for j in range(share // 128):
                at = j * 256 + k * 128
                low = low + dot_nt(
                    gg[:, at : at + 128], flat(feed_out[k, :, :, j * 128 : (j + 1) * 128])
                )
            both[i, :, k * LANES : (k + 1) * LANES] = (low * mask).astype(bf16)
        reduce.before(i)

        @pl.loop(0, width // tile)
        def _(n):
            at = span(n, tile)
            got = (
                dot_nt(gg[...], weave[at, :])
                + dot_nn(both[i, :, :LANES], flat(feed_in[0, :, :, at]))
                + dot_nn(both[i, :, LANES:], flat(feed_in[1, :, :, at]))
            ).astype(bf16)
            part[i, :, at] = got[:rows]
            odd[i % 2, :, at] = got[rows:]

        reduce.after(i)
        for k in range(2):
            for j in range(share // 128):
                at = j * 256 + k * 128
                t_feed_out[k, :, j * 128 : (j + 1) * 128] += dot_tn(
                    narrow[i, k], gg[:, at : at + 128]
                )
        t_down_out[...] += dot_tn(narrow[i, 2], land[i])

    share_table[: 2 * LANES] = t_feed_out[...].reshape(2 * LANES, share).astype(bf16)
    share_table[2 * LANES :] = t_down_in[...].astype(bf16)
    spread.scatter()
    gather.finish()
    reload = [pltpu.make_async_copy(feed_all.at[i], land.at[i], fetch.at[2 + i]) for i in range(4)]
    for c in reload:
        c.start()

    def tables():
        spread.gather()
        for c in reload:
            c.wait()
        backs = both[...].reshape(8 * rows, 2 * LANES)

        @pl.loop(0, width // 256)
        def _(n):
            at = span(n, 256)
            got = dot_tn(backs, land[:, :, at].reshape(8 * rows, 256)).astype(bf16)
            last = t_down_out[:, at].astype(bf16)
            for a in range(ADAPTERS):
                first = slice(a * RANK, (a + 1) * RANK)
                second = slice(LANES + a * RANK, LANES + (a + 1) * RANK)
                feed_table[a, :RANK, at] = got[first]
                feed_table[a, RANK : 2 * RANK, at] = got[second]
                feed_table[a, 2 * RANK :, at] = last[first]

    def write(at, total):
        grad_feed[at, :] = total.astype(grad_feed.dtype)

    reduce.finish(write, tables)
    spread.finish()


def feed_scratch(rows, width, extra=0):
    count = PlaneGather.COUNT + PlaneReduce.COUNT + extra
    return [
        pltpu.VMEM((4, rows, width), bf16),
        pltpu.VMEM((2, rows, width), bf16),
        pltpu.VMEM((4, rows, width), bf16),
        pltpu.VMEM((rows, width), bf16),
        pltpu.VMEM((rows, width), bf16),
        pltpu.VMEM((rows, width), bf16),
        pltpu.SemaphoreType.DMA((count,)),
        pltpu.SemaphoreType.DMA((count,)),
    ]


ANY = pl.BlockSpec(memory_space=pl.ANY)


def feed_forward(own, middle, cotangent, gains, masks, down_out, tables, gate, up, down):
    rows, width = own.shape
    share = gate.shape[1]
    return pl.pallas_call(
        feed_forward_kernel,
        out_shape=(
            shape((rows, width), bf16),
            shape((rows, width), bf16),
            shape((4, 3, 2 * rows, LANES), bf16),
            shape((4, 2 * rows, width), bf16),
            shape((4, 2, 2 * rows, share), bf16),
        ),
        in_specs=[VM] * 6 + [ANY] * 6,
        out_specs=(VM, VM, VM, ANY, ANY),
        scratch_shapes=feed_table_scratch(width, share)
        + [
            pltpu.VMEM((width, 2 * share), bf16),
            pltpu.VMEM(down.shape, bf16),
            pltpu.VMEM((4, 2 * rows, width), bf16),
            pltpu.VMEM((2 * rows, share), bf16),
            pltpu.VMEM((2, 2, 2 * rows, share), bf16),
        ]
        + feed_scratch(rows, width)
        + [pltpu.SemaphoreType.DMA((6 + share // 64,)), pltpu.SemaphoreType.DMA((4,))],
        compiler_params=pltpu.CompilerParams(
            collective_id=1, has_side_effects=True, vmem_limit_bytes=62 << 20
        ),
        name="feed_forward",
    )(own, middle, cotangent, gains, masks, down_out, *tables, gate, up, down)


def feed_backward(own, masks, down_out, narrow, tables, gate, up, down, gate_up, feed_all):
    rows, width = own.shape
    share = gate.shape[1]
    planes = lax.axis_size("ulysses")
    piece = 3 * LANES // planes
    return pl.pallas_call(
        feed_backward_kernel,
        out_shape=(
            shape((rows, width), bf16),
            shape((ADAPTERS, 3 * RANK, width), bf16),
            shape((planes, piece, share), bf16),
        ),
        in_specs=[VM] * 4 + [ANY] * 8,
        out_specs=(VM, VM, ANY),
        scratch_shapes=[
            pltpu.VMEM((2 * rows, LANES), bf16),
            pltpu.VMEM((4, 2 * rows, 2 * LANES), bf16),
            pltpu.VMEM((2, LANES, share), f32),
            pltpu.VMEM((LANES, share), f32),
            pltpu.VMEM((LANES, width), f32),
            pltpu.VMEM((3 * LANES, share), bf16),
            pltpu.VMEM((planes - 1, piece, share), bf16),
            pltpu.VMEM((piece, share), bf16),
        ]
        + feed_table_scratch(width, share)
        + [
            pltpu.VMEM((width, 2 * share), bf16),
            pltpu.VMEM(down.shape, bf16),
            pltpu.VMEM((4, 2 * rows, width), bf16),
            pltpu.VMEM((2, 2 * rows, share), bf16),
            pltpu.VMEM((2 * rows, 2 * share), bf16),
        ]
        + feed_scratch(rows, width, TableSum.COUNT)
        + [pltpu.SemaphoreType.DMA((6 + share // 64,)), pltpu.SemaphoreType.DMA((6,))],
        compiler_params=pltpu.CompilerParams(
            collective_id=2, has_side_effects=True, vmem_limit_bytes=62 << 20
        ),
        name="feed_backward",
    )(own, masks, down_out, narrow, *tables, gate, up, down, gate_up, feed_all)


def flat(table):
    return table.reshape(LANES, table.shape[-1])


def head_table_copies(
    b, heads_hbm, query_out_hbm, kv_out_hbm, heads_in, query_out, key_out, value_out
):
    lanes = pl.ds(pl.multiple_of(b * 2 * HEAD, 128), 2 * HEAD)
    lane = pl.ds(pl.multiple_of(b * HEAD, 128), HEAD)
    return [(heads_hbm.at[:, i], heads_in.at[i]) for i in range(3)] + [
        (query_out_hbm.at[:, :, lanes], query_out),
        (kv_out_hbm.at[:, 0, :, lane], key_out),
        (kv_out_hbm.at[:, 1, :, lane], value_out),
    ]


def head_table_scratch(width):
    return [
        pltpu.VMEM((3, ADAPTERS, RANK, width), bf16),
        pltpu.VMEM((ADAPTERS, RANK, 2 * HEAD), bf16),
        pltpu.VMEM((ADAPTERS, RANK, HEAD), bf16),
        pltpu.VMEM((ADAPTERS, RANK, HEAD), bf16),
    ]


def adapter_mask(ids, t, z, planes, rows):
    sequence = 0 if t * planes * rows < PROMPT else 1 + ((t * planes + z) * rows - PROMPT) // CONT
    owner = lax.broadcasted_iota(jnp.int32, (1, LANES), 1) // RANK
    return jnp.where(owner == ids[0, sequence], 1.0, 0.0)


def rms_rows(source, gains, which, target, rows, add=None):
    gain = gains.at[pl.ds(which, 1)]

    @pl.loop(0, rows // 32)
    def _(i):
        at = span(i, 32)
        v = source[at, :].astype(f32)
        out = v * lax.rsqrt(jnp.mean(v * v, axis=-1, keepdims=True) + epsilon) * gain[...]
        if add is not None:
            out = out + add[at, :].astype(f32)
        target[at, :] = out.astype(target.dtype)


def attention_forward_kernel(
    tokens, gains, ids, mix_in, mix_out, heads_hbm, query_out_hbm, kv_out_hbm,
    query_hbm, key_hbm, value_hbm, out_hbm, gate_hbm, up_hbm,
    queries, values_prompt, values_cont, attended, sums, narrow, mixed_out, narrow_mix,
    attn_out_out, middle_out, normed_feed, cosine, sine, masks_out, normed_out, wall_out, out_out, gate_share,
    up_share,
    heads_in, query_out, key_out, value_out, masks, masks_got, attn_out, middle,
    normed_all, wall, wo, kvp, kvc, acc, total, mixed, send, recv, local,
):
    rows, width = tokens.shape
    dp, b, z = lax.axis_index("dp"), lax.axis_index("blk"), lax.axis_index("ulysses")
    planes = lax.axis_size("ulysses")
    x, y, c = dp % 2, b // 2, b % 2
    base = dp - x
    rank = x * 4 + b
    b_c, b_y = b + 1 - 2 * c, (b + 2) % 4
    b_yc = (b_c + 2) % 4
    pc, py, pyc = (dp, b_c, z), (dp, b_y, z), (dp, b_yc, z)
    other = base + 1 - x
    px, pxc, pxy, pxyc = (other, b, z), (other, b_c, z), (other, b_y, z), (other, b_yc, z)
    pz = (dp, b, z + 1 - 2 * (z % 2))
    left, right = (dp, b, z - 1), (dp, b, z + 1)
    depth = query_hbm.shape[0]
    share = gate_share.shape[1]
    part = out_hbm.shape[0]
    copy = sender(send, recv)

    def block(i):
        return span(i, rows)

    def weight_rows(i):
        return pl.ds(pl.multiple_of(i * depth, 16), depth)

    def out_rows(i):
        return span(i, part)

    heads = ((query_hbm, 2 * HEAD, 0), (key_hbm, HEAD, 2 * HEAD), (value_hbm, HEAD, 3 * HEAD))

    def columns_of(ref, target, size):
        return ref.at[:, pl.ds(pl.multiple_of(target * size, 128), size)]

    own_loads = [
        pltpu.make_async_copy(
            columns_of(ref, b, size), wall.at[weight_rows(rank), pl.ds(to, size)], local.at[i]
        )
        for i, (ref, size, to) in enumerate(heads)
    ]
    own_loads.append(pltpu.make_async_copy(out_hbm, wo.at[out_rows(rank)], local.at[3]))
    table_loads = [
        pltpu.make_async_copy(src, dst, local.at[12 + i])
        for i, (src, dst) in enumerate(
            head_table_copies(
                b, heads_hbm, query_out_hbm, kv_out_hbm, heads_in, query_out, key_out, value_out
            )
        )
    ]
    own_rows = [
        pltpu.make_async_copy(
            columns_of(ref, rank, share), out.at[weight_rows(rank)], local.at[4 + i]
        )
        for i, (ref, out) in enumerate(((gate_hbm, gate_share), (up_hbm, up_share)))
    ]
    for cp in own_loads + table_loads:
        cp.start()

    barrier = pltpu.get_barrier_semaphore()
    for peer in (pc, py, pyc, px, pxc, pxy, pxyc) + tuple(
        (dp, b, (z + d) % planes) for d in range(1, planes)
    ):
        pl.semaphore_signal(barrier, inc=1, device_id=peer, device_id_type=MESH)

    rms_rows(tokens, gains, 0, normed_all.at[block(b)], rows)
    masks[...] = jnp.zeros_like(masks)
    for t in range(4):
        masks[t : t + 1, :] = adapter_mask(ids, t, z, planes, rows)
    masks_out[0] = masks[...]
    pl.semaphore_wait(barrier, 6 + planes)

    stage = []
    for j, (peer, pb) in enumerate(((py, b_y), (pyc, b_yc), (pc, b_c))):
        for i, (ref, size, to) in enumerate(heads):
            stage.append(
                copy(
                    3 + 3 * j + i,
                    columns_of(ref, pb, size),
                    wall.at[weight_rows(rank), pl.ds(to, size)],
                    peer,
                )
            )
    token_copies = [
        copy(0, normed_all.at[block(b)], normed_all.at[block(b)], py),
        copy(1, normed_all.at[block(b)], normed_all.at[block(b)], pc),
        copy(2, normed_all.at[block(b_y)], normed_all.at[block(b_y)], pc),
    ]
    across = [
        copy(12 + i, wall.at[weight_rows(x * 4 + o)], wall.at[weight_rows(x * 4 + o)], px)
        for i, o in enumerate((b, b_c, b_y, b_yc))
    ]
    for cp in stage[:3]:
        cp.start()
    token_copies[0].start()
    for cp in stage[3:]:
        cp.start()
    token_copies[1].start()
    mask_copy = copy(34, masks, masks_got, px)
    mask_copy.start()
    for cp in own_loads[:3]:
        cp.wait()
    across[0].start()
    for cp in stage[6:]:
        cp.wait_recv()
    across[1].start()
    for cp in stage[:3]:
        cp.wait_recv()
    across[2].start()
    for cp in stage[3:6]:
        cp.wait_recv()
    across[3].start()
    token_copies[0].wait_recv()
    token_copies[2].start()
    lane = lax.broadcasted_iota(jnp.int32, (rows, HEAD // 2), 1).astype(f32)
    inverse = jnp.exp(lane * (-2.0 / HEAD * math.log(rope_base)))

    @pl.loop(0, 4)
    def _(t):
        at = block(t)
        token = (t * planes + z) * rows + lax.broadcasted_iota(jnp.int32, (rows, HEAD // 2), 0)
        position = jnp.where(token >= PROMPT, PROMPT + (token - PROMPT) % CONT, token)
        angle = position.astype(f32) * inverse
        cosine[at, :] = jnp.cos(angle)
        sine[at, :] = jnp.sin(angle)

    for cp in table_loads:
        cp.wait()
    mask_copy.wait()
    masks_out[1] = masks_got[...]

    half = part // 2
    rx, ry, rxy = (1 - x) * 4 + b, x * 4 + b_y, (1 - x) * 4 + b_y

    def wo_part(r, h):
        return wo.at[pl.ds(pl.multiple_of(r * part + h * half, 16), half)]

    wo_first = [
        (16, wo_part(rank, 0), px),
        (17, wo_part(rank, 1), py),
        (18, wo_part(rank, 1), px),
        (19, wo_part(rank, 0), py),
        (20, wo.at[out_rows(rank)], pc),
    ]
    wo_next = [
        (21, wo_part(rx, 0), py),
        (22, wo_part(ry, 1), px),
        (23, wo.at[out_rows(rx)], pc),
        (24, wo.at[out_rows(ry)], pc),
        (25, wo.at[out_rows(rxy)], pc),
    ]
    wo_first = [copy(i, ref, ref, peer) for i, ref, peer in wo_first]
    wo_next = [copy(i, ref, ref, peer) for i, ref, peer in wo_next]
    swaps = [
        copy(26 + i, columns_of(ref, x * 4 + b_c, share), out.at[weight_rows(rank)], pc)
        for i, (ref, out) in enumerate(((gate_hbm, gate_share), (up_hbm, up_share)))
    ]
    chips = (
        ((px, rx), (pxc, (1 - x) * 4 + b_c)),
        ((py, ry), (pyc, x * 4 + b_yc)),
        ((pxy, rxy), (pxyc, (1 - x) * 4 + b_yc)),
    )
    got_ranks = (
        (1 - x) * 4 + y * 2 + z % 2, x * 4 + (1 - y) * 2 + z % 2, (1 - x) * 4 + (1 - y) * 2 + z % 2,
    )
    direct, relay, whole = {}, {}, []
    for n, targets in enumerate(chips):
        for i, (ref, out) in enumerate(((gate_hbm, gate_share), (up_hbm, up_share))):
            kind = 2 * n + i
            if kind in (0, 2):
                whole += [
                    copy(63 + kind + j, columns_of(ref, pr, share), out.at[weight_rows(rank)], peer)
                    for j, (peer, pr) in enumerate(targets)
                ]
                continue
            direct[kind] = [
                pltpu.make_async_remote_copy(
                    columns_of(ref, pr, share),
                    out.at[weight_rows(rank)],
                    send.at[51 + 2 * kind + j],
                    recv.at[51 + kind],
                    device_id=peer,
                    device_id_type=MESH,
                )
                for j, (peer, pr) in enumerate(targets)
            ]
            got = out.at[weight_rows(got_ranks[n])]
            relay[kind] = copy(28 + kind, got, got, pz)

    def send_direct(kinds):
        @pl.when(c == z % 2)
        def _():
            for kind in kinds:
                for cp in direct[kind]:
                    cp.start()

    def pass_along(kinds):
        for kind in kinds:
            direct[kind][0].wait_recv()
            relay[kind].start()

    own_loads[3].wait()
    for cp in across:
        cp.wait_recv()
    for cp in wo_first:
        cp.start()
    send_direct((4, 5))
    for cp in swaps + own_rows:
        cp.start()
    token_copies[1].wait_recv()
    token_copies[2].wait_recv()

    outs = [
        pltpu.make_async_copy(normed_all, normed_out, local.at[6]),
        pltpu.make_async_copy(wall, wall_out, local.at[7]),
        pltpu.make_async_copy(wo, out_out, local.at[8]),
        pltpu.make_async_copy(kvp, values_prompt, local.at[9]),
        pltpu.make_async_copy(kvc, values_cont, local.at[10]),
        pltpu.make_async_copy(mixed, mixed_out, local.at[11]),
    ]
    outs[0].start()
    outs[1].start()

    half_head = HEAD // 2

    @pl.loop(0, 4)
    def _(t):
        at = block(t)
        mask = masks[pl.ds(t, 1), :]
        cos, sin = cosine[at, :], sine[at, :]
        a = normed_all[at, :]
        for i in range(3):
            lanes = slice(i * LANES, (i + 1) * LANES)
            narrow[at, lanes] = (dot_nt(a, flat(heads_in[i])) * mask).astype(bf16)

        def turned(pre, scale):
            first, second = pre[:, :half_head], pre[:, half_head:]
            one, two = first * cos - second * sin, second * cos + first * sin
            if scale != 1.0:
                one, two = one * scale, two * scale
            return jnp.concatenate([one, two], axis=1).astype(bf16)

        for h in range(2):
            lanes = slice(h * HEAD, (h + 1) * HEAD)
            pre = dot_nn(a, wall[:, lanes]) + dot_nn(
                narrow[at, :LANES], flat(query_out[:, :, lanes])
            )
            queries[t, h * rows : (h + 1) * rows, :] = turned(pre, HEAD ** (-0.5))
        pre = dot_nn(a, wall[:, 2 * HEAD : 3 * HEAD]) + dot_nn(
            narrow[at, LANES : 2 * LANES], flat(key_out[...])
        )
        key = turned(pre, 1.0)
        value = (
            dot_nn(a, wall[:, 3 * HEAD :]) + dot_nn(
                narrow[at, 2 * LANES :], flat(value_out[...])
            )
        ).astype(bf16)

        @pl.when(t < 2)
        def _():
            kvp[z, 0, t] = key
            kvp[z, 1, t] = value

        @pl.when(t >= 2)
        def _():
            kvc[0, t - 2] = key
            kvc[1, t - 2] = value

    def hop(direction, d):
        index = 42 + d if direction > 0 else 45 + d
        zz = z - d * direction
        return copy(index, kvp.at[zz], kvp.at[zz], right if direction > 0 else left)

    def pass_on(direction, d):
        reach = z < planes - 1 if direction > 0 else z > 0

        @pl.when(reach)
        def _():
            hop(direction, d).start()

    pass_on(1, 0)
    pass_on(-1, 0)

    send_direct((1, 3))
    acc[...] = jnp.zeros_like(acc)
    total[...] = jnp.zeros_like(total)
    row = lax.broadcasted_iota(jnp.int32, (2 * rows, rows), 0) % rows
    causal = lax.broadcasted_iota(jnp.int32, (2 * rows, rows), 1) <= row

    def step(t, k, v, masked):
        e = jnp.exp(soft_cap * jnp.tanh(dot_nt(queries[t], k) * (1.0 / soft_cap)))
        if masked:
            e = jnp.where(causal, e, 0.0)
        some = e[:, :128]
        for n in range(128, rows, 128):
            some = some + e[:, n : n + 128]
        total[t] += some
        acc[t] += dot_nn(e.astype(bf16), v)

    step(0, kvp[z, 0, 0], kvp[z, 1, 0], True)
    step(1, kvp[z, 0, 0], kvp[z, 1, 0], False)
    step(1, kvp[z, 0, 1], kvp[z, 1, 1], True)

    @pl.loop(2, 4)
    def _(t):
        step(t, kvc[0, t - 2], kvc[1, t - 2], True)
        step(t, kvp[z, 0, 0], kvp[z, 1, 0], False)
        step(t, kvp[z, 0, 1], kvp[z, 1, 1], False)

    for cp in whole:
        cp.start()
    wo_first[0].wait_recv()
    wo_next[0].start()
    wo_first[1].wait_recv()
    wo_next[1].start()

    @pl.loop(0, 2 * (planes - 1))
    def _(i):
        d = i // 2 + 1
        direction = 1 - 2 * (i % 2)
        zz = z - d * direction

        @pl.when(i == 2)
        def _():
            pass_along((4, 5))

        @pl.when((zz >= 0) & (zz < planes))
        def _():
            index = 42 + 3 * (i % 2) + d - 1
            here = pltpu.make_async_remote_copy(
                kvp.at[zz], kvp.at[zz], send.at[index], recv.at[index], device_id=left,
                device_id_type=MESH,
            )
            here.wait_recv()

            @pl.when((i % 2 == 0) & (z < planes - 1))
            def _():
                pltpu.make_async_remote_copy(
                    kvp.at[zz], kvp.at[zz], send.at[index + 1], recv.at[index + 1],
                    device_id=right, device_id_type=MESH,
                ).start()

            @pl.when((i % 2 == 1) & (z > 0))
            def _():
                pltpu.make_async_remote_copy(
                    kvp.at[zz], kvp.at[zz], send.at[index + 1], recv.at[index + 1],
                    device_id=left, device_id_type=MESH,
                ).start()

            step(1, kvp[zz, 0, 0], kvp[zz, 1, 0], False)

            @pl.when(zz < z)
            def _():
                step(0, kvp[zz, 0, 0], kvp[zz, 1, 0], False)
                step(1, kvp[zz, 0, 1], kvp[zz, 1, 1], False)

            @pl.loop(2, 4)
            def _(t):
                step(t, kvp[zz, 0, 0], kvp[zz, 1, 0], False)
                step(t, kvp[zz, 0, 1], kvp[zz, 1, 1], False)

    outs[3].start()
    outs[4].start()
    ones = jnp.ones((8, 128), f32)

    @pl.loop(0, 4)
    def _(t):
        whole = jnp.sum(total[t], axis=1, keepdims=True)
        got = (acc[t] / whole).astype(bf16)
        attended[t, :, :HEAD] = got[:rows]
        attended[t, :, HEAD:] = got[rows:]
        sums[t] = lax.dot_general(
            ones, total[t], (((1,), (1,)), ((), ())), precision=lax.Precision.HIGHEST,
            preferred_element_type=f32,
        )

    lanes = pl.ds(pl.multiple_of(b * 2 * HEAD, 128), 2 * HEAD)
    mixes = [
        copy(48 + i, attended.at[o], mixed.at[:, lanes], peer)
        for i, (peer, o) in enumerate(((py, b_y), (pyc, b_yc), (pc, b_c)))
    ]
    for cp in mixes:
        cp.start()
    mixed[:, lanes] = attended[b]
    pass_along((1, 3))
    wo_first[2].wait_recv()
    wo_next[2].start()
    wo_first[3].wait_recv()
    wo_next[3].start()
    wo_next[0].wait_recv()
    wo_next[1].wait_recv()
    wo_next[4].start()
    wo_first[4].wait_recv()
    for cp in wo_next[2:]:
        cp.wait_recv()
    for cp in mixes:
        cp.wait_recv()
    outs[2].start()
    outs[5].start()
    narrow_mix[...] = (dot_nt(mixed[...], mix_in[...]) * masks[pl.ds(b, 1), :]).astype(bf16)

    @pl.loop(0, width // 384)
    def _(n):
        at = span(n, 384)
        attn_out[:, at] = dot_nn(mixed[...], wo[:, at]) + dot_nn(narrow_mix[...], mix_out[:, at])

    rms_rows(attn_out, gains, 1, middle, rows, add=tokens)
    rms_rows(middle, gains, 2, normed_feed, rows)
    attn_out_out[...] = attn_out[...].astype(bf16)
    middle_out[...] = middle[...].astype(bf16)

    for cp in swaps + whole:
        cp.wait()
    for cp in relay.values():
        cp.wait()

    @pl.when(c == z % 2)
    def _():
        for pair in direct.values():
            for cp in pair:
                cp.wait_send()

    for cp in own_rows + outs:
        cp.wait()
    for cp in stage + token_copies + across + wo_first + wo_next + mixes:
        cp.wait_send()

    @pl.loop(0, 2 * (planes - 1))
    def _(i):
        d = i // 2
        direction = 1 - 2 * (i % 2)
        zz = z - d * direction
        onward = z + direction

        @pl.when((zz >= 0) & (zz < planes) & (onward >= 0) & (onward < planes))
        def _():
            index = 42 + 3 * (i % 2) + d
            pltpu.make_async_remote_copy(
                kvp.at[zz], kvp.at[zz], send.at[index], recv.at[index], device_id=left,
                device_id_type=MESH,
            ).wait_send()


def attention_forward(tokens, gains, ids, mix_in, mix_out, tables, weights, share):
    rows, width = tokens.shape
    planes = lax.axis_size("ulysses")
    return pl.pallas_call(
        attention_forward_kernel,
        out_shape=(
            shape((4, 2 * rows, HEAD), bf16),
            shape((planes, 2, 2, rows, HEAD), bf16),
            shape((2, 2, rows, HEAD), bf16),
            shape((4, rows, 2 * HEAD), bf16),
            shape((4, 8, 2 * rows), f32),
            shape((4 * rows, 3 * LANES), bf16),
            shape((rows, 8 * HEAD), bf16),
            shape((rows, LANES), bf16),
            shape((rows, width), bf16),
            shape((rows, width), bf16),
            shape((rows, width), bf16),
            shape((4 * rows, HEAD // 2), f32),
            shape((4 * rows, HEAD // 2), f32),
            shape((2, 16, LANES), f32),
            shape((4 * rows, width), bf16),
            shape((width, 4 * HEAD), bf16),
            shape((8 * HEAD, width), bf16),
            shape((width, share), bf16),
            shape((width, share), bf16),
        ),
        in_specs=[VM, VM, pl.BlockSpec(memory_space=pltpu.SMEM), VM, VM] + [ANY] * 9,
        out_specs=(VM, ANY, ANY, VM, VM, VM, ANY) + (VM,) * 7 + (ANY,) * 5,
        scratch_shapes=head_table_scratch(width)
        + [
            pltpu.VMEM((16, LANES), f32),
            pltpu.VMEM((16, LANES), f32),
            pltpu.VMEM((rows, width), f32),
            pltpu.VMEM((rows, width), f32),
            pltpu.VMEM((4 * rows, width), bf16),
            pltpu.VMEM((width, 4 * HEAD), bf16),
            pltpu.VMEM((8 * HEAD, width), bf16),
            pltpu.VMEM((planes, 2, 2, rows, HEAD), bf16),
            pltpu.VMEM((2, 2, rows, HEAD), bf16),
            pltpu.VMEM((4, 2 * rows, HEAD), f32),
            pltpu.VMEM((4, 2 * rows, 128), f32),
            pltpu.VMEM((rows, 8 * HEAD), bf16),
            pltpu.SemaphoreType.DMA((67,)),
            pltpu.SemaphoreType.DMA((67,)),
            pltpu.SemaphoreType.DMA((18,)),
        ],
        compiler_params=pltpu.CompilerParams(
            collective_id=3, has_side_effects=True, vmem_limit_bytes=62 << 20
        ),
        name="attention_forward",
    )(tokens, gains, ids, mix_in, mix_out, *tables, *weights)


class Places:
    def __init__(self):
        dp, b, z = lax.axis_index("dp"), lax.axis_index("blk"), lax.axis_index("ulysses")
        self.b, self.z, self.planes = b, z, lax.axis_size("ulysses")
        x, c = dp % 2, b % 2
        self.x, self.y, self.c = x, b // 2, c
        self.b_c, self.b_y = b + 1 - 2 * c, (b + 2) % 4
        self.b_yc = (self.b_c + 2) % 4
        other = dp + 1 - 2 * x
        self.dp, self.other = dp, other
        self.pc, self.py, self.pyc = (dp, self.b_c, z), (dp, self.b_y, z), (dp, self.b_yc, z)
        self.px = (other, b, z)
        self.plane = (
            self.pc, self.py, self.pyc, self.px,
            (other, self.b_c, z), (other, self.b_y, z), (other, self.b_yc, z),
        )
        self.rank = x * 4 + b
        self.near = (x * 4 + b, (1 - x) * 4 + b, (1 - x) * 4 + self.b_y, x * 4 + self.b_y)
        self.far = (x * 4 + self.b_c, (1 - x) * 4 + self.b_c, (1 - x) * 4 + self.b_yc, x * 4 + self.b_yc)

    def along(self, d):
        return (self.z + d) % self.planes

    def up(self, d):
        return (self.dp, self.b, self.along(d))


class TableSum:
    COUNT = 6

    def __init__(self, place, copy, first, source, arrived, piece, target, local):
        self.place, self.source, self.arrived, self.piece = place, source, arrived, piece
        n = place.planes
        self.q = piece.shape[0]
        self.out = [
            copy(first + d - 1, source.at[span(place.along(d), self.q)], arrived.at[d - 1], place.up(d))
            for d in range(1, n)
        ]
        self.own = pltpu.make_async_copy(piece, target(place.z), local)
        self.back = [
            copy(first + 2 + d, piece, target(place.z), place.up(d)) for d in range(1, n)
        ]

    def scatter(self):
        for c in self.out:
            c.start()

    def gather(self):
        for c in self.out:
            c.wait_recv()
        got = self.source[span(self.place.z, self.q), :].astype(f32)
        for i in range(self.place.planes - 1):
            got = got + self.arrived[i].astype(f32)
        self.piece[...] = got.astype(bf16)
        self.own.start()
        for c in self.back:
            c.start()

    def ready(self):
        for c in self.back:
            c.wait_recv()
        self.own.wait()

    def finish(self):
        self.ready()
        self.close()

    def close(self):
        for c in self.out + self.back:
            c.wait_send()


class PlaneSpread:
    COUNT = 10

    def __init__(self, place, copy, first, own, gathered):
        half = place.planes // 2
        parts = (pl.ds(0, half), pl.ds(half, half))
        mine, rx, rxy, ry = place.near
        px, py, pc = place.px, place.py, place.pc

        def same(i, ref, peer):
            return copy(first + i, ref, ref, peer)

        def send(i, part, peer):
            return copy(first + i, own.at[part], gathered.at[mine, part], peer)

        self.first = [
            send(0, parts[0], px),
            send(1, parts[1], py),
            send(2, parts[1], px),
            send(3, parts[0], py),
            copy(first + 4, own, gathered.at[mine], pc),
        ]
        self.next = [
            same(5, gathered.at[rx, parts[0]], py),
            same(6, gathered.at[ry, parts[1]], px),
            same(7, gathered.at[rx], pc),
            same(8, gathered.at[ry], pc),
            same(9, gathered.at[rxy], pc),
        ]

    def plane(self):
        for c in self.first:
            c.start()

    def forward(self):
        for i in range(4):
            self.first[i].wait_recv()
            self.next[i].start()

    def corner(self):
        self.next[0].wait_recv()
        self.next[1].wait_recv()
        self.next[4].start()

    def finish(self):
        self.first[4].wait_recv()
        for c in self.next[2:]:
            c.wait_recv()
        for c in self.first + self.next:
            c.wait_send()


class TableSpread:
    COUNT = TableSum.COUNT + PlaneSpread.COUNT

    def __init__(self, place, copy, first, source, arrived, piece, gathered, local):
        own = gathered.at[place.rank]
        self.sum = TableSum(
            place, copy, first, source, arrived, piece, lambda z: gathered.at[place.rank, z], local
        )
        self.spread = PlaneSpread(place, copy, first + TableSum.COUNT, own, gathered)
        self.scatter, self.gather = self.sum.scatter, self.sum.gather
        self.forward, self.corner = self.spread.forward, self.spread.corner

    def plane(self):
        self.sum.ready()
        self.spread.plane()

    def finish(self):
        self.sum.close()
        self.spread.finish()


class TableReduce:
    COUNT = 10

    def __init__(self, place, copy, first, table, part, from_core, from_x, from_y, diag, total, local):
        self.part, self.from_core, self.from_x, self.from_y = part, from_core, from_x, from_y
        self.diag, self.total = diag, total
        m = total.shape[0]
        self.m, self.h = m, m // 2
        h0, h1 = pl.ds(0, self.h), pl.ds(self.h, self.h)
        self.h0, self.h1 = h0, h1
        self.core = [
            copy(first + i, table.at[place.far[i]], from_core.at[i], place.pc) for i in range(4)
        ]
        self.load = [
            pltpu.make_async_copy(table.at[place.near[i]], part.at[i], local(i)) for i in range(4)
        ]
        self.d = [
            copy(first + 4, part.at[2, h0], diag.at[h0], place.px),
            copy(first + 5, part.at[2, h1], diag.at[h1], place.py),
        ]
        self.e = [
            copy(first + 6, part.at[1, h0], from_x.at[h0], place.px),
            copy(first + 7, part.at[3, h1], from_y.at[h1], place.py),
            copy(first + 8, part.at[1, h1], from_x.at[h1], place.px),
            copy(first + 9, part.at[3, h0], from_y.at[h0], place.py),
        ]

    def begin(self):
        for c in self.core + self.load:
            c.start()

    def merge(self):
        for i in (2, 1, 3, 0):
            self.load[i].wait()
            self.core[i].wait_recv()
            add_into(self.part.at[i], self.from_core.at[i], self.m, 16)
            if i == 2:
                self.d[0].start()
                self.d[1].start()
        self.e[0].start()
        self.e[1].start()

    def corner(self):
        self.d[0].wait_recv()
        add_into(self.part.at[3, self.h0], self.diag.at[self.h0], self.h, 16)
        self.e[3].start()
        self.d[1].wait_recv()
        add_into(self.part.at[1, self.h1], self.diag.at[self.h1], self.h, 16)
        self.e[2].start()

    def finish(self):
        for e in self.e:
            e.wait_recv()

        @pl.loop(0, self.m // 16)
        def _(i):
            at = span(i, 16)
            self.total[at, :] = (
                self.part[0, at, :].astype(f32)
                + self.from_x[at, :].astype(f32)
                + self.from_y[at, :].astype(f32)
            ).astype(bf16)

        for c in self.core + self.d + self.e:
            c.wait_send()


def attention_backward_kernel(
    middle, attn_out, cotangent, gains, masks, mixed, narrow_mix, mix_in, mix_out,
    queries, kvp, kvc, attended, sums, narrow, cosine, sine,
    grad_feed_hbm, tokens_hbm, heads_hbm, query_out_hbm, kv_out_hbm, out_hbm, normed_hbm, wall_hbm, feed_hbm, feed_share,
    tokens_grad, g_feed_table, g_feed_share, g_head_table, g_head_share,
    heads_in, query_out, key_out, value_out, wo, wall, grad_attn, grad_mixed,
    g, delta, inv, dq, kv_own, kv_far, kv_send, kv_got, grad_pre, back,
    from_core, from_y,
    feed_table, a_part, a_core, a_x, a_y, a_diag, a_total, a_in, a_piece,
    h_table, h_part, h_core, h_x, h_y, h_diag, h_total, h_in, h_piece,
    o_table, o_got, o_total, o_in, o_piece,
    send, recv, local,
):
    rows, width = tokens_grad.shape
    place = Places()
    b, z, planes = place.b, place.z, place.planes
    copy = sender(send, recv)
    normed_all = wo.at[pl.ds(0, 4 * rows)]
    part = [wo.at[pl.ds((4 + i) * rows, rows)] for i in range(4)]
    own_share = pltpu.make_async_copy(feed_share, g_feed_share.at[place.rank], local.at[0])
    loads = [
        pltpu.make_async_copy(src, dst, local.at[14 + i])
        for i, (src, dst) in enumerate(
            [(out_hbm, wo)]
            + head_table_copies(
                b, heads_hbm, query_out_hbm, kv_out_hbm, heads_in, query_out, key_out, value_out
            )
            + [(wall_hbm, wall), (feed_hbm, feed_table.at[:, pl.ds(0, 3 * RANK)])]
        )
    ]
    grad_feed = from_y
    bring_feed = pltpu.make_async_copy(grad_feed_hbm, grad_feed, local.at[24])
    bring_feed.start()
    late = pltpu.make_async_copy(normed_hbm, normed_all, local.at[1])
    for c in loads:
        c.start()
    own_share.start()
    barrier = pltpu.get_barrier_semaphore()
    peers = list(place.plane) + [place.up(d) for d in range(1, planes)]
    for peer in peers:
        pl.semaphore_signal(barrier, inc=1, device_id=peer, device_id_type=MESH)
    pl.semaphore_wait(barrier, len(peers))

    swaps = []
    for j, (peer, pb) in enumerate(
        ((place.py, place.b_y), (place.pyc, place.b_yc), (place.pc, place.b_c))
    ):
        for h in range(2):
            lanes = pl.ds(pl.multiple_of(pb * 2 * HEAD + h * HEAD, 128), HEAD)
            swaps.append(
                copy(
                    2 * j + h,
                    grad_mixed.at[:, lanes],
                    g.at[b, pl.ds(h * rows, rows)],
                    peer,
                )
            )
    at = 12
    feed_reduce = TableReduce(
        place, copy, at, feed_table, a_part, a_core, a_x, a_y, a_diag, a_total,
        lambda i: local.at[2 + i],
    )
    at += TableReduce.COUNT
    feed_spread = TableSpread(place, copy, at, a_total, a_in, a_piece, g_feed_table, local.at[6])
    at += TableSpread.COUNT
    share_spread = PlaneSpread(place, copy, at, feed_share, g_feed_share)
    at += PlaneSpread.COUNT
    head_reduce = TableReduce(
        place, copy, at, h_table, h_part, h_core, h_x, h_y, h_diag, h_total,
        lambda i: local.at[8 + i],
    )
    at += TableReduce.COUNT
    head_spread = TableSpread(place, copy, at, h_total, h_in, h_piece, g_head_table, local.at[12])
    at += TableSpread.COUNT
    out_spread = TableSpread(place, copy, at, o_total, o_in, o_piece, g_head_share, local.at[13])
    at += TableSpread.COUNT
    lanes_half = o_total.shape[0]
    out_swap = copy(
        at, o_table.at[span(1 - place.x, lanes_half)], o_got, place.px
    )

    bring_feed.wait()

    @pl.loop(0, rows // 32)
    def _(i):
        at = span(i, 32)
        grad = cotangent[at, :].astype(f32) + norm_grad(
            middle[at, :].astype(f32), gains[2:3, :], grad_feed[at, :].astype(f32)
        )
        tokens_grad[at, :] = grad
        grad_attn[at, :] = norm_grad(attn_out[at, :].astype(f32), gains[1:2, :], grad).astype(bf16)

    back_mix = (dot_nt(grad_attn[...], mix_out[...]) * masks[0, pl.ds(b, 1), :]).astype(bf16)
    loads[0].wait()
    for j, pb in enumerate((place.b_y, place.b_yc, place.b_c, b)):

        @pl.loop(0, 2)
        def _(h):
            at = span(pb * 2 + h, HEAD)
            grad_mixed[:, at] = (
                dot_nt(grad_attn[...], wo[at, :]) + dot_nn(back_mix, mix_in[:, at])
            ).astype(bf16)

        if j < 3:
            for c in swaps[2 * j : 2 * j + 2]:
                c.start()
    late.start()
    for c in loads[1:]:
        c.wait()
    for n in range(8):
        lanes = slice(n * HEAD, (n + 1) * HEAD)
        got = dot_tn(back_mix, mixed[:, lanes]).astype(bf16)
        for a in range(ADAPTERS):
            h_table[a, 3 * RANK :, lanes] = got[a * RANK : (a + 1) * RANK]
    h_table[:, 3 * RANK :, 8 * HEAD :] = jnp.zeros((ADAPTERS, RANK, width - 8 * HEAD), bf16)

    @pl.loop(0, width // 256)
    def _(n):
        at = span(n, 256)
        got = dot_tn(narrow_mix[...], grad_attn[:, at]).astype(bf16)
        for a in range(ADAPTERS):
            feed_table[a, 3 * RANK :, at] = got[a * RANK : (a + 1) * RANK]

    tokens = grad_attn
    bring_tokens = pltpu.make_async_copy(tokens_hbm, tokens, local.at[23])
    bring_tokens.start()
    feed_reduce.begin()
    for h in range(2):
        lanes = pl.ds(pl.multiple_of(b * 2 * HEAD + h * HEAD, 128), HEAD)
        g[b, h * rows : (h + 1) * rows, :] = grad_mixed[:, lanes]
    for c in swaps:
        c.wait()
    share_spread.plane()

    ones = jnp.ones((8, HEAD), f32)

    @pl.loop(0, 4)
    def _(t):
        for h in range(2):
            at_h = slice(h * rows, (h + 1) * rows)
            lanes = slice(h * HEAD, (h + 1) * HEAD)
            product = g[t, at_h, :].astype(f32) * attended[t, :, lanes].astype(f32)
            delta[t, :, at_h] = lax.dot_general(
                ones, product, (((1,), (1,)), ((), ())), precision=lax.Precision.HIGHEST,
                preferred_element_type=f32,
            )
        inv[t] = 1.0 / sums[t]

    query = lax.broadcasted_iota(jnp.int32, (rows, 2 * rows), 1) % rows
    causal = lax.broadcasted_iota(jnp.int32, (rows, 2 * rows), 0) <= query

    def step(t, k, v, total, slot, masked):
        q, gt = queries[t], g[t]
        th = jnp.tanh(dot_nt(k, q) * (1.0 / soft_cap))
        p = jnp.exp(soft_cap * th) * inv[t, 0:1, :]
        if masked:
            p = jnp.where(causal, p, 0.0)
        total[1, slot] += dot_nn(p.astype(bf16), gt)
        ds = (p * (dot_nt(v, gt) - delta[t, 0:1, :]) * (1.0 - th * th)).astype(bf16)
        total[0, slot] += dot_nn(ds, q)
        dq[t] += dot_tn(ds, k)

    dq[...] = jnp.zeros_like(dq)
    kv_own[...] = jnp.zeros_like(kv_own)

    def kv_copy(d):
        return copy(6 + d - 1, kv_send.at[d - 1], kv_got.at[d - 1], place.up(d))

    @pl.loop(1, planes)
    def _(d):
        zz = (z + d) % planes
        kv_far[...] = jnp.zeros_like(kv_far)
        step(1, kvp[zz, 0, 0], kvp[zz, 1, 0], kv_far, 0, False)

        @pl.when(zz < z)
        def _():
            step(0, kvp[zz, 0, 0], kvp[zz, 1, 0], kv_far, 0, False)
            step(1, kvp[zz, 0, 1], kvp[zz, 1, 1], kv_far, 1, False)

        @pl.loop(2, 4)
        def _(t):
            step(t, kvp[zz, 0, 0], kvp[zz, 1, 0], kv_far, 0, False)
            step(t, kvp[zz, 0, 1], kvp[zz, 1, 1], kv_far, 1, False)

        kv_send[d - 1] = kv_far[...].astype(bf16)
        for k in range(1, planes):

            @pl.when(d == k)
            def _(k=k):
                kv_copy(k).start()
                if k == 1:
                    feed_reduce.merge()
                if k == 2:
                    feed_reduce.corner()
                    share_spread.forward()
                if k == 3:
                    share_spread.corner()

    feed_reduce.finish()
    feed_spread.scatter()
    step(0, kvp[z, 0, 0], kvp[z, 1, 0], kv_own, 0, True)
    step(1, kvp[z, 0, 0], kvp[z, 1, 0], kv_own, 0, False)
    step(1, kvp[z, 0, 1], kvp[z, 1, 1], kv_own, 1, True)

    @pl.loop(2, 4)
    def _(t):
        step(t, kvc[0, t - 2], kvc[1, t - 2], kv_own, t, True)
        step(t, kvp[z, 0, 0], kvp[z, 1, 0], kv_own, 0, False)
        step(t, kvp[z, 0, 1], kvp[z, 1, 1], kv_own, 1, False)

    late.wait()
    feed_spread.gather()
    for d in range(1, planes):
        kv_copy(d).wait_recv()
        kv_own[:, 0:2] += kv_got[d - 1].astype(f32)
    half_head = HEAD // 2

    @pl.loop(0, 4)
    def _(t):
        at = span(t, rows)
        cos, sin = cosine[at, :], sine[at, :]
        mask = masks[0, pl.ds(t, 1), :]

        def turned(pre, scale):
            first, second = pre[:, :half_head], pre[:, half_head:]
            one, two = first * cos + second * sin, second * cos - first * sin
            if scale != 1.0:
                one, two = one * scale, two * scale
            return jnp.concatenate([one, two], axis=1).astype(bf16)

        for h in range(2):
            grad_pre[at, h * HEAD : (h + 1) * HEAD] = turned(
                dq[t, h * rows : (h + 1) * rows, :], HEAD ** (-0.5)
            )
        grad_pre[at, 2 * HEAD : 3 * HEAD] = turned(kv_own[0, t], 1.0)
        grad_pre[at, 3 * HEAD :] = kv_own[1, t].astype(bf16)
        for i, (lanes, table) in enumerate(
            (
                (slice(0, 2 * HEAD), query_out),
                (slice(2 * HEAD, 3 * HEAD), key_out),
                (slice(3 * HEAD, 4 * HEAD), value_out),
            )
        ):
            back[at, i * LANES : (i + 1) * LANES] = (
                dot_nt(grad_pre[at, lanes], flat(table[...])) * mask
            ).astype(bf16)

    feed_spread.plane()
    for i, lanes in enumerate(
        (slice(0, 2 * HEAD), slice(2 * HEAD, 3 * HEAD), slice(3 * HEAD, 4 * HEAD))
    ):
        o_table[:, lanes] = dot_tn(
            narrow[:, i * LANES : (i + 1) * LANES], grad_pre[:, lanes]
        ).astype(bf16)
    out_swap.start()

    @pl.loop(0, width // 256)
    def _(n):
        at = span(n, 256)
        got = dot_tn(back[...], normed_all[:, at]).astype(bf16)
        for i in range(3):
            for a in range(ADAPTERS):
                first = i * LANES + a * RANK
                h_table[a, i * RANK : (i + 1) * RANK, at] = got[first : first + RANK]

    head_reduce.begin()

    def project(slot, target):
        at_rows = span(target, rows)

        @pl.loop(0, width // 256)
        def _(n):
            at = span(n, 256)
            part[slot][:, at] = (
                dot_nt(grad_pre[at_rows, :], wall[at, :])
                + dot_nn(back[at_rows, :], heads_in[:, :, :, at].reshape(3 * LANES, 256))
            ).astype(bf16)

    to_core = [copy(9 + i, part[i], from_core.at[i], place.pc) for i in range(2)]
    to_y = copy(11, part[2], from_y, place.py)
    project(0, place.b_yc)
    to_core[0].start()
    head_reduce.merge()
    feed_spread.forward()
    project(2, place.b_y)
    head_reduce.corner()
    to_core[0].wait_recv()
    add_into(part[2], from_core.at[0], rows)
    to_y.start()
    out_swap.wait_recv()

    @pl.loop(0, lanes_half // 16)
    def _(i):
        at = span(i, 16)
        mine = pl.ds(pl.multiple_of(place.x * lanes_half + i * 16, 16), 16)
        o_total[at, :] = (o_table[mine, :].astype(f32) + o_got[at, :].astype(f32)).astype(bf16)

    feed_spread.corner()
    out_spread.scatter()
    head_reduce.finish()
    head_spread.scatter()
    project(1, place.b_c)
    to_core[1].start()
    head_spread.gather()
    out_spread.gather()
    project(3, b)
    head_spread.plane()
    out_spread.plane()
    head_spread.forward()
    out_spread.forward()
    to_core[1].wait_recv()
    head_spread.corner()
    out_spread.corner()
    to_y.wait_recv()
    bring_tokens.wait()

    @pl.loop(0, rows // 32)
    def _(i):
        at = span(i, 32)
        grad = (
            part[3][at, :].astype(f32)
            + from_core[1, at, :].astype(f32)
            + from_y[at, :].astype(f32)
        )
        tokens_grad[at, :] += norm_grad(tokens[at, :].astype(f32), gains[0:1, :], grad)

    for spread in (share_spread, feed_spread, out_spread, head_spread):
        spread.finish()
    own_share.wait()
    out_swap.wait_send()
    to_y.wait_send()
    for c in to_core:
        c.wait_send()
    for d in range(1, planes):
        kv_copy(d).wait_send()


def attention_backward(rows_in, kept, grad_feed, tokens, tables, weights, feed_table, feed_share):
    rows, width = rows_in[0].shape
    planes = lax.axis_size("ulysses")
    m = 4 * RANK
    hm = 4 * RANK
    ow = 4 * HEAD
    om = LANES // 2
    count = 12 + 2 * TableReduce.COUNT + 3 * TableSpread.COUNT + PlaneSpread.COUNT + 1

    def reduce_scratch(m):
        return [
            pltpu.VMEM((ADAPTERS, m, width), bf16),
            pltpu.VMEM((4, m, width), bf16),
            pltpu.VMEM((4, m, width), bf16),
            pltpu.VMEM((m, width), bf16),
            pltpu.VMEM((m, width), bf16),
            pltpu.VMEM((m, width), bf16),
            pltpu.VMEM((m, width), bf16),
        ]

    def spread_scratch(m, w):
        return [
            pltpu.VMEM((planes - 1, m // planes, w), bf16),
            pltpu.VMEM((m // planes, w), bf16),
        ]

    return pl.pallas_call(
        attention_backward_kernel,
        out_shape=(
            shape((rows, width), f32),
            shape((8, planes, m // planes, width), bf16),
            shape((8,) + feed_share.shape, bf16),
            shape((8, planes, hm // planes, width), bf16),
            shape((8, planes, om // planes, ow), bf16),
        ),
        in_specs=[VM] * 17 + [ANY] * 10,
        out_specs=(VM, ANY, ANY, ANY, ANY),
        scratch_shapes=head_table_scratch(width)
        + [
            pltpu.VMEM((8 * HEAD, width), bf16),
            pltpu.VMEM((width, 4 * HEAD), bf16),
            pltpu.VMEM((rows, width), bf16),
            pltpu.VMEM((rows, 8 * HEAD), bf16),
            pltpu.VMEM((4, 2 * rows, HEAD), bf16),
            pltpu.VMEM((4, 8, 2 * rows), f32),
            pltpu.VMEM((4, 8, 2 * rows), f32),
            pltpu.VMEM((4, 2 * rows, HEAD), f32),
            pltpu.VMEM((2, 4, rows, HEAD), f32),
            pltpu.VMEM((2, 2, rows, HEAD), f32),
            pltpu.VMEM((planes - 1, 2, 2, rows, HEAD), bf16),
            pltpu.VMEM((planes - 1, 2, 2, rows, HEAD), bf16),
            pltpu.VMEM((4 * rows, 4 * HEAD), bf16),
            pltpu.VMEM((4 * rows, 3 * LANES), bf16),
            pltpu.VMEM((2, rows, width), bf16),
            pltpu.VMEM((rows, width), bf16),
        ]
        + reduce_scratch(m)
        + spread_scratch(m, width)
        + reduce_scratch(hm)
        + spread_scratch(hm, width)
        + [
            pltpu.VMEM((LANES, ow), bf16),
            pltpu.VMEM((om, ow), bf16),
            pltpu.VMEM((om, ow), bf16),
        ]
        + spread_scratch(om, ow)
        + [
            pltpu.SemaphoreType.DMA((count,)),
            pltpu.SemaphoreType.DMA((count,)),
            pltpu.SemaphoreType.DMA((25,)),
        ],
        compiler_params=pltpu.CompilerParams(
            collective_id=4, has_side_effects=True, vmem_limit_bytes=63 << 20
        ),
        name="attention_backward",
    )(*rows_in, *kept, grad_feed, tokens, *tables, *weights, feed_table, feed_share)


def shards(
    tokens,
    query_weight,
    key_projection,
    value_projection,
    out_weight,
    gate_weight,
    up_weight,
    down_weight,
    attn_in_gain,
    attn_out_gain,
    feed_in_gain,
    feed_out_gain,
    adapt_heads_in,
    adapt_query_out,
    adapter_key_value_second,
    adapt_mix_in,
    adapt_mix_out,
    adapt_feed_in,
    adapt_feed_out,
    adapt_down_in,
    adapt_down_out,
    adapter_ids,
    cotangent,
):
    width = tokens.shape[1]
    blk_n = lax.axis_size("blk")
    dp_n = lax.axis_size("dp")
    rank = lax.axis_index("dp") % 2 * blk_n + lax.axis_index("blk")
    ff = gate_weight.shape[1]
    share = ff // (2 * blk_n)
    weights = (
        query_weight, key_projection, value_projection, out_weight, gate_weight, up_weight,
        down_weight,
    )
    if dp_n > 2:
        weights = tuple(
            lax.dynamic_slice_in_dim(
                lax.all_gather(weight, PLANE, axis=0, tiled=True),
                rank * (weight.shape[0] * dp_n // 2),
                weight.shape[0] * dp_n // 2,
            )
            for weight in weights
        )
    down_rows = weights[6]
    gains = jnp.stack([attn_in_gain, attn_out_gain, feed_in_gain, feed_out_gain])
    mix_in, mix_out, down_out = flat(adapt_mix_in), flat(adapt_mix_out), flat(adapt_down_out)
    head_tables = (adapt_heads_in, adapt_query_out, adapter_key_value_second)
    feed_tables = (adapt_feed_in, adapt_feed_out, adapt_down_in)
    (
        queries, kvp, kvc, attended, exp_sum, narrow_heads, mixed, narrow_mix, attn_out, middle,
        normed_feed, cosine, sine, masks, normed_all, head_weight, out_full, gate_share, up_share,
    ) = attention_forward(
        tokens, gains, adapter_ids, mix_in, mix_out, head_tables, weights[:6], share
    )
    layer_out, grad_branch, narrow_feed, feed_all, gate_up = feed_forward(
        normed_feed, middle, cotangent, gains, masks, down_out, feed_tables, gate_share, up_share,
        down_rows,
    )
    grad_feed, feed_table, share_sum = feed_backward(
        grad_branch, masks, down_out, narrow_feed, feed_tables, gate_share, up_share, down_rows,
        gate_up, feed_all,
    )
    tokens_grad, feed_rows, feed_columns, head_rows, head_columns = attention_backward(
        (
            middle, attn_out, cotangent, gains, masks, mixed, narrow_mix, mix_in, mix_out,
        ),
        (queries, kvp, kvc, attended, exp_sum, narrow_heads, cosine, sine),
        grad_feed,
        tokens,
        head_tables,
        (out_full, normed_all, head_weight),
        feed_table,
        share_sum,
    )

    feed_rows = feed_rows.reshape(ADAPTERS, 4, RANK, width)
    feed_columns = (
        feed_columns.reshape(8, 3, ADAPTERS, RANK, share)
        .transpose(2, 1, 3, 0, 4)
        .reshape(ADAPTERS, 3, RANK, ff)
    )
    head_rows = head_rows.reshape(ADAPTERS, 4, RANK, width)
    head_columns = (
        head_columns.reshape(2, 4, LANES // 2, 4 * HEAD)
        .transpose(0, 2, 1, 3)
        .reshape(ADAPTERS, RANK, 4, 4 * HEAD)
    )

    def joined(first, last):
        return head_columns[..., first:last].reshape(ADAPTERS, RANK, -1)

    summed = (
        head_rows[:, :3],
        joined(0, 2 * HEAD),
        jnp.stack([joined(2 * HEAD, 3 * HEAD), joined(3 * HEAD, 4 * HEAD)], axis=1),
        head_rows[:, 3, :, : mixed.shape[1]],
        feed_rows[:, 3],
        feed_rows[:, :2],
        feed_columns[:, :2],
        feed_columns[:, 2],
        feed_rows[:, 2],
    )
    summed = tuple(table.astype(f32) for table in summed)
    if dp_n > 2:
        summed = tuple(lax.psum(table * 0.5, "dp") for table in summed)
    return (layer_out, tokens_grad) + summed


def solution(mesh):
    sharded = P(EVERY, None)
    rowwise = P(PLANE, None)
    placed = (
        (sharded,) + (rowwise,) * 7 + (P(),) * 13 + (P("dp", None), sharded)
    )
    return jax.shard_map(
        shards,
        mesh=mesh,
        in_specs=placed,
        out_specs=(sharded, sharded) + (P(),) * 9,
        check_vma=False,
    )
```

```python
import math

import jax
import jax.numpy as jnp
from jax import lax
from jax.experimental import pallas as pl
from jax.experimental.pallas import tpu as pltpu
from jax.sharding import PartitionSpec as P

HEADS = 8
KV_HEADS = 4
HEAD = 256
RANK = 16
ADAPTERS = 8
LANES = RANK * ADAPTERS
PROMPT = 2048
CONT = 256
CONTS = 8

epsilon = 1e-06
soft_cap = 50.0
rope_base = 10000.0
PLANE = ("dp", "blk")
EVERY = ("dp", "blk", "ulysses")
f32 = jnp.float32
bf16 = jnp.bfloat16


def dot_nn(a, b):
    return jnp.dot(a, b, preferred_element_type=f32)


def dot_nt(a, b):
    return lax.dot_general(a, b, (((1,), (1,)), ((), ())), preferred_element_type=f32)


def dot_tn(a, b):
    return lax.dot_general(a, b, (((0,), (0,)), ((), ())), preferred_element_type=f32)


def norm_grad(values, gain_row, grad_out):
    scale = lax.rsqrt(jnp.mean(values * values, axis=-1, keepdims=True) + epsilon)
    weighted = grad_out * gain_row
    return scale * weighted - values * (
        scale * scale * scale * jnp.mean(values * weighted, axis=-1, keepdims=True)
    )


def shape(dims, dtype):
    return jax.ShapeDtypeStruct(dims, dtype)


VM = pl.BlockSpec(memory_space=pltpu.VMEM)


MESH = pl.DeviceIdType.MESH


def neighbours():
    dp, b, z = lax.axis_index("dp"), lax.axis_index("blk"), lax.axis_index("ulysses")
    across_x = (dp + 1 - 2 * (dp % 2), b, z)
    across_y = (dp, (b + 2) % 4, z)
    sibling = (dp, b + 1 - 2 * (b % 2), z)
    return across_x, across_y, sibling


def greet(peers):
    barrier = pltpu.get_barrier_semaphore()
    for peer in peers:
        pl.semaphore_signal(barrier, inc=1, device_id=peer, device_id_type=MESH)
    pl.semaphore_wait(barrier, len(peers))


def sender(send, recv):
    def copy(index, src, dst, peer):
        return pltpu.make_async_remote_copy(
            src, dst, send.at[index], recv.at[index], device_id=peer, device_id_type=MESH
        )

    return copy


def add_into(target, source, count, step=32):
    @pl.loop(0, count // step)
    def _(i):
        at = pl.ds(pl.multiple_of(i * step, step), step)
        target[at, :] = (target[at, :].astype(f32) + source[at, :].astype(f32)).astype(target.dtype)


class PlaneGather:
    COUNT = 10

    def __init__(self, copy, own, land, rows):
        px, py, pc = neighbours()
        h = rows // 2
        h0, h1 = pl.ds(0, h), pl.ds(h, h)
        near, far = pl.ds(0, rows), pl.ds(rows, rows)
        self.c = [
            copy(0, own, land.at[0, far], pc),
            copy(1, own.at[h0], land.at[1, h0], px),
            copy(2, own.at[h1], land.at[1, h1], py),
            copy(3, own.at[h1], land.at[3, h0], px),
            copy(4, own.at[h0], land.at[3, h1], py),
            copy(5, land.at[1, h0], land.at[2, h0], py),
            copy(6, land.at[1, h1], land.at[2, h1], px),
            copy(7, land.at[1, near], land.at[1, far], pc),
            copy(8, land.at[3, near], land.at[3, far], pc),
            copy(9, land.at[2, near], land.at[2, far], pc),
        ]

    def begin(self):
        for i in range(3):
            self.c[i].start()

    def before(self, i):
        c = self.c

        @pl.when(i == 0)
        def _():
            c[0].wait_recv()

        @pl.when(i == 1)
        def _():
            c[1].wait_recv()
            c[5].start()
            c[2].wait_recv()
            c[6].start()
            c[7].start()
            for k in (3, 4):
                c[k].start()
            c[7].wait_recv()

        @pl.when(i == 2)
        def _():
            c[5].wait_recv()
            c[6].wait_recv()
            c[9].start()
            c[9].wait_recv()

        @pl.when(i == 3)
        def _():
            c[3].wait_recv()
            c[4].wait_recv()
            c[8].start()
            c[8].wait_recv()

    def finish(self):
        for c in self.c:
            c.wait_send()


def plane_masks(masks, i, rows):
    b = lax.axis_index("blk")
    diagonal = i // 2 * (1 - i % 2)
    away = (i + 2) // 3
    out = jnp.zeros((2 * rows, LANES), f32)
    place = lax.broadcasted_iota(jnp.int32, (2 * rows, LANES), 0) // (rows // 2)
    for half, (group, shift) in enumerate(((away, diagonal), (diagonal, away))):
        near = (b + 2 * shift) % 4
        far = near + 1 - 2 * (near % 2)
        out = jnp.where(place == half, masks[group, pl.ds(near, 1), :], out)
        out = jnp.where(place == 2 + half, masks[group, pl.ds(far, 1), :], out)
    return out


def feed_table_copies(rank, share, feed_in_hbm, feed_out_hbm, down_in_hbm, feed_in, feed_out, down_in):
    lanes = pl.ds(pl.multiple_of(rank * share, 128), share)
    return [
        (feed_in_hbm.at[:, 0], feed_in.at[0]),
        (feed_in_hbm.at[:, 1], feed_in.at[1]),
        (feed_out_hbm.at[:, 0, :, lanes], feed_out.at[0]),
        (feed_out_hbm.at[:, 1, :, lanes], feed_out.at[1]),
        (down_in_hbm.at[:, :, lanes], down_in),
    ]


def feed_table_scratch(width, share):
    return [
        pltpu.VMEM((2, ADAPTERS, RANK, width), bf16),
        pltpu.VMEM((2, ADAPTERS, RANK, share), bf16),
        pltpu.VMEM((ADAPTERS, RANK, share), bf16),
    ]


class PlaneReduce:
    COUNT = 10

    def __init__(self, copy, part, odd, from_core, from_x, from_y, diag, rows, first):
        px, py, pc = neighbours()
        h = rows // 2
        self.h = h
        self.rows = rows
        h0, h1 = pl.ds(0, h), pl.ds(h, h)
        self.part, self.from_core = part, from_core
        self.from_x, self.from_y, self.diag = from_x, from_y, diag
        self.core = [
            copy(first + i, odd.at[i % 2], from_core.at[i], pc) for i in range(4)
        ]
        self.d = [
            copy(first + 4, part.at[2, h0], diag.at[h0], px),
            copy(first + 5, part.at[2, h1], diag.at[h1], py),
        ]
        self.e = [
            copy(first + 6, part.at[1, h0], from_x.at[h0], px),
            copy(first + 7, part.at[1, h1], from_y.at[h1], py),
            copy(first + 8, part.at[3, h0], from_x.at[h1], px),
            copy(first + 9, part.at[3, h1], from_y.at[h0], py),
        ]

    def merge(self, i):
        self.core[i].wait_recv()
        add_into(self.part.at[i], self.from_core.at[i], self.rows)

    def before(self, i):
        for k in (2, 3):

            @pl.when(i == k)
            def _(k=k):
                self.core[k - 2].wait_send()

    def after(self, i):
        for k in range(4):

            @pl.when(i == k)
            def _(k=k):
                self.core[k].start()
                if k == 2:
                    self.merge(1)
                    self.e[0].start()
                    self.e[1].start()
                    self.merge(2)
                    self.d[0].start()
                    self.d[1].start()

    def finish(self, write, between=None):
        h, h0, h1 = self.h, pl.ds(0, self.h), pl.ds(self.h, self.h)
        self.merge(3)
        self.d[0].wait_recv()
        add_into(self.part.at[3, h1], self.diag.at[h0], h)
        self.e[3].start()
        self.d[1].wait_recv()
        add_into(self.part.at[3, h0], self.diag.at[h1], h)
        self.e[2].start()
        if between is not None:
            between()
        self.merge(0)
        for e in self.e:
            e.wait_recv()

        @pl.loop(0, self.rows // 32)
        def _(i):
            at = pl.ds(pl.multiple_of(i * 32, 32), 32)
            write(
                at,
                self.part[0, at, :].astype(f32)
                + self.from_x[at, :].astype(f32)
                + self.from_y[at, :].astype(f32),
            )

        for c in self.core[2:] + self.d + self.e:
            c.wait_send()


GELU_SLOPE = 0.7978845608028654
GELU_CUBE = 0.044715


def plane_rank():
    return lax.axis_index("dp") % 2 * 4 + lax.axis_index("blk")


def span(i, size):
    return pl.ds(pl.multiple_of(i * size, size), size)


def woven(gate_hbm, up_hbm, both):
    out = []
    for j in range(gate_hbm.shape[1] // 128):
        for k, ref in enumerate((gate_hbm, up_hbm)):
            out.append(
                (ref.at[:, pl.ds(j * 128, 128)], both.at[:, pl.ds(j * 256 + k * 128, 128)])
            )
    return out


def feed_forward_kernel(
    own, middle, cotangent, gains, masks, down_out, feed_in_hbm, feed_out_hbm, down_in_hbm,
    gate_hbm, up_hbm, down_hbm,
    layer_out, grad_branch, narrow, feed_all, gate_up,
    feed_in, feed_out, down_in, weave, down, land, hidden, saved, part, odd, from_core, from_x, from_y, diag,
    send, recv, load, store,
):
    rows = own.shape[0]
    share = gate_hbm.shape[1]
    width = own.shape[1]
    tile = 256
    loads = [
        pltpu.make_async_copy(s, d, load.at[i])
        for i, (s, d) in enumerate(
            woven(gate_hbm, up_hbm, weave)
            + [(down_hbm, down)]
            + feed_table_copies(
                plane_rank(), share, feed_in_hbm, feed_out_hbm, down_in_hbm, feed_in, feed_out,
                down_in,
            )
        )
    ]
    for c in loads:
        c.start()
    greet(neighbours())
    copy = sender(send, recv)
    gather = PlaneGather(copy, own, land, rows)
    reduce = PlaneReduce(
        copy, part, odd, from_core, from_x, from_y, diag, rows, PlaneGather.COUNT
    )
    gather.begin()
    land[0, :rows, :] = own[...]
    for c in loads:
        c.wait()

    def keep(i):
        slot = i % 2
        return (
            pltpu.make_async_copy(saved.at[slot], gate_up.at[i], store.at[slot]),
            pltpu.make_async_copy(land.at[i], feed_all.at[i], store.at[2 + slot]),
        )

    @pl.loop(0, 4)
    def _(i):
        gather.before(i)
        slot = i % 2

        @pl.when(i >= 2)
        def _():
            for c in keep(i - 2):
                c.wait()

        mask = plane_masks(masks, i, rows)
        for k in range(2):
            narrow[i, k] = (dot_nt(land[i], flat(feed_in[k])) * mask).astype(bf16)

        @pl.loop(0, share // 128)
        def _(n):
            at = span(n, 128)
            pre = dot_nn(land[i], weave[:, span(n, 256)])
            g = pre[:, :128] + dot_nn(narrow[i, 0], flat(feed_out[0, :, :, at]))
            u = pre[:, 128:] + dot_nn(narrow[i, 1], flat(feed_out[1, :, :, at]))
            saved[slot, 0, :, at] = g.astype(bf16)
            saved[slot, 1, :, at] = u.astype(bf16)
            th = jnp.tanh(GELU_SLOPE * (g + GELU_CUBE * g * g * g))
            hidden[:, at] = (0.5 * g * (1.0 + th) * u).astype(bf16)

        for c in keep(i):
            c.start()
        narrow[i, 2] = (dot_nt(hidden[...], flat(down_in[...])) * mask).astype(bf16)
        reduce.before(i)

        @pl.loop(0, width // tile)
        def _(n):
            at = span(n, tile)
            got = dot_nn(hidden[...], down[:, at]) + dot_nn(narrow[i, 2], down_out[:, at])
            got = got.astype(bf16)
            part[i, :, at] = got[:rows]
            odd[i % 2, :, at] = got[rows:]

        reduce.after(i)

    def write(at, branch):
        scale = lax.rsqrt(jnp.mean(branch * branch, axis=-1, keepdims=True) + epsilon)
        gain = gains[3:4, :]
        layer_out[at, :] = (middle[at, :].astype(f32) + branch * scale * gain).astype(bf16)
        grad_branch[at, :] = norm_grad(branch, gain, cotangent[at, :].astype(f32)).astype(bf16)

    reduce.finish(write)
    gather.finish()
    for i in (2, 3):
        for c in keep(i):
            c.wait()


def feed_backward_kernel(
    own, masks, down_out, narrow, feed_in_hbm, feed_out_hbm, down_in_hbm,
    gate_hbm, up_hbm, down_hbm, gate_up, feed_all,
    grad_feed, feed_table, share_sum,
    back, both, t_feed_out, t_down_in, t_down_out, share_table, share_in, share_piece,
    feed_in, feed_out, down_in, weave, down, land, saved, gg, part, odd, from_core, from_x, from_y, diag,
    send, recv, load, fetch,
):
    rows = own.shape[0]
    share = gate_hbm.shape[1]
    width = own.shape[1]
    tile = 256
    loads = [
        pltpu.make_async_copy(s, d, load.at[i])
        for i, (s, d) in enumerate(
            woven(gate_hbm, up_hbm, weave)
            + [(down_hbm, down)]
            + feed_table_copies(
                plane_rank(), share, feed_in_hbm, feed_out_hbm, down_in_hbm, feed_in, feed_out,
                down_in,
            )
        )
    ]

    def bring(i):
        return pltpu.make_async_copy(gate_up.at[i], saved, fetch.at[0])

    for c in loads:
        c.start()
    bring(0).start()
    place = Places()
    greet(list(neighbours()) + [place.up(d) for d in range(1, place.planes)])
    copy = sender(send, recv)
    spread = TableSum(
        place, copy, PlaneGather.COUNT + PlaneReduce.COUNT, share_table, share_in, share_piece,
        lambda z: share_sum.at[z], fetch.at[1],
    )
    gather = PlaneGather(copy, own, land, rows)
    reduce = PlaneReduce(
        copy, part, odd, from_core, from_x, from_y, diag, rows, PlaneGather.COUNT
    )
    gather.begin()
    land[0, :rows, :] = own[...]
    t_feed_out[...] = jnp.zeros_like(t_feed_out)
    t_down_in[...] = jnp.zeros_like(t_down_in)
    t_down_out[...] = jnp.zeros_like(t_down_out)
    for c in loads:
        c.wait()

    @pl.loop(0, 4)
    def _(i):
        gather.before(i)
        bring(i).wait()
        mask = plane_masks(masks, i, rows)
        back[...] = (dot_nt(land[i], down_out[...]) * mask).astype(bf16)

        @pl.loop(0, 2)
        def _(n):
            at = span(n, rows)
            gh = dot_nt(land[i, at, :], down[...]) + dot_nn(back[at, :], flat(down_in[...]))
            g = saved[0, at, :].astype(f32)
            u = saved[1, at, :].astype(f32)
            th = jnp.tanh(GELU_SLOPE * (g + GELU_CUBE * g * g * g))
            gelu = 0.5 * g * (1.0 + th)
            slope = 0.5 * (1.0 + th) + 0.5 * g * (1.0 - th * th) * GELU_SLOPE * (
                1.0 + 3.0 * GELU_CUBE * g * g
            )
            saved[0, at, :] = (gelu * u).astype(bf16)
            left = (gh * u * slope).astype(bf16)
            right = (gh * gelu).astype(bf16)
            for j in range(share // 128):
                lanes = slice(j * 128, (j + 1) * 128)
                gg[at, j * 256 : j * 256 + 128] = left[:, lanes]
                gg[at, j * 256 + 128 : (j + 1) * 256] = right[:, lanes]

        t_down_in[...] += dot_tn(back[...], saved[0])

        @pl.when(i < 3)
        def _():
            bring(i + 1).start()

        for k in range(2):
            low = jnp.zeros((2 * rows, LANES), f32)
            for j in range(share // 128):
                at = j * 256 + k * 128
                low = low + dot_nt(
                    gg[:, at : at + 128], flat(feed_out[k, :, :, j * 128 : (j + 1) * 128])
                )
            both[i, :, k * LANES : (k + 1) * LANES] = (low * mask).astype(bf16)
        reduce.before(i)

        @pl.loop(0, width // tile)
        def _(n):
            at = span(n, tile)
            got = (
                dot_nt(gg[...], weave[at, :])
                + dot_nn(both[i, :, :LANES], flat(feed_in[0, :, :, at]))
                + dot_nn(both[i, :, LANES:], flat(feed_in[1, :, :, at]))
            ).astype(bf16)
            part[i, :, at] = got[:rows]
            odd[i % 2, :, at] = got[rows:]

        reduce.after(i)
        for k in range(2):
            for j in range(share // 128):
                at = j * 256 + k * 128
                t_feed_out[k, :, j * 128 : (j + 1) * 128] += dot_tn(
                    narrow[i, k], gg[:, at : at + 128]
                )
        t_down_out[...] += dot_tn(narrow[i, 2], land[i])

    share_table[: 2 * LANES] = t_feed_out[...].reshape(2 * LANES, share).astype(bf16)
    share_table[2 * LANES :] = t_down_in[...].astype(bf16)
    spread.scatter()
    gather.finish()
    reload = [pltpu.make_async_copy(feed_all.at[i], land.at[i], fetch.at[2 + i]) for i in range(4)]
    for c in reload:
        c.start()

    def tables():
        spread.gather()
        for c in reload:
            c.wait()
        backs = both[...].reshape(8 * rows, 2 * LANES)

        @pl.loop(0, width // 256)
        def _(n):
            at = span(n, 256)
            got = dot_tn(backs, land[:, :, at].reshape(8 * rows, 256)).astype(bf16)
            last = t_down_out[:, at].astype(bf16)
            for a in range(ADAPTERS):
                first = slice(a * RANK, (a + 1) * RANK)
                second = slice(LANES + a * RANK, LANES + (a + 1) * RANK)
                feed_table[a, :RANK, at] = got[first]
                feed_table[a, RANK : 2 * RANK, at] = got[second]
                feed_table[a, 2 * RANK :, at] = last[first]

    def write(at, total):
        grad_feed[at, :] = total.astype(grad_feed.dtype)

    reduce.finish(write, tables)
    spread.finish()


def feed_scratch(rows, width, extra=0):
    count = PlaneGather.COUNT + PlaneReduce.COUNT + extra
    return [
        pltpu.VMEM((4, rows, width), bf16),
        pltpu.VMEM((2, rows, width), bf16),
        pltpu.VMEM((4, rows, width), bf16),
        pltpu.VMEM((rows, width), bf16),
        pltpu.VMEM((rows, width), bf16),
        pltpu.VMEM((rows, width), bf16),
        pltpu.SemaphoreType.DMA((count,)),
        pltpu.SemaphoreType.DMA((count,)),
    ]


ANY = pl.BlockSpec(memory_space=pl.ANY)


def feed_forward(own, middle, cotangent, gains, masks, down_out, tables, gate, up, down):
    rows, width = own.shape
    share = gate.shape[1]
    return pl.pallas_call(
        feed_forward_kernel,
        out_shape=(
            shape((rows, width), bf16),
            shape((rows, width), bf16),
            shape((4, 3, 2 * rows, LANES), bf16),
            shape((4, 2 * rows, width), bf16),
            shape((4, 2, 2 * rows, share), bf16),
        ),
        in_specs=[VM] * 6 + [ANY] * 6,
        out_specs=(VM, VM, VM, ANY, ANY),
        scratch_shapes=feed_table_scratch(width, share)
        + [
            pltpu.VMEM((width, 2 * share), bf16),
            pltpu.VMEM(down.shape, bf16),
            pltpu.VMEM((4, 2 * rows, width), bf16),
            pltpu.VMEM((2 * rows, share), bf16),
            pltpu.VMEM((2, 2, 2 * rows, share), bf16),
        ]
        + feed_scratch(rows, width)
        + [pltpu.SemaphoreType.DMA((6 + share // 64,)), pltpu.SemaphoreType.DMA((4,))],
        compiler_params=pltpu.CompilerParams(
            collective_id=1, has_side_effects=True, vmem_limit_bytes=62 << 20
        ),
        name="feed_forward",
    )(own, middle, cotangent, gains, masks, down_out, *tables, gate, up, down)


def feed_backward(own, masks, down_out, narrow, tables, gate, up, down, gate_up, feed_all):
    rows, width = own.shape
    share = gate.shape[1]
    planes = lax.axis_size("ulysses")
    piece = 3 * LANES // planes
    return pl.pallas_call(
        feed_backward_kernel,
        out_shape=(
            shape((rows, width), bf16),
            shape((ADAPTERS, 3 * RANK, width), bf16),
            shape((planes, piece, share), bf16),
        ),
        in_specs=[VM] * 4 + [ANY] * 8,
        out_specs=(VM, VM, ANY),
        scratch_shapes=[
            pltpu.VMEM((2 * rows, LANES), bf16),
            pltpu.VMEM((4, 2 * rows, 2 * LANES), bf16),
            pltpu.VMEM((2, LANES, share), f32),
            pltpu.VMEM((LANES, share), f32),
            pltpu.VMEM((LANES, width), f32),
            pltpu.VMEM((3 * LANES, share), bf16),
            pltpu.VMEM((planes - 1, piece, share), bf16),
            pltpu.VMEM((piece, share), bf16),
        ]
        + feed_table_scratch(width, share)
        + [
            pltpu.VMEM((width, 2 * share), bf16),
            pltpu.VMEM(down.shape, bf16),
            pltpu.VMEM((4, 2 * rows, width), bf16),
            pltpu.VMEM((2, 2 * rows, share), bf16),
            pltpu.VMEM((2 * rows, 2 * share), bf16),
        ]
        + feed_scratch(rows, width, TableSum.COUNT)
        + [pltpu.SemaphoreType.DMA((6 + share // 64,)), pltpu.SemaphoreType.DMA((6,))],
        compiler_params=pltpu.CompilerParams(
            collective_id=2, has_side_effects=True, vmem_limit_bytes=62 << 20
        ),
        name="feed_backward",
    )(own, masks, down_out, narrow, *tables, gate, up, down, gate_up, feed_all)


def flat(table):
    return table.reshape(LANES, table.shape[-1])


def head_table_copies(
    b, heads_hbm, query_out_hbm, kv_out_hbm, heads_in, query_out, key_out, value_out
):
    lanes = pl.ds(pl.multiple_of(b * 2 * HEAD, 128), 2 * HEAD)
    lane = pl.ds(pl.multiple_of(b * HEAD, 128), HEAD)
    return [(heads_hbm.at[:, i], heads_in.at[i]) for i in range(3)] + [
        (query_out_hbm.at[:, :, lanes], query_out),
        (kv_out_hbm.at[:, 0, :, lane], key_out),
        (kv_out_hbm.at[:, 1, :, lane], value_out),
    ]


def head_table_scratch(width):
    return [
        pltpu.VMEM((3, ADAPTERS, RANK, width), bf16),
        pltpu.VMEM((ADAPTERS, RANK, 2 * HEAD), bf16),
        pltpu.VMEM((ADAPTERS, RANK, HEAD), bf16),
        pltpu.VMEM((ADAPTERS, RANK, HEAD), bf16),
    ]


def adapter_mask(ids, t, z, planes, rows):
    sequence = 0 if t * planes * rows < PROMPT else 1 + ((t * planes + z) * rows - PROMPT) // CONT
    owner = lax.broadcasted_iota(jnp.int32, (1, LANES), 1) // RANK
    return jnp.where(owner == ids[0, sequence], 1.0, 0.0)


def rms_rows(source, gains, which, target, rows, add=None):
    gain = gains.at[pl.ds(which, 1)]

    @pl.loop(0, rows // 32)
    def _(i):
        at = span(i, 32)
        v = source[at, :].astype(f32)
        out = v * lax.rsqrt(jnp.mean(v * v, axis=-1, keepdims=True) + epsilon) * gain[...]
        if add is not None:
            out = out + add[at, :].astype(f32)
        target[at, :] = out.astype(target.dtype)


def attention_forward_kernel(
    tokens, gains, ids, mix_in, mix_out, heads_hbm, query_out_hbm, kv_out_hbm,
    query_hbm, key_hbm, value_hbm, out_hbm, gate_hbm, up_hbm,
    queries, values_prompt, values_cont, attended, sums, narrow, mixed_out, narrow_mix,
    attn_out_out, middle_out, normed_feed, cosine, sine, masks_out, normed_out, wall_out, out_out, gate_share,
    up_share,
    heads_in, query_out, key_out, value_out, masks, masks_got, attn_out, middle,
    normed_all, wall, wo, kvp, kvc, acc, total, mixed, send, recv, local,
):
    rows, width = tokens.shape
    dp, b, z = lax.axis_index("dp"), lax.axis_index("blk"), lax.axis_index("ulysses")
    planes = lax.axis_size("ulysses")
    x, y, c = dp % 2, b // 2, b % 2
    base = dp - x
    rank = x * 4 + b
    b_c, b_y = b + 1 - 2 * c, (b + 2) % 4
    b_yc = (b_c + 2) % 4
    pc, py, pyc = (dp, b_c, z), (dp, b_y, z), (dp, b_yc, z)
    other = base + 1 - x
    px, pxc, pxy, pxyc = (other, b, z), (other, b_c, z), (other, b_y, z), (other, b_yc, z)
    pz = (dp, b, z + 1 - 2 * (z % 2))
    left, right = (dp, b, z - 1), (dp, b, z + 1)
    depth = query_hbm.shape[0]
    share = gate_share.shape[1]
    part = out_hbm.shape[0]
    copy = sender(send, recv)

    def block(i):
        return span(i, rows)

    def weight_rows(i):
        return pl.ds(pl.multiple_of(i * depth, 16), depth)

    def out_rows(i):
        return span(i, part)

    heads = ((query_hbm, 2 * HEAD, 0), (key_hbm, HEAD, 2 * HEAD), (value_hbm, HEAD, 3 * HEAD))

    def columns_of(ref, target, size):
        return ref.at[:, pl.ds(pl.multiple_of(target * size, 128), size)]

    own_loads = [
        pltpu.make_async_copy(
            columns_of(ref, b, size), wall.at[weight_rows(rank), pl.ds(to, size)], local.at[i]
        )
        for i, (ref, size, to) in enumerate(heads)
    ]
    own_loads.append(pltpu.make_async_copy(out_hbm, wo.at[out_rows(rank)], local.at[3]))
    table_loads = [
        pltpu.make_async_copy(src, dst, local.at[12 + i])
        for i, (src, dst) in enumerate(
            head_table_copies(
                b, heads_hbm, query_out_hbm, kv_out_hbm, heads_in, query_out, key_out, value_out
            )
        )
    ]
    own_rows = [
        pltpu.make_async_copy(
            columns_of(ref, rank, share), out.at[weight_rows(rank)], local.at[4 + i]
        )
        for i, (ref, out) in enumerate(((gate_hbm, gate_share), (up_hbm, up_share)))
    ]
    for cp in own_loads + table_loads:
        cp.start()

    barrier = pltpu.get_barrier_semaphore()
    for peer in (pc, py, pyc, px, pxc, pxy, pxyc) + tuple(
        (dp, b, (z + d) % planes) for d in range(1, planes)
    ):
        pl.semaphore_signal(barrier, inc=1, device_id=peer, device_id_type=MESH)

    rms_rows(tokens, gains, 0, normed_all.at[block(b)], rows)
    masks[...] = jnp.zeros_like(masks)
    for t in range(4):
        masks[t : t + 1, :] = adapter_mask(ids, t, z, planes, rows)
    masks_out[0] = masks[...]
    pl.semaphore_wait(barrier, 6 + planes)

    stage = []
    for j, (peer, pb) in enumerate(((py, b_y), (pyc, b_yc), (pc, b_c))):
        for i, (ref, size, to) in enumerate(heads):
            stage.append(
                copy(
                    3 + 3 * j + i,
                    columns_of(ref, pb, size),
                    wall.at[weight_rows(rank), pl.ds(to, size)],
                    peer,
                )
            )
    token_copies = [
        copy(0, normed_all.at[block(b)], normed_all.at[block(b)], py),
        copy(1, normed_all.at[block(b)], normed_all.at[block(b)], pc),
        copy(2, normed_all.at[block(b_y)], normed_all.at[block(b_y)], pc),
    ]
    across = [
        copy(12 + i, wall.at[weight_rows(x * 4 + o)], wall.at[weight_rows(x * 4 + o)], px)
        for i, o in enumerate((b, b_c, b_y, b_yc))
    ]
    for cp in stage[:3]:
        cp.start()
    for cp in stage[3:]:
        cp.start()
    token_copies[1].start()
    mask_copy = copy(34, masks, masks_got, px)
    mask_copy.start()
    for cp in own_loads[:3]:
        cp.wait()
    across[0].start()
    lane = lax.broadcasted_iota(jnp.int32, (rows, HEAD // 2), 1).astype(f32)
    inverse = jnp.exp(lane * (-2.0 / HEAD * math.log(rope_base)))

    @pl.loop(0, 4)
    def _(t):
        at = block(t)
        token = (t * planes + z) * rows + lax.broadcasted_iota(jnp.int32, (rows, HEAD // 2), 0)
        position = jnp.where(token >= PROMPT, PROMPT + (token - PROMPT) % CONT, token)
        angle = position.astype(f32) * inverse
        cosine[at, :] = jnp.cos(angle)
        sine[at, :] = jnp.sin(angle)

    for cp in stage[6:]:
        cp.wait_recv()
    across[1].start()
    for cp in stage[:3]:
        cp.wait_recv()
    token_copies[0].start()
    across[2].start()
    for cp in stage[3:6]:
        cp.wait_recv()
    across[3].start()
    token_copies[0].wait_recv()
    token_copies[2].start()
    for cp in table_loads:
        cp.wait()
    mask_copy.wait()
    masks_out[1] = masks_got[...]

    half = part // 2
    rx, ry, rxy = (1 - x) * 4 + b, x * 4 + b_y, (1 - x) * 4 + b_y

    def wo_part(r, h):
        return wo.at[pl.ds(pl.multiple_of(r * part + h * half, 16), half)]

    wo_first = [
        (16, wo_part(rank, 0), px),
        (17, wo_part(rank, 1), py),
        (18, wo_part(rank, 1), px),
        (19, wo_part(rank, 0), py),
        (20, wo.at[out_rows(rank)], pc),
    ]
    wo_next = [
        (21, wo_part(rx, 0), py),
        (22, wo_part(ry, 1), px),
        (23, wo.at[out_rows(rx)], pc),
        (24, wo.at[out_rows(ry)], pc),
        (25, wo.at[out_rows(rxy)], pc),
    ]
    wo_first = [copy(i, ref, ref, peer) for i, ref, peer in wo_first]
    wo_next = [copy(i, ref, ref, peer) for i, ref, peer in wo_next]
    swaps = [
        copy(26 + i, columns_of(ref, x * 4 + b_c, share), out.at[weight_rows(rank)], pc)
        for i, (ref, out) in enumerate(((gate_hbm, gate_share), (up_hbm, up_share)))
    ]
    chips = (
        ((px, rx), (pxc, (1 - x) * 4 + b_c)),
        ((py, ry), (pyc, x * 4 + b_yc)),
        ((pxy, rxy), (pxyc, (1 - x) * 4 + b_yc)),
    )
    got_ranks = (
        (1 - x) * 4 + y * 2 + z % 2, x * 4 + (1 - y) * 2 + z % 2, (1 - x) * 4 + (1 - y) * 2 + z % 2,
    )
    direct, relay, whole = {}, {}, []
    for n, targets in enumerate(chips):
        for i, (ref, out) in enumerate(((gate_hbm, gate_share), (up_hbm, up_share))):
            kind = 2 * n + i
            if kind in (0, 2):
                whole += [
                    copy(63 + kind + j, columns_of(ref, pr, share), out.at[weight_rows(rank)], peer)
                    for j, (peer, pr) in enumerate(targets)
                ]
                continue
            direct[kind] = [
                pltpu.make_async_remote_copy(
                    columns_of(ref, pr, share),
                    out.at[weight_rows(rank)],
                    send.at[51 + 2 * kind + j],
                    recv.at[51 + kind],
                    device_id=peer,
                    device_id_type=MESH,
                )
                for j, (peer, pr) in enumerate(targets)
            ]
            got = out.at[weight_rows(got_ranks[n])]
            relay[kind] = copy(28 + kind, got, got, pz)

    def send_direct(kinds):
        @pl.when(c == z % 2)
        def _():
            for kind in kinds:
                for cp in direct[kind]:
                    cp.start()

    def pass_along(kinds):
        for kind in kinds:
            direct[kind][0].wait_recv()
            relay[kind].start()

    own_loads[3].wait()
    for cp in across:
        cp.wait_recv()
    for cp in wo_first:
        cp.start()
    send_direct((4, 5))
    for cp in swaps + own_rows:
        cp.start()
    token_copies[1].wait_recv()
    token_copies[2].wait_recv()

    outs = [
        pltpu.make_async_copy(normed_all, normed_out, local.at[6]),
        pltpu.make_async_copy(wall, wall_out, local.at[7]),
        pltpu.make_async_copy(wo, out_out, local.at[8]),
        pltpu.make_async_copy(kvp, values_prompt, local.at[9]),
        pltpu.make_async_copy(kvc, values_cont, local.at[10]),
        pltpu.make_async_copy(mixed, mixed_out, local.at[11]),
    ]
    outs[0].start()
    outs[1].start()

    half_head = HEAD // 2

    def turned(pre, at, scale):
        cos, sin = cosine[at, :], sine[at, :]
        first, second = pre[:, :half_head], pre[:, half_head:]
        one, two = first * cos - second * sin, second * cos + first * sin
        if scale != 1.0:
            one, two = one * scale, two * scale
        return jnp.concatenate([one, two], axis=1).astype(bf16)

    def keys_values(p):
        at = pl.ds(2 * p * rows, 2 * rows)
        first = lax.broadcasted_iota(jnp.int32, (2 * rows, 3 * LANES), 0) < rows
        both = [jnp.concatenate([masks[pl.ds(2 * p + k, 1), :]] * 3, axis=1) for k in range(2)]
        mask = jnp.where(first, both[0], both[1])
        low = dot_nt(normed_all[at, :], heads_in[...].reshape(3 * LANES, width))
        narrow[at, :] = (low * mask).astype(bf16)
        pre = dot_nn(normed_all[at, :], wall[:, 2 * HEAD : 3 * HEAD]) + dot_nn(
            narrow[at, LANES : 2 * LANES], flat(key_out[...])
        )
        key = turned(pre, at, 1.0)
        value = (
            dot_nn(normed_all[at, :], wall[:, 3 * HEAD :])
            + dot_nn(narrow[at, 2 * LANES :], flat(value_out[...]))
        ).astype(bf16)
        for k in range(2):
            part_rows = slice(k * rows, (k + 1) * rows)
            if p == 0:
                kvp[z, 0, k] = key[part_rows]
                kvp[z, 1, k] = value[part_rows]
            else:
                kvc[0, k] = key[part_rows]
                kvc[1, k] = value[part_rows]

    keys_values(0)
    def hop(direction, d):
        index = 42 + d if direction > 0 else 45 + d
        zz = z - d * direction
        return copy(index, kvp.at[zz], kvp.at[zz], right if direction > 0 else left)

    def pass_on(direction, d):
        reach = z < planes - 1 if direction > 0 else z > 0

        @pl.when(reach)
        def _():
            hop(direction, d).start()

    pass_on(1, 0)
    pass_on(-1, 0)
    keys_values(1)

    @pl.loop(0, 2)
    def _(p):
        at = span(p, 2 * rows)
        for h in range(2):
            lanes = slice(h * HEAD, (h + 1) * HEAD)
            pre = dot_nn(normed_all[at, :], wall[:, lanes]) + dot_nn(
                narrow[at, :LANES], flat(query_out[:, :, lanes])
            )
            got = turned(pre, at, HEAD ** (-0.5))
            for k in range(2):
                queries[2 * p + k, h * rows : (h + 1) * rows, :] = got[k * rows : (k + 1) * rows]

    send_direct((1, 3))
    acc[...] = jnp.zeros_like(acc)
    total[...] = jnp.zeros_like(total)
    row = lax.broadcasted_iota(jnp.int32, (2 * rows, rows), 0) % rows
    causal = lax.broadcasted_iota(jnp.int32, (2 * rows, rows), 1) <= row

    def step(t, k, v, masked):
        e = jnp.exp(soft_cap * jnp.tanh(dot_nt(queries[t], k) * (1.0 / soft_cap)))
        if masked:
            e = jnp.where(causal, e, 0.0)
        some = e[:, :128]
        for n in range(128, rows, 128):
            some = some + e[:, n : n + 128]
        total[t] += some
        acc[t] += dot_nn(e.astype(bf16), v)

    step(0, kvp[z, 0, 0], kvp[z, 1, 0], True)
    step(1, kvp[z, 0, 0], kvp[z, 1, 0], False)
    step(1, kvp[z, 0, 1], kvp[z, 1, 1], True)

    @pl.loop(2, 4)
    def _(t):
        step(t, kvc[0, t - 2], kvc[1, t - 2], True)
        step(t, kvp[z, 0, 0], kvp[z, 1, 0], False)
        step(t, kvp[z, 0, 1], kvp[z, 1, 1], False)

    wo_first[0].wait_recv()
    wo_next[0].start()
    wo_first[1].wait_recv()
    wo_next[1].start()

    @pl.loop(0, 2 * (planes - 1))
    def _(i):
        d = i // 2 + 1
        direction = 1 - 2 * (i % 2)
        zz = z - d * direction

        @pl.when((zz >= 0) & (zz < planes))
        def _():
            index = 42 + 3 * (i % 2) + d - 1
            here = pltpu.make_async_remote_copy(
                kvp.at[zz], kvp.at[zz], send.at[index], recv.at[index], device_id=left,
                device_id_type=MESH,
            )
            here.wait_recv()

            @pl.when((i % 2 == 0) & (z < planes - 1))
            def _():
                pltpu.make_async_remote_copy(
                    kvp.at[zz], kvp.at[zz], send.at[index + 1], recv.at[index + 1],
                    device_id=right, device_id_type=MESH,
                ).start()

            @pl.when((i % 2 == 1) & (z > 0))
            def _():
                pltpu.make_async_remote_copy(
                    kvp.at[zz], kvp.at[zz], send.at[index + 1], recv.at[index + 1],
                    device_id=left, device_id_type=MESH,
                ).start()

            step(1, kvp[zz, 0, 0], kvp[zz, 1, 0], False)

            @pl.when(zz < z)
            def _():
                step(0, kvp[zz, 0, 0], kvp[zz, 1, 0], False)
                step(1, kvp[zz, 0, 1], kvp[zz, 1, 1], False)

            @pl.loop(2, 4)
            def _(t):
                step(t, kvp[zz, 0, 0], kvp[zz, 1, 0], False)
                step(t, kvp[zz, 0, 1], kvp[zz, 1, 1], False)

    outs[3].start()
    outs[4].start()
    ones = jnp.ones((8, 128), f32)

    @pl.loop(0, 4)
    def _(t):
        whole = jnp.sum(total[t], axis=1, keepdims=True)
        got = (acc[t] / whole).astype(bf16)
        attended[t, :, :HEAD] = got[:rows]
        attended[t, :, HEAD:] = got[rows:]
        sums[t] = lax.dot_general(
            ones, total[t], (((1,), (1,)), ((), ())), precision=lax.Precision.HIGHEST,
            preferred_element_type=f32,
        )

    lanes = pl.ds(pl.multiple_of(b * 2 * HEAD, 128), 2 * HEAD)
    mixes = [
        copy(48 + i, attended.at[o], mixed.at[:, lanes], peer)
        for i, (peer, o) in enumerate(((py, b_y), (pyc, b_yc), (pc, b_c)))
    ]
    for cp in mixes:
        cp.start()
    for cp in whole:
        cp.start()
    mixed[:, lanes] = attended[b]
    pass_along((4, 5))
    pass_along((1, 3))
    wo_first[2].wait_recv()
    wo_next[2].start()
    wo_first[3].wait_recv()
    wo_next[3].start()
    wo_next[0].wait_recv()
    wo_next[1].wait_recv()
    wo_next[4].start()
    wo_first[4].wait_recv()
    for cp in wo_next[2:]:
        cp.wait_recv()
    for cp in mixes:
        cp.wait_recv()
    outs[2].start()
    outs[5].start()
    narrow_mix[...] = (dot_nt(mixed[...], mix_in[...]) * masks[pl.ds(b, 1), :]).astype(bf16)

    @pl.loop(0, width // 384)
    def _(n):
        at = span(n, 384)
        attn_out[:, at] = dot_nn(mixed[...], wo[:, at]) + dot_nn(narrow_mix[...], mix_out[:, at])

    rms_rows(attn_out, gains, 1, middle, rows, add=tokens)
    rms_rows(middle, gains, 2, normed_feed, rows)
    attn_out_out[...] = attn_out[...].astype(bf16)
    middle_out[...] = middle[...].astype(bf16)

    for cp in swaps + whole:
        cp.wait()
    for cp in relay.values():
        cp.wait()

    @pl.when(c == z % 2)
    def _():
        for pair in direct.values():
            for cp in pair:
                cp.wait_send()

    for cp in own_rows + outs:
        cp.wait()
    for cp in stage + token_copies + across + wo_first + wo_next + mixes:
        cp.wait_send()

    @pl.loop(0, 2 * (planes - 1))
    def _(i):
        d = i // 2
        direction = 1 - 2 * (i % 2)
        zz = z - d * direction
        onward = z + direction

        @pl.when((zz >= 0) & (zz < planes) & (onward >= 0) & (onward < planes))
        def _():
            index = 42 + 3 * (i % 2) + d
            pltpu.make_async_remote_copy(
                kvp.at[zz], kvp.at[zz], send.at[index], recv.at[index], device_id=left,
                device_id_type=MESH,
            ).wait_send()


def attention_forward(tokens, gains, ids, mix_in, mix_out, tables, weights, share):
    rows, width = tokens.shape
    planes = lax.axis_size("ulysses")
    return pl.pallas_call(
        attention_forward_kernel,
        out_shape=(
            shape((4, 2 * rows, HEAD), bf16),
            shape((planes, 2, 2, rows, HEAD), bf16),
            shape((2, 2, rows, HEAD), bf16),
            shape((4, rows, 2 * HEAD), bf16),
            shape((4, 8, 2 * rows), f32),
            shape((4 * rows, 3 * LANES), bf16),
            shape((rows, 8 * HEAD), bf16),
            shape((rows, LANES), bf16),
            shape((rows, width), bf16),
            shape((rows, width), bf16),
            shape((rows, width), bf16),
            shape((4 * rows, HEAD // 2), f32),
            shape((4 * rows, HEAD // 2), f32),
            shape((2, 16, LANES), f32),
            shape((4 * rows, width), bf16),
            shape((width, 4 * HEAD), bf16),
            shape((8 * HEAD, width), bf16),
            shape((width, share), bf16),
            shape((width, share), bf16),
        ),
        in_specs=[VM, VM, pl.BlockSpec(memory_space=pltpu.SMEM), VM, VM] + [ANY] * 9,
        out_specs=(VM, ANY, ANY, VM, VM, VM, ANY) + (VM,) * 7 + (ANY,) * 5,
        scratch_shapes=head_table_scratch(width)
        + [
            pltpu.VMEM((16, LANES), f32),
            pltpu.VMEM((16, LANES), f32),
            pltpu.VMEM((rows, width), f32),
            pltpu.VMEM((rows, width), f32),
            pltpu.VMEM((4 * rows, width), bf16),
            pltpu.VMEM((width, 4 * HEAD), bf16),
            pltpu.VMEM((8 * HEAD, width), bf16),
            pltpu.VMEM((planes, 2, 2, rows, HEAD), bf16),
            pltpu.VMEM((2, 2, rows, HEAD), bf16),
            pltpu.VMEM((4, 2 * rows, HEAD), f32),
            pltpu.VMEM((4, 2 * rows, 128), f32),
            pltpu.VMEM((rows, 8 * HEAD), bf16),
            pltpu.SemaphoreType.DMA((67,)),
            pltpu.SemaphoreType.DMA((67,)),
            pltpu.SemaphoreType.DMA((18,)),
        ],
        compiler_params=pltpu.CompilerParams(
            collective_id=3, has_side_effects=True, vmem_limit_bytes=62 << 20
        ),
        name="attention_forward",
    )(tokens, gains, ids, mix_in, mix_out, *tables, *weights)


class Places:
    def __init__(self):
        dp, b, z = lax.axis_index("dp"), lax.axis_index("blk"), lax.axis_index("ulysses")
        self.b, self.z, self.planes = b, z, lax.axis_size("ulysses")
        x, c = dp % 2, b % 2
        self.x, self.y, self.c = x, b // 2, c
        self.b_c, self.b_y = b + 1 - 2 * c, (b + 2) % 4
        self.b_yc = (self.b_c + 2) % 4
        other = dp + 1 - 2 * x
        self.dp, self.other = dp, other
        self.pc, self.py, self.pyc = (dp, self.b_c, z), (dp, self.b_y, z), (dp, self.b_yc, z)
        self.px = (other, b, z)
        self.plane = (
            self.pc, self.py, self.pyc, self.px,
            (other, self.b_c, z), (other, self.b_y, z), (other, self.b_yc, z),
        )
        self.rank = x * 4 + b
        self.near = (x * 4 + b, (1 - x) * 4 + b, (1 - x) * 4 + self.b_y, x * 4 + self.b_y)
        self.far = (x * 4 + self.b_c, (1 - x) * 4 + self.b_c, (1 - x) * 4 + self.b_yc, x * 4 + self.b_yc)

    def along(self, d):
        return (self.z + d) % self.planes

    def up(self, d):
        return (self.dp, self.b, self.along(d))


class TableSum:
    COUNT = 6

    def __init__(self, place, copy, first, source, arrived, piece, target, local):
        self.place, self.source, self.arrived, self.piece = place, source, arrived, piece
        n = place.planes
        self.q = piece.shape[0]
        self.out = [
            copy(first + d - 1, source.at[span(place.along(d), self.q)], arrived.at[d - 1], place.up(d))
            for d in range(1, n)
        ]
        self.own = pltpu.make_async_copy(piece, target(place.z), local)
        self.back = [
            copy(first + 2 + d, piece, target(place.z), place.up(d)) for d in range(1, n)
        ]

    def scatter(self):
        for c in self.out:
            c.start()

    def gather(self):
        for c in self.out:
            c.wait_recv()
        got = self.source[span(self.place.z, self.q), :].astype(f32)
        for i in range(self.place.planes - 1):
            got = got + self.arrived[i].astype(f32)
        self.piece[...] = got.astype(bf16)
        self.own.start()
        for c in self.back:
            c.start()

    def ready(self):
        for c in self.back:
            c.wait_recv()
        self.own.wait()

    def finish(self):
        self.ready()
        self.close()

    def close(self):
        for c in self.out + self.back:
            c.wait_send()


class PlaneSpread:
    COUNT = 10

    def __init__(self, place, copy, first, own, gathered):
        half = place.planes // 2
        parts = (pl.ds(0, half), pl.ds(half, half))
        mine, rx, rxy, ry = place.near
        px, py, pc = place.px, place.py, place.pc

        def same(i, ref, peer):
            return copy(first + i, ref, ref, peer)

        def send(i, part, peer):
            return copy(first + i, own.at[part], gathered.at[mine, part], peer)

        self.first = [
            send(0, parts[0], px),
            send(1, parts[1], py),
            send(2, parts[1], px),
            send(3, parts[0], py),
            copy(first + 4, own, gathered.at[mine], pc),
        ]
        self.next = [
            same(5, gathered.at[rx, parts[0]], py),
            same(6, gathered.at[ry, parts[1]], px),
            same(7, gathered.at[rx], pc),
            same(8, gathered.at[ry], pc),
            same(9, gathered.at[rxy], pc),
        ]

    def plane(self):
        for c in self.first:
            c.start()

    def forward(self):
        for i in range(4):
            self.first[i].wait_recv()
            self.next[i].start()

    def corner(self):
        self.next[0].wait_recv()
        self.next[1].wait_recv()
        self.next[4].start()

    def finish(self):
        self.first[4].wait_recv()
        for c in self.next[2:]:
            c.wait_recv()
        for c in self.first + self.next:
            c.wait_send()


class TableSpread:
    COUNT = TableSum.COUNT + PlaneSpread.COUNT

    def __init__(self, place, copy, first, source, arrived, piece, gathered, local):
        own = gathered.at[place.rank]
        self.sum = TableSum(
            place, copy, first, source, arrived, piece, lambda z: gathered.at[place.rank, z], local
        )
        self.spread = PlaneSpread(place, copy, first + TableSum.COUNT, own, gathered)
        self.scatter, self.gather = self.sum.scatter, self.sum.gather
        self.forward, self.corner = self.spread.forward, self.spread.corner

    def plane(self):
        self.sum.ready()
        self.spread.plane()

    def finish(self):
        self.sum.close()
        self.spread.finish()


class TableReduce:
    COUNT = 10

    def __init__(self, place, copy, first, table, part, from_core, from_x, from_y, diag, total, local):
        self.part, self.from_core, self.from_x, self.from_y = part, from_core, from_x, from_y
        self.diag, self.total = diag, total
        m = total.shape[0]
        self.m, self.h = m, m // 2
        h0, h1 = pl.ds(0, self.h), pl.ds(self.h, self.h)
        self.h0, self.h1 = h0, h1
        self.core = [
            copy(first + i, table.at[place.far[i]], from_core.at[i], place.pc) for i in range(4)
        ]
        self.load = [
            pltpu.make_async_copy(table.at[place.near[i]], part.at[i], local(i)) for i in range(4)
        ]
        self.d = [
            copy(first + 4, part.at[2, h0], diag.at[h0], place.px),
            copy(first + 5, part.at[2, h1], diag.at[h1], place.py),
        ]
        self.e = [
            copy(first + 6, part.at[1, h0], from_x.at[h0], place.px),
            copy(first + 7, part.at[3, h1], from_y.at[h1], place.py),
            copy(first + 8, part.at[1, h1], from_x.at[h1], place.px),
            copy(first + 9, part.at[3, h0], from_y.at[h0], place.py),
        ]

    def begin(self):
        for c in self.core + self.load:
            c.start()

    def merge(self):
        for i in (2, 1, 3, 0):
            self.load[i].wait()
            self.core[i].wait_recv()
            add_into(self.part.at[i], self.from_core.at[i], self.m, 16)
            if i == 2:
                self.d[0].start()
                self.d[1].start()
        self.e[0].start()
        self.e[1].start()

    def corner(self):
        self.d[0].wait_recv()
        add_into(self.part.at[3, self.h0], self.diag.at[self.h0], self.h, 16)
        self.e[3].start()
        self.d[1].wait_recv()
        add_into(self.part.at[1, self.h1], self.diag.at[self.h1], self.h, 16)
        self.e[2].start()

    def finish(self):
        for e in self.e:
            e.wait_recv()

        @pl.loop(0, self.m // 16)
        def _(i):
            at = span(i, 16)
            self.total[at, :] = (
                self.part[0, at, :].astype(f32)
                + self.from_x[at, :].astype(f32)
                + self.from_y[at, :].astype(f32)
            ).astype(bf16)

        for c in self.core + self.d + self.e:
            c.wait_send()


def attention_backward_kernel(
    middle, attn_out, cotangent, gains, masks, mixed, narrow_mix, mix_in, mix_out,
    queries, kvp, kvc, attended, sums, narrow, cosine, sine,
    grad_feed_hbm, tokens_hbm, heads_hbm, query_out_hbm, kv_out_hbm, out_hbm, normed_hbm, wall_hbm, feed_hbm, feed_share,
    tokens_grad, g_feed_table, g_feed_share, g_head_table, g_head_share,
    heads_in, query_out, key_out, value_out, wo, wall, grad_attn, grad_mixed,
    g, delta, inv, dq, kv_own, kv_far, kv_send, kv_got, grad_pre, back,
    from_core, from_y,
    feed_table, a_part, a_core, a_x, a_y, a_diag, a_total, a_in, a_piece,
    h_table, h_part, h_core, h_x, h_y, h_diag, h_total, h_in, h_piece,
    o_table, o_got, o_total, o_in, o_piece,
    send, recv, local,
):
    rows, width = tokens_grad.shape
    place = Places()
    b, z, planes = place.b, place.z, place.planes
    copy = sender(send, recv)
    normed_all = wo.at[pl.ds(0, 4 * rows)]
    part = [wo.at[pl.ds((4 + i) * rows, rows)] for i in range(4)]
    own_share = pltpu.make_async_copy(feed_share, g_feed_share.at[place.rank], local.at[0])
    loads = [
        pltpu.make_async_copy(src, dst, local.at[14 + i])
        for i, (src, dst) in enumerate(
            [(out_hbm, wo)]
            + head_table_copies(
                b, heads_hbm, query_out_hbm, kv_out_hbm, heads_in, query_out, key_out, value_out
            )
            + [(wall_hbm, wall), (feed_hbm, feed_table.at[:, pl.ds(0, 3 * RANK)])]
        )
    ]
    grad_feed = from_y
    bring_feed = pltpu.make_async_copy(grad_feed_hbm, grad_feed, local.at[24])
    bring_feed.start()
    late = pltpu.make_async_copy(normed_hbm, normed_all, local.at[1])
    for c in loads:
        c.start()
    own_share.start()
    barrier = pltpu.get_barrier_semaphore()
    peers = list(place.plane) + [place.up(d) for d in range(1, planes)]
    for peer in peers:
        pl.semaphore_signal(barrier, inc=1, device_id=peer, device_id_type=MESH)
    pl.semaphore_wait(barrier, len(peers))

    swaps = []
    for j, (peer, pb) in enumerate(
        ((place.py, place.b_y), (place.pyc, place.b_yc), (place.pc, place.b_c))
    ):
        for h in range(2):
            lanes = pl.ds(pl.multiple_of(pb * 2 * HEAD + h * HEAD, 128), HEAD)
            swaps.append(
                copy(
                    2 * j + h,
                    grad_mixed.at[:, lanes],
                    g.at[b, pl.ds(h * rows, rows)],
                    peer,
                )
            )
    at = 12
    feed_reduce = TableReduce(
        place, copy, at, feed_table, a_part, a_core, a_x, a_y, a_diag, a_total,
        lambda i: local.at[2 + i],
    )
    at += TableReduce.COUNT
    feed_spread = TableSpread(place, copy, at, a_total, a_in, a_piece, g_feed_table, local.at[6])
    at += TableSpread.COUNT
    share_spread = PlaneSpread(place, copy, at, feed_share, g_feed_share)
    at += PlaneSpread.COUNT
    head_reduce = TableReduce(
        place, copy, at, h_table, h_part, h_core, h_x, h_y, h_diag, h_total,
        lambda i: local.at[8 + i],
    )
    at += TableReduce.COUNT
    head_spread = TableSpread(place, copy, at, h_total, h_in, h_piece, g_head_table, local.at[12])
    at += TableSpread.COUNT
    out_spread = TableSpread(place, copy, at, o_total, o_in, o_piece, g_head_share, local.at[13])
    at += TableSpread.COUNT
    lanes_half = o_total.shape[0]
    out_swap = copy(
        at, o_table.at[span(1 - place.x, lanes_half)], o_got, place.px
    )

    bring_feed.wait()

    @pl.loop(0, rows // 32)
    def _(i):
        at = span(i, 32)
        grad = cotangent[at, :].astype(f32) + norm_grad(
            middle[at, :].astype(f32), gains[2:3, :], grad_feed[at, :].astype(f32)
        )
        tokens_grad[at, :] = grad
        grad_attn[at, :] = norm_grad(attn_out[at, :].astype(f32), gains[1:2, :], grad).astype(bf16)

    back_mix = (dot_nt(grad_attn[...], mix_out[...]) * masks[0, pl.ds(b, 1), :]).astype(bf16)
    loads[0].wait()
    for j, pb in enumerate((place.b_y, place.b_yc, place.b_c, b)):

        @pl.loop(0, 2)
        def _(h):
            at = span(pb * 2 + h, HEAD)
            grad_mixed[:, at] = (
                dot_nt(grad_attn[...], wo[at, :]) + dot_nn(back_mix, mix_in[:, at])
            ).astype(bf16)

        if j < 3:
            for c in swaps[2 * j : 2 * j + 2]:
                c.start()
    late.start()
    for c in loads[1:]:
        c.wait()
    for n in range(8):
        lanes = slice(n * HEAD, (n + 1) * HEAD)
        got = dot_tn(back_mix, mixed[:, lanes]).astype(bf16)
        for a in range(ADAPTERS):
            h_table[a, 3 * RANK :, lanes] = got[a * RANK : (a + 1) * RANK]
    h_table[:, 3 * RANK :, 8 * HEAD :] = jnp.zeros((ADAPTERS, RANK, width - 8 * HEAD), bf16)

    @pl.loop(0, width // 256)
    def _(n):
        at = span(n, 256)
        got = dot_tn(narrow_mix[...], grad_attn[:, at]).astype(bf16)
        for a in range(ADAPTERS):
            feed_table[a, 3 * RANK :, at] = got[a * RANK : (a + 1) * RANK]

    tokens = grad_attn
    bring_tokens = pltpu.make_async_copy(tokens_hbm, tokens, local.at[23])
    bring_tokens.start()
    feed_reduce.begin()
    for h in range(2):
        lanes = pl.ds(pl.multiple_of(b * 2 * HEAD + h * HEAD, 128), HEAD)
        g[b, h * rows : (h + 1) * rows, :] = grad_mixed[:, lanes]
    for c in swaps:
        c.wait()
    share_spread.plane()

    ones = jnp.ones((8, HEAD), f32)

    @pl.loop(0, 4)
    def _(t):
        for h in range(2):
            at_h = slice(h * rows, (h + 1) * rows)
            lanes = slice(h * HEAD, (h + 1) * HEAD)
            product = g[t, at_h, :].astype(f32) * attended[t, :, lanes].astype(f32)
            delta[t, :, at_h] = lax.dot_general(
                ones, product, (((1,), (1,)), ((), ())), precision=lax.Precision.HIGHEST,
                preferred_element_type=f32,
            )
        inv[t] = 1.0 / sums[t]

    query = lax.broadcasted_iota(jnp.int32, (rows, 2 * rows), 1) % rows
    causal = lax.broadcasted_iota(jnp.int32, (rows, 2 * rows), 0) <= query

    def step(t, k, v, total, slot, masked):
        q, gt = queries[t], g[t]
        th = jnp.tanh(dot_nt(k, q) * (1.0 / soft_cap))
        p = jnp.exp(soft_cap * th) * inv[t, 0:1, :]
        if masked:
            p = jnp.where(causal, p, 0.0)
        total[1, slot] += dot_nn(p.astype(bf16), gt)
        ds = (p * (dot_nt(v, gt) - delta[t, 0:1, :]) * (1.0 - th * th)).astype(bf16)
        total[0, slot] += dot_nn(ds, q)
        dq[t] += dot_tn(ds, k)

    dq[...] = jnp.zeros_like(dq)
    kv_own[...] = jnp.zeros_like(kv_own)

    def kv_copy(d):
        return copy(6 + d - 1, kv_send.at[d - 1], kv_got.at[d - 1], place.up(d))

    @pl.loop(1, planes)
    def _(d):
        zz = (z + d) % planes
        kv_far[...] = jnp.zeros_like(kv_far)
        step(1, kvp[zz, 0, 0], kvp[zz, 1, 0], kv_far, 0, False)

        @pl.when(zz < z)
        def _():
            step(0, kvp[zz, 0, 0], kvp[zz, 1, 0], kv_far, 0, False)
            step(1, kvp[zz, 0, 1], kvp[zz, 1, 1], kv_far, 1, False)

        @pl.loop(2, 4)
        def _(t):
            step(t, kvp[zz, 0, 0], kvp[zz, 1, 0], kv_far, 0, False)
            step(t, kvp[zz, 0, 1], kvp[zz, 1, 1], kv_far, 1, False)

        kv_send[d - 1] = kv_far[...].astype(bf16)
        for k in range(1, planes):

            @pl.when(d == k)
            def _(k=k):
                kv_copy(k).start()
                if k == 1:
                    feed_reduce.merge()
                if k == 2:
                    feed_reduce.corner()
                    share_spread.forward()
                if k == 3:
                    share_spread.corner()

    feed_reduce.finish()
    feed_spread.scatter()
    step(0, kvp[z, 0, 0], kvp[z, 1, 0], kv_own, 0, True)
    step(1, kvp[z, 0, 0], kvp[z, 1, 0], kv_own, 0, False)
    step(1, kvp[z, 0, 1], kvp[z, 1, 1], kv_own, 1, True)

    @pl.loop(2, 4)
    def _(t):
        step(t, kvc[0, t - 2], kvc[1, t - 2], kv_own, t, True)
        step(t, kvp[z, 0, 0], kvp[z, 1, 0], kv_own, 0, False)
        step(t, kvp[z, 0, 1], kvp[z, 1, 1], kv_own, 1, False)

    late.wait()
    feed_spread.gather()
    for d in range(1, planes):
        kv_copy(d).wait_recv()
        kv_own[:, 0:2] += kv_got[d - 1].astype(f32)
    half_head = HEAD // 2

    @pl.loop(0, 4)
    def _(t):
        at = span(t, rows)
        cos, sin = cosine[at, :], sine[at, :]
        mask = masks[0, pl.ds(t, 1), :]

        def turned(pre, scale):
            first, second = pre[:, :half_head], pre[:, half_head:]
            one, two = first * cos + second * sin, second * cos - first * sin
            if scale != 1.0:
                one, two = one * scale, two * scale
            return jnp.concatenate([one, two], axis=1).astype(bf16)

        for h in range(2):
            grad_pre[at, h * HEAD : (h + 1) * HEAD] = turned(
                dq[t, h * rows : (h + 1) * rows, :], HEAD ** (-0.5)
            )
        grad_pre[at, 2 * HEAD : 3 * HEAD] = turned(kv_own[0, t], 1.0)
        grad_pre[at, 3 * HEAD :] = kv_own[1, t].astype(bf16)
        for i, (lanes, table) in enumerate(
            (
                (slice(0, 2 * HEAD), query_out),
                (slice(2 * HEAD, 3 * HEAD), key_out),
                (slice(3 * HEAD, 4 * HEAD), value_out),
            )
        ):
            back[at, i * LANES : (i + 1) * LANES] = (
                dot_nt(grad_pre[at, lanes], flat(table[...])) * mask
            ).astype(bf16)

    feed_spread.plane()
    for i, lanes in enumerate(
        (slice(0, 2 * HEAD), slice(2 * HEAD, 3 * HEAD), slice(3 * HEAD, 4 * HEAD))
    ):
        o_table[:, lanes] = dot_tn(
            narrow[:, i * LANES : (i + 1) * LANES], grad_pre[:, lanes]
        ).astype(bf16)
    out_swap.start()

    @pl.loop(0, width // 256)
    def _(n):
        at = span(n, 256)
        got = dot_tn(back[...], normed_all[:, at]).astype(bf16)
        for i in range(3):
            for a in range(ADAPTERS):
                first = i * LANES + a * RANK
                h_table[a, i * RANK : (i + 1) * RANK, at] = got[first : first + RANK]

    head_reduce.begin()

    def project(slot, target):
        at_rows = span(target, rows)

        @pl.loop(0, width // 256)
        def _(n):
            at = span(n, 256)
            part[slot][:, at] = (
                dot_nt(grad_pre[at_rows, :], wall[at, :])
                + dot_nn(back[at_rows, :], heads_in[:, :, :, at].reshape(3 * LANES, 256))
            ).astype(bf16)

    to_core = [copy(9 + i, part[i], from_core.at[i], place.pc) for i in range(2)]
    to_y = copy(11, part[2], from_y, place.py)
    project(0, place.b_yc)
    to_core[0].start()
    head_reduce.merge()
    feed_spread.forward()
    project(2, place.b_y)
    head_reduce.corner()
    to_core[0].wait_recv()
    add_into(part[2], from_core.at[0], rows)
    to_y.start()
    out_swap.wait_recv()

    @pl.loop(0, lanes_half // 16)
    def _(i):
        at = span(i, 16)
        mine = pl.ds(pl.multiple_of(place.x * lanes_half + i * 16, 16), 16)
        o_total[at, :] = (o_table[mine, :].astype(f32) + o_got[at, :].astype(f32)).astype(bf16)

    feed_spread.corner()
    out_spread.scatter()
    head_reduce.finish()
    head_spread.scatter()
    project(1, place.b_c)
    to_core[1].start()
    head_spread.gather()
    out_spread.gather()
    project(3, b)
    head_spread.plane()
    out_spread.plane()
    head_spread.forward()
    out_spread.forward()
    to_core[1].wait_recv()
    head_spread.corner()
    out_spread.corner()
    to_y.wait_recv()
    bring_tokens.wait()

    @pl.loop(0, rows // 32)
    def _(i):
        at = span(i, 32)
        grad = (
            part[3][at, :].astype(f32)
            + from_core[1, at, :].astype(f32)
            + from_y[at, :].astype(f32)
        )
        tokens_grad[at, :] += norm_grad(tokens[at, :].astype(f32), gains[0:1, :], grad)

    for spread in (share_spread, feed_spread, out_spread, head_spread):
        spread.finish()
    own_share.wait()
    out_swap.wait_send()
    to_y.wait_send()
    for c in to_core:
        c.wait_send()
    for d in range(1, planes):
        kv_copy(d).wait_send()


def attention_backward(rows_in, kept, grad_feed, tokens, tables, weights, feed_table, feed_share):
    rows, width = rows_in[0].shape
    planes = lax.axis_size("ulysses")
    m = 4 * RANK
    hm = 4 * RANK
    ow = 4 * HEAD
    om = LANES // 2
    count = 12 + 2 * TableReduce.COUNT + 3 * TableSpread.COUNT + PlaneSpread.COUNT + 1

    def reduce_scratch(m):
        return [
            pltpu.VMEM((ADAPTERS, m, width), bf16),
            pltpu.VMEM((4, m, width), bf16),
            pltpu.VMEM((4, m, width), bf16),
            pltpu.VMEM((m, width), bf16),
            pltpu.VMEM((m, width), bf16),
            pltpu.VMEM((m, width), bf16),
            pltpu.VMEM((m, width), bf16),
        ]

    def spread_scratch(m, w):
        return [
            pltpu.VMEM((planes - 1, m // planes, w), bf16),
            pltpu.VMEM((m // planes, w), bf16),
        ]

    return pl.pallas_call(
        attention_backward_kernel,
        out_shape=(
            shape((rows, width), f32),
            shape((8, planes, m // planes, width), bf16),
            shape((8,) + feed_share.shape, bf16),
            shape((8, planes, hm // planes, width), bf16),
            shape((8, planes, om // planes, ow), bf16),
        ),
        in_specs=[VM] * 17 + [ANY] * 10,
        out_specs=(VM, ANY, ANY, ANY, ANY),
        scratch_shapes=head_table_scratch(width)
        + [
            pltpu.VMEM((8 * HEAD, width), bf16),
            pltpu.VMEM((width, 4 * HEAD), bf16),
            pltpu.VMEM((rows, width), bf16),
            pltpu.VMEM((rows, 8 * HEAD), bf16),
            pltpu.VMEM((4, 2 * rows, HEAD), bf16),
            pltpu.VMEM((4, 8, 2 * rows), f32),
            pltpu.VMEM((4, 8, 2 * rows), f32),
            pltpu.VMEM((4, 2 * rows, HEAD), f32),
            pltpu.VMEM((2, 4, rows, HEAD), f32),
            pltpu.VMEM((2, 2, rows, HEAD), f32),
            pltpu.VMEM((planes - 1, 2, 2, rows, HEAD), bf16),
            pltpu.VMEM((planes - 1, 2, 2, rows, HEAD), bf16),
            pltpu.VMEM((4 * rows, 4 * HEAD), bf16),
            pltpu.VMEM((4 * rows, 3 * LANES), bf16),
            pltpu.VMEM((2, rows, width), bf16),
            pltpu.VMEM((rows, width), bf16),
        ]
        + reduce_scratch(m)
        + spread_scratch(m, width)
        + reduce_scratch(hm)
        + spread_scratch(hm, width)
        + [
            pltpu.VMEM((LANES, ow), bf16),
            pltpu.VMEM((om, ow), bf16),
            pltpu.VMEM((om, ow), bf16),
        ]
        + spread_scratch(om, ow)
        + [
            pltpu.SemaphoreType.DMA((count,)),
            pltpu.SemaphoreType.DMA((count,)),
            pltpu.SemaphoreType.DMA((25,)),
        ],
        compiler_params=pltpu.CompilerParams(
            collective_id=4, has_side_effects=True, vmem_limit_bytes=63 << 20
        ),
        name="attention_backward",
    )(*rows_in, *kept, grad_feed, tokens, *tables, *weights, feed_table, feed_share)


def lay_out_kernel(
    feed_rows, feed_columns, head_rows, head_columns,
    heads_in, query_out, kv_out, t_mix_in, t_mix_out, feed_in, feed_out, t_down_in, t_down_out,
):
    rows = feed_rows[0]
    feed_in[0, 0] = rows[0].astype(f32)
    feed_in[0, 1] = rows[1].astype(f32)
    t_down_out[0] = rows[2].astype(f32)
    t_mix_out[0] = rows[3].astype(f32)
    rows = head_rows[0]
    for i in range(3):
        heads_in[0, i] = rows[i].astype(f32)
    t_mix_in[0] = rows[3, :, : t_mix_in.shape[2]].astype(f32)
    share = feed_out.shape[3]
    table = feed_columns[0].reshape(3, ADAPTERS, RANK, share)
    for a in range(ADAPTERS):
        feed_out[a, 0] = table[0, a].astype(f32)
        feed_out[a, 1] = table[1, a].astype(f32)
        t_down_in[a] = table[2, a].astype(f32)
    for a in range(head_columns.shape[1]):
        got = head_columns[0, a].astype(f32)
        query_out[a] = got[:, : 2 * HEAD]
        kv_out[a, 0] = got[:, 2 * HEAD : 3 * HEAD]
        kv_out[a, 1] = got[:, 3 * HEAD :]


def lay_out(feed_rows, feed_columns, head_rows, head_columns):
    planes, _, width = feed_rows.shape[1:]
    share = feed_columns.shape[3]
    ff = 8 * share

    def whole(array):
        return pl.BlockSpec((1,) + array.shape[1:], lambda r: (r, 0, 0, 0))

    return pl.pallas_call(
        lay_out_kernel,
        grid=(8,),
        out_shape=(
            shape((ADAPTERS, 3, RANK, width), f32),
            shape((ADAPTERS, RANK, 8 * HEAD), f32),
            shape((ADAPTERS, 2, RANK, 4 * HEAD), f32),
            shape((ADAPTERS, RANK, 8 * HEAD), f32),
            shape((ADAPTERS, RANK, width), f32),
            shape((ADAPTERS, 2, RANK, width), f32),
            shape((ADAPTERS, 2, RANK, ff), f32),
            shape((ADAPTERS, RANK, ff), f32),
            shape((ADAPTERS, RANK, width), f32),
        ),
        in_specs=[whole(x) for x in (feed_rows, feed_columns, head_rows, head_columns)],
        out_specs=(
            pl.BlockSpec((1, 3, RANK, width), lambda r: (r, 0, 0, 0)),
            pl.BlockSpec((planes, RANK, 2 * HEAD), lambda r: (r // 4, 0, r % 4)),
            pl.BlockSpec((planes, 2, RANK, HEAD), lambda r: (r // 4, 0, 0, r % 4)),
            pl.BlockSpec((1, RANK, 8 * HEAD), lambda r: (r, 0, 0)),
            pl.BlockSpec((1, RANK, width), lambda r: (r, 0, 0)),
            pl.BlockSpec((1, 2, RANK, width), lambda r: (r, 0, 0, 0)),
            pl.BlockSpec((ADAPTERS, 2, RANK, share), lambda r: (0, 0, 0, r)),
            pl.BlockSpec((ADAPTERS, RANK, share), lambda r: (0, 0, r)),
            pl.BlockSpec((1, RANK, width), lambda r: (r, 0, 0)),
        ),
        compiler_params=pltpu.CompilerParams(vmem_limit_bytes=62 << 20),
        name="lay_out",
    )(feed_rows, feed_columns, head_rows, head_columns)


def shards(
    tokens,
    query_weight,
    key_projection,
    value_projection,
    out_weight,
    gate_weight,
    up_weight,
    down_weight,
    attn_in_gain,
    attn_out_gain,
    feed_in_gain,
    feed_out_gain,
    adapt_heads_in,
    adapt_query_out,
    adapter_key_value_second,
    adapt_mix_in,
    adapt_mix_out,
    adapt_feed_in,
    adapt_feed_out,
    adapt_down_in,
    adapt_down_out,
    adapter_ids,
    cotangent,
):
    width = tokens.shape[1]
    blk_n = lax.axis_size("blk")
    dp_n = lax.axis_size("dp")
    rank = lax.axis_index("dp") % 2 * blk_n + lax.axis_index("blk")
    ff = gate_weight.shape[1]
    share = ff // (2 * blk_n)
    weights = (
        query_weight, key_projection, value_projection, out_weight, gate_weight, up_weight,
        down_weight,
    )
    if dp_n > 2:
        weights = tuple(
            lax.dynamic_slice_in_dim(
                lax.all_gather(weight, PLANE, axis=0, tiled=True),
                rank * (weight.shape[0] * dp_n // 2),
                weight.shape[0] * dp_n // 2,
            )
            for weight in weights
        )
    down_rows = weights[6]
    gains = jnp.stack([attn_in_gain, attn_out_gain, feed_in_gain, feed_out_gain])
    mix_in, mix_out, down_out = flat(adapt_mix_in), flat(adapt_mix_out), flat(adapt_down_out)
    head_tables = (adapt_heads_in, adapt_query_out, adapter_key_value_second)
    feed_tables = (adapt_feed_in, adapt_feed_out, adapt_down_in)
    (
        queries, kvp, kvc, attended, exp_sum, narrow_heads, mixed, narrow_mix, attn_out, middle,
        normed_feed, cosine, sine, masks, normed_all, head_weight, out_full, gate_share, up_share,
    ) = attention_forward(
        tokens, gains, adapter_ids, mix_in, mix_out, head_tables, weights[:6], share
    )
    layer_out, grad_branch, narrow_feed, feed_all, gate_up = feed_forward(
        normed_feed, middle, cotangent, gains, masks, down_out, feed_tables, gate_share, up_share,
        down_rows,
    )
    grad_feed, feed_table, share_sum = feed_backward(
        grad_branch, masks, down_out, narrow_feed, feed_tables, gate_share, up_share, down_rows,
        gate_up, feed_all,
    )
    tokens_grad, feed_rows, feed_columns, head_rows, head_columns = attention_backward(
        (
            middle, attn_out, cotangent, gains, masks, mixed, narrow_mix, mix_in, mix_out,
        ),
        (queries, kvp, kvc, attended, exp_sum, narrow_heads, cosine, sine),
        grad_feed,
        tokens,
        head_tables,
        (out_full, normed_all, head_weight),
        feed_table,
        share_sum,
    )

    summed = lay_out(feed_rows, feed_columns, head_rows, head_columns)
    if dp_n > 2:
        summed = tuple(lax.psum(table * 0.5, "dp") for table in summed)
    return (layer_out, tokens_grad) + summed


def solution(mesh):
    sharded = P(EVERY, None)
    rowwise = P(PLANE, None)
    placed = (
        (sharded,) + (rowwise,) * 7 + (P(),) * 13 + (P("dp", None), sharded)
    )
    return jax.shard_map(
        shards,
        mesh=mesh,
        in_specs=placed,
        out_specs=(sharded, sharded) + (P(),) * 9,
        check_vma=False,
    )
```

```python
import math

import jax
import jax.numpy as jnp
from jax import lax
from jax.experimental import pallas as pl
from jax.experimental.pallas import tpu as pltpu
from jax.sharding import PartitionSpec as P

HEADS = 8
KV_HEADS = 4
HEAD = 256
RANK = 16
ADAPTERS = 8
LANES = RANK * ADAPTERS
PROMPT = 2048
CONT = 256
CONTS = 8

epsilon = 1e-06
soft_cap = 50.0
rope_base = 10000.0
PLANE = ("dp", "blk")
EVERY = ("dp", "blk", "ulysses")
f32 = jnp.float32
bf16 = jnp.bfloat16


def dot_nn(a, b):
    return jnp.dot(a, b, preferred_element_type=f32)


def dot_nt(a, b):
    return lax.dot_general(a, b, (((1,), (1,)), ((), ())), preferred_element_type=f32)


def dot_tn(a, b):
    return lax.dot_general(a, b, (((0,), (0,)), ((), ())), preferred_element_type=f32)


def norm_grad(values, gain_row, grad_out):
    scale = lax.rsqrt(jnp.mean(values * values, axis=-1, keepdims=True) + epsilon)
    weighted = grad_out * gain_row
    return scale * weighted - values * (
        scale * scale * scale * jnp.mean(values * weighted, axis=-1, keepdims=True)
    )


def shape(dims, dtype):
    return jax.ShapeDtypeStruct(dims, dtype)


VM = pl.BlockSpec(memory_space=pltpu.VMEM)


MESH = pl.DeviceIdType.MESH


def neighbours():
    dp, b, z = lax.axis_index("dp"), lax.axis_index("blk"), lax.axis_index("ulysses")
    across_x = (dp + 1 - 2 * (dp % 2), b, z)
    across_y = (dp, (b + 2) % 4, z)
    sibling = (dp, b + 1 - 2 * (b % 2), z)
    return across_x, across_y, sibling


def greet(peers):
    barrier = pltpu.get_barrier_semaphore()
    for peer in peers:
        pl.semaphore_signal(barrier, inc=1, device_id=peer, device_id_type=MESH)
    pl.semaphore_wait(barrier, len(peers))


def sender(send, recv):
    def copy(index, src, dst, peer):
        return pltpu.make_async_remote_copy(
            src, dst, send.at[index], recv.at[index], device_id=peer, device_id_type=MESH
        )

    return copy


def add_into(target, source, count, step=32):
    @pl.loop(0, count // step)
    def _(i):
        at = pl.ds(pl.multiple_of(i * step, step), step)
        target[at, :] = (target[at, :].astype(f32) + source[at, :].astype(f32)).astype(target.dtype)


class PlaneGather:
    COUNT = 10

    def __init__(self, copy, own, land, rows):
        px, py, pc = neighbours()
        h = rows // 2
        h0, h1 = pl.ds(0, h), pl.ds(h, h)
        near, far = pl.ds(0, rows), pl.ds(rows, rows)
        self.c = [
            copy(0, own, land.at[0, far], pc),
            copy(1, own.at[h0], land.at[1, h0], px),
            copy(2, own.at[h1], land.at[1, h1], py),
            copy(3, own.at[h1], land.at[3, h0], px),
            copy(4, own.at[h0], land.at[3, h1], py),
            copy(5, land.at[1, h0], land.at[2, h0], py),
            copy(6, land.at[1, h1], land.at[2, h1], px),
            copy(7, land.at[1, near], land.at[1, far], pc),
            copy(8, land.at[3, near], land.at[3, far], pc),
            copy(9, land.at[2, near], land.at[2, far], pc),
        ]

    def begin(self):
        for i in range(3):
            self.c[i].start()

    def before(self, i):
        c = self.c

        @pl.when(i == 0)
        def _():
            c[0].wait_recv()

        @pl.when(i == 1)
        def _():
            c[1].wait_recv()
            c[5].start()
            c[2].wait_recv()
            c[6].start()
            c[7].start()
            for k in (3, 4):
                c[k].start()
            c[7].wait_recv()

        @pl.when(i == 2)
        def _():
            c[5].wait_recv()
            c[6].wait_recv()
            c[9].start()
            c[9].wait_recv()

        @pl.when(i == 3)
        def _():
            c[3].wait_recv()
            c[4].wait_recv()
            c[8].start()
            c[8].wait_recv()

    def finish(self):
        for c in self.c:
            c.wait_send()


def plane_masks(masks, i, rows):
    b = lax.axis_index("blk")
    diagonal = i // 2 * (1 - i % 2)
    away = (i + 2) // 3
    out = jnp.zeros((2 * rows, LANES), f32)
    place = lax.broadcasted_iota(jnp.int32, (2 * rows, LANES), 0) // (rows // 2)
    for half, (group, shift) in enumerate(((away, diagonal), (diagonal, away))):
        near = (b + 2 * shift) % 4
        far = near + 1 - 2 * (near % 2)
        out = jnp.where(place == half, masks[group, pl.ds(near, 1), :], out)
        out = jnp.where(place == 2 + half, masks[group, pl.ds(far, 1), :], out)
    return out


def feed_table_copies(rank, share, feed_in_hbm, feed_out_hbm, down_in_hbm, feed_in, feed_out, down_in):
    lanes = pl.ds(pl.multiple_of(rank * share, 128), share)
    return [
        (feed_in_hbm.at[:, 0], feed_in.at[0]),
        (feed_in_hbm.at[:, 1], feed_in.at[1]),
        (feed_out_hbm.at[:, 0, :, lanes], feed_out.at[0]),
        (feed_out_hbm.at[:, 1, :, lanes], feed_out.at[1]),
        (down_in_hbm.at[:, :, lanes], down_in),
    ]


def feed_table_scratch(width, share):
    return [
        pltpu.VMEM((2, ADAPTERS, RANK, width), bf16),
        pltpu.VMEM((2, ADAPTERS, RANK, share), bf16),
        pltpu.VMEM((ADAPTERS, RANK, share), bf16),
    ]


class PlaneReduce:
    COUNT = 10

    def __init__(self, copy, part, odd, from_core, from_x, from_y, diag, rows, first):
        px, py, pc = neighbours()
        h = rows // 2
        self.h = h
        self.rows = rows
        h0, h1 = pl.ds(0, h), pl.ds(h, h)
        self.part, self.from_core = part, from_core
        self.from_x, self.from_y, self.diag = from_x, from_y, diag
        self.core = [
            copy(first + i, odd.at[i % 2], from_core.at[i], pc) for i in range(4)
        ]
        self.d = [
            copy(first + 4, part.at[2, h0], diag.at[h0], px),
            copy(first + 5, part.at[2, h1], diag.at[h1], py),
        ]
        self.e = [
            copy(first + 6, part.at[1, h0], from_x.at[h0], px),
            copy(first + 7, part.at[1, h1], from_y.at[h1], py),
            copy(first + 8, part.at[3, h0], from_x.at[h1], px),
            copy(first + 9, part.at[3, h1], from_y.at[h0], py),
        ]

    def merge(self, i):
        self.core[i].wait_recv()
        add_into(self.part.at[i], self.from_core.at[i], self.rows)

    def before(self, i):
        for k in (2, 3):

            @pl.when(i == k)
            def _(k=k):
                self.core[k - 2].wait_send()

    def after(self, i):
        for k in range(4):

            @pl.when(i == k)
            def _(k=k):
                self.core[k].start()
                if k == 2:
                    self.merge(1)
                    self.e[0].start()
                    self.e[1].start()
                    self.merge(2)
                    self.d[0].start()
                    self.d[1].start()

    def finish(self, write, between=None):
        h, h0, h1 = self.h, pl.ds(0, self.h), pl.ds(self.h, self.h)
        self.merge(3)
        self.d[0].wait_recv()
        add_into(self.part.at[3, h1], self.diag.at[h0], h)
        self.e[3].start()
        self.d[1].wait_recv()
        add_into(self.part.at[3, h0], self.diag.at[h1], h)
        self.e[2].start()
        if between is not None:
            between()
        self.merge(0)
        for e in self.e:
            e.wait_recv()

        @pl.loop(0, self.rows // 32)
        def _(i):
            at = pl.ds(pl.multiple_of(i * 32, 32), 32)
            write(
                at,
                self.part[0, at, :].astype(f32)
                + self.from_x[at, :].astype(f32)
                + self.from_y[at, :].astype(f32),
            )

        for c in self.core[2:] + self.d + self.e:
            c.wait_send()


GELU_SLOPE = 0.7978845608028654
GELU_CUBE = 0.044715


def plane_rank():
    return lax.axis_index("dp") % 2 * 4 + lax.axis_index("blk")


def span(i, size):
    return pl.ds(pl.multiple_of(i * size, size), size)


def woven(gate_hbm, up_hbm, both):
    out = []
    for j in range(gate_hbm.shape[1] // 128):
        for k, ref in enumerate((gate_hbm, up_hbm)):
            out.append(
                (ref.at[:, pl.ds(j * 128, 128)], both.at[:, pl.ds(j * 256 + k * 128, 128)])
            )
    return out


def weave_table(feed_out, woven_out):
    woven_out[...] = jnp.zeros_like(woven_out)
    for j in range(feed_out.shape[3] // 128):
        for k in range(2):
            at = j * 256 + k * 128
            woven_out[k, :, :, at : at + 128] = feed_out[k, :, :, j * 128 : (j + 1) * 128]


def feed_forward_kernel(
    own, middle, cotangent, gains, masks, down_out, feed_in_hbm, feed_out_hbm, down_in_hbm,
    gate_hbm, up_hbm, down_hbm,
    layer_out, grad_branch, narrow, feed_all, gate_up,
    narrow_two, woven_out, feed_in, feed_out, down_in, weave, down, land, hidden, saved, part, odd, from_core, from_x, from_y, diag,
    send, recv, load, store,
):
    rows = own.shape[0]
    share = gate_hbm.shape[1]
    width = own.shape[1]
    tile = 256
    loads = [
        pltpu.make_async_copy(s, d, load.at[i])
        for i, (s, d) in enumerate(
            woven(gate_hbm, up_hbm, weave)
            + [(down_hbm, down)]
            + feed_table_copies(
                plane_rank(), share, feed_in_hbm, feed_out_hbm, down_in_hbm, feed_in, feed_out,
                down_in,
            )
        )
    ]
    for c in loads:
        c.start()
    greet(neighbours())
    copy = sender(send, recv)
    gather = PlaneGather(copy, own, land, rows)
    reduce = PlaneReduce(
        copy, part, odd, from_core, from_x, from_y, diag, rows, PlaneGather.COUNT
    )
    gather.begin()
    land[0, :rows, :] = own[...]
    for c in loads:
        c.wait()
    weave_table(feed_out, woven_out)

    def keep(i):
        slot = i % 2
        return (
            pltpu.make_async_copy(saved.at[slot], gate_up.at[i], store.at[slot]),
            pltpu.make_async_copy(land.at[i], feed_all.at[i], store.at[2 + slot]),
        )

    @pl.loop(0, 4)
    def _(i):
        gather.before(i)
        slot = i % 2

        @pl.when(i >= 2)
        def _():
            for c in keep(i - 2):
                c.wait()

        mask = plane_masks(masks, i, rows)
        low = dot_nt(land[i], feed_in[...].reshape(2 * LANES, width))
        for k in range(2):
            lanes = slice(k * LANES, (k + 1) * LANES)
            narrow_two[:, lanes] = (low[:, lanes] * mask).astype(bf16)
            narrow[i, k] = narrow_two[:, lanes]

        @pl.loop(0, share // 128)
        def _(n):
            at = span(n, 128)
            pair = span(n, 256)
            pre = dot_nn(land[i], weave[:, pair]) + dot_nn(
                narrow_two[...], woven_out[:, :, :, pair].reshape(2 * LANES, 256)
            )
            g, u = pre[:, :128], pre[:, 128:]
            saved[slot, 0, :, at] = g.astype(bf16)
            saved[slot, 1, :, at] = u.astype(bf16)
            th = jnp.tanh(GELU_SLOPE * (g + GELU_CUBE * g * g * g))
            hidden[:, at] = (0.5 * g * (1.0 + th) * u).astype(bf16)

        for c in keep(i):
            c.start()
        narrow[i, 2] = (dot_nt(hidden[...], flat(down_in[...])) * mask).astype(bf16)
        reduce.before(i)

        @pl.loop(0, width // tile)
        def _(n):
            at = span(n, tile)
            got = dot_nn(hidden[...], down[:, at]) + dot_nn(narrow[i, 2], down_out[:, at])
            got = got.astype(bf16)
            part[i, :, at] = got[:rows]
            odd[i % 2, :, at] = got[rows:]

        reduce.after(i)

    def write(at, branch):
        scale = lax.rsqrt(jnp.mean(branch * branch, axis=-1, keepdims=True) + epsilon)
        gain = gains[3:4, :]
        layer_out[at, :] = (middle[at, :].astype(f32) + branch * scale * gain).astype(bf16)
        grad_branch[at, :] = norm_grad(branch, gain, cotangent[at, :].astype(f32)).astype(bf16)

    reduce.finish(write)
    gather.finish()
    for i in (2, 3):
        for c in keep(i):
            c.wait()


def feed_backward_kernel(
    own, masks, down_out, narrow, feed_in_hbm, feed_out_hbm, down_in_hbm,
    gate_hbm, up_hbm, down_hbm, gate_up, feed_all,
    grad_feed, feed_table, share_sum,
    back, both, t_feed_out, t_down_in, t_down_out, share_table, share_in, share_piece,
    woven_out, feed_in, feed_out, down_in, weave, down, land, saved, gg, part, odd, from_core, from_x, from_y, diag,
    send, recv, load, fetch,
):
    rows = own.shape[0]
    share = gate_hbm.shape[1]
    width = own.shape[1]
    tile = 256
    loads = [
        pltpu.make_async_copy(s, d, load.at[i])
        for i, (s, d) in enumerate(
            woven(gate_hbm, up_hbm, weave)
            + [(down_hbm, down)]
            + feed_table_copies(
                plane_rank(), share, feed_in_hbm, feed_out_hbm, down_in_hbm, feed_in, feed_out,
                down_in,
            )
        )
    ]

    def bring(i):
        return pltpu.make_async_copy(gate_up.at[i], saved, fetch.at[0])

    for c in loads:
        c.start()
    bring(0).start()
    place = Places()
    greet(list(neighbours()) + [place.up(d) for d in range(1, place.planes)])
    copy = sender(send, recv)
    spread = TableSum(
        place, copy, PlaneGather.COUNT + PlaneReduce.COUNT, share_table, share_in, share_piece,
        lambda z: share_sum.at[z], fetch.at[1],
    )
    gather = PlaneGather(copy, own, land, rows)
    reduce = PlaneReduce(
        copy, part, odd, from_core, from_x, from_y, diag, rows, PlaneGather.COUNT
    )
    gather.begin()
    land[0, :rows, :] = own[...]
    t_feed_out[...] = jnp.zeros_like(t_feed_out)
    t_down_in[...] = jnp.zeros_like(t_down_in)
    t_down_out[...] = jnp.zeros_like(t_down_out)
    for c in loads:
        c.wait()
    weave_table(feed_out, woven_out)

    @pl.loop(0, 4)
    def _(i):
        gather.before(i)
        bring(i).wait()
        mask = plane_masks(masks, i, rows)
        back[...] = (dot_nt(land[i], down_out[...]) * mask).astype(bf16)

        @pl.loop(0, 2)
        def _(n):
            at = span(n, rows)
            gh = dot_nt(land[i, at, :], down[...]) + dot_nn(back[at, :], flat(down_in[...]))
            g = saved[0, at, :].astype(f32)
            u = saved[1, at, :].astype(f32)
            th = jnp.tanh(GELU_SLOPE * (g + GELU_CUBE * g * g * g))
            gelu = 0.5 * g * (1.0 + th)
            slope = 0.5 * (1.0 + th) + 0.5 * g * (1.0 - th * th) * GELU_SLOPE * (
                1.0 + 3.0 * GELU_CUBE * g * g
            )
            saved[0, at, :] = (gelu * u).astype(bf16)
            left = (gh * u * slope).astype(bf16)
            right = (gh * gelu).astype(bf16)
            for j in range(share // 128):
                lanes = slice(j * 128, (j + 1) * 128)
                gg[at, j * 256 : j * 256 + 128] = left[:, lanes]
                gg[at, j * 256 + 128 : (j + 1) * 256] = right[:, lanes]

        t_down_in[...] += dot_tn(back[...], saved[0])

        @pl.when(i < 3)
        def _():
            bring(i + 1).start()

        low = dot_nt(gg[...], woven_out[...].reshape(2 * LANES, 2 * share))
        for k in range(2):
            lanes = slice(k * LANES, (k + 1) * LANES)
            both[i, :, lanes] = (low[:, lanes] * mask).astype(bf16)
        reduce.before(i)

        @pl.loop(0, width // tile)
        def _(n):
            at = span(n, tile)
            got = (
                dot_nt(gg[...], weave[at, :])
                + dot_nn(both[i], feed_in[:, :, :, at].reshape(2 * LANES, 256))
            ).astype(bf16)
            part[i, :, at] = got[:rows]
            odd[i % 2, :, at] = got[rows:]

        reduce.after(i)
        for k in range(2):
            for j in range(share // 128):
                at = j * 256 + k * 128
                t_feed_out[k, :, j * 128 : (j + 1) * 128] += dot_tn(
                    narrow[i, k], gg[:, at : at + 128]
                )
        t_down_out[...] += dot_tn(narrow[i, 2], land[i])

    share_table[: 2 * LANES] = t_feed_out[...].reshape(2 * LANES, share).astype(bf16)
    share_table[2 * LANES :] = t_down_in[...].astype(bf16)
    spread.scatter()
    gather.finish()
    reload = [pltpu.make_async_copy(feed_all.at[i], land.at[i], fetch.at[2 + i]) for i in range(4)]
    for c in reload:
        c.start()

    def tables():
        spread.gather()
        for c in reload:
            c.wait()
        backs = both[...].reshape(8 * rows, 2 * LANES)

        @pl.loop(0, width // 256)
        def _(n):
            at = span(n, 256)
            got = dot_tn(backs, land[:, :, at].reshape(8 * rows, 256)).astype(bf16)
            last = t_down_out[:, at].astype(bf16)
            for a in range(ADAPTERS):
                first = slice(a * RANK, (a + 1) * RANK)
                second = slice(LANES + a * RANK, LANES + (a + 1) * RANK)
                feed_table[a, :RANK, at] = got[first]
                feed_table[a, RANK : 2 * RANK, at] = got[second]
                feed_table[a, 2 * RANK :, at] = last[first]

    def write(at, total):
        grad_feed[at, :] = total.astype(grad_feed.dtype)

    reduce.finish(write, tables)
    spread.finish()


def feed_scratch(rows, width, extra=0):
    count = PlaneGather.COUNT + PlaneReduce.COUNT + extra
    return [
        pltpu.VMEM((4, rows, width), bf16),
        pltpu.VMEM((2, rows, width), bf16),
        pltpu.VMEM((4, rows, width), bf16),
        pltpu.VMEM((rows, width), bf16),
        pltpu.VMEM((rows, width), bf16),
        pltpu.VMEM((rows, width), bf16),
        pltpu.SemaphoreType.DMA((count,)),
        pltpu.SemaphoreType.DMA((count,)),
    ]


ANY = pl.BlockSpec(memory_space=pl.ANY)


def feed_forward(own, middle, cotangent, gains, masks, down_out, tables, gate, up, down):
    rows, width = own.shape
    share = gate.shape[1]
    return pl.pallas_call(
        feed_forward_kernel,
        out_shape=(
            shape((rows, width), bf16),
            shape((rows, width), bf16),
            shape((4, 3, 2 * rows, LANES), bf16),
            shape((4, 2 * rows, width), bf16),
            shape((4, 2, 2 * rows, share), bf16),
        ),
        in_specs=[VM] * 6 + [ANY] * 6,
        out_specs=(VM, VM, VM, ANY, ANY),
        scratch_shapes=[
            pltpu.VMEM((2 * rows, 2 * LANES), bf16),
            pltpu.VMEM((2, ADAPTERS, RANK, 2 * share), bf16),
        ]
        + feed_table_scratch(width, share)
        + [
            pltpu.VMEM((width, 2 * share), bf16),
            pltpu.VMEM(down.shape, bf16),
            pltpu.VMEM((4, 2 * rows, width), bf16),
            pltpu.VMEM((2 * rows, share), bf16),
            pltpu.VMEM((2, 2, 2 * rows, share), bf16),
        ]
        + feed_scratch(rows, width)
        + [pltpu.SemaphoreType.DMA((6 + share // 64,)), pltpu.SemaphoreType.DMA((4,))],
        compiler_params=pltpu.CompilerParams(
            collective_id=1, has_side_effects=True, vmem_limit_bytes=62 << 20
        ),
        name="feed_forward",
    )(own, middle, cotangent, gains, masks, down_out, *tables, gate, up, down)


def feed_backward(own, masks, down_out, narrow, tables, gate, up, down, gate_up, feed_all):
    rows, width = own.shape
    share = gate.shape[1]
    planes = lax.axis_size("ulysses")
    piece = 3 * LANES // planes
    return pl.pallas_call(
        feed_backward_kernel,
        out_shape=(
            shape((rows, width), bf16),
            shape((ADAPTERS, 3 * RANK, width), bf16),
            shape((planes, piece, share), bf16),
        ),
        in_specs=[VM] * 4 + [ANY] * 8,
        out_specs=(VM, VM, ANY),
        scratch_shapes=[
            pltpu.VMEM((2 * rows, LANES), bf16),
            pltpu.VMEM((4, 2 * rows, 2 * LANES), bf16),
            pltpu.VMEM((2, LANES, share), f32),
            pltpu.VMEM((LANES, share), f32),
            pltpu.VMEM((LANES, width), f32),
            pltpu.VMEM((3 * LANES, share), bf16),
            pltpu.VMEM((planes - 1, piece, share), bf16),
            pltpu.VMEM((piece, share), bf16),
            pltpu.VMEM((2, ADAPTERS, RANK, 2 * share), bf16),
        ]
        + feed_table_scratch(width, share)
        + [
            pltpu.VMEM((width, 2 * share), bf16),
            pltpu.VMEM(down.shape, bf16),
            pltpu.VMEM((4, 2 * rows, width), bf16),
            pltpu.VMEM((2, 2 * rows, share), bf16),
            pltpu.VMEM((2 * rows, 2 * share), bf16),
        ]
        + feed_scratch(rows, width, TableSum.COUNT)
        + [pltpu.SemaphoreType.DMA((6 + share // 64,)), pltpu.SemaphoreType.DMA((6,))],
        compiler_params=pltpu.CompilerParams(
            collective_id=2, has_side_effects=True, vmem_limit_bytes=62 << 20
        ),
        name="feed_backward",
    )(own, masks, down_out, narrow, *tables, gate, up, down, gate_up, feed_all)


def flat(table):
    return table.reshape(LANES, table.shape[-1])


def head_table_copies(
    b, heads_hbm, query_out_hbm, kv_out_hbm, heads_in, query_out, key_out, value_out
):
    lanes = pl.ds(pl.multiple_of(b * 2 * HEAD, 128), 2 * HEAD)
    lane = pl.ds(pl.multiple_of(b * HEAD, 128), HEAD)
    return [(heads_hbm.at[:, i], heads_in.at[i]) for i in range(3)] + [
        (query_out_hbm.at[:, :, lanes], query_out),
        (kv_out_hbm.at[:, 0, :, lane], key_out),
        (kv_out_hbm.at[:, 1, :, lane], value_out),
    ]


def head_table_scratch(width):
    return [
        pltpu.VMEM((3, ADAPTERS, RANK, width), bf16),
        pltpu.VMEM((ADAPTERS, RANK, 2 * HEAD), bf16),
        pltpu.VMEM((ADAPTERS, RANK, HEAD), bf16),
        pltpu.VMEM((ADAPTERS, RANK, HEAD), bf16),
    ]


def adapter_mask(ids, t, z, planes, rows):
    sequence = 0 if t * planes * rows < PROMPT else 1 + ((t * planes + z) * rows - PROMPT) // CONT
    owner = lax.broadcasted_iota(jnp.int32, (1, LANES), 1) // RANK
    return jnp.where(owner == ids[0, sequence], 1.0, 0.0)


def rms_rows(source, gains, which, target, rows, add=None):
    gain = gains.at[pl.ds(which, 1)]

    @pl.loop(0, rows // 32)
    def _(i):
        at = span(i, 32)
        v = source[at, :].astype(f32)
        out = v * lax.rsqrt(jnp.mean(v * v, axis=-1, keepdims=True) + epsilon) * gain[...]
        if add is not None:
            out = out + add[at, :].astype(f32)
        target[at, :] = out.astype(target.dtype)


def attention_forward_kernel(
    tokens, gains, ids, mix_in, mix_out, heads_hbm, query_out_hbm, kv_out_hbm,
    query_hbm, key_hbm, value_hbm, out_hbm, gate_hbm, up_hbm,
    queries, values_prompt, values_cont, attended, sums, narrow, mixed_out, narrow_mix,
    attn_out_out, middle_out, normed_feed, cosine, sine, masks_out, normed_out, wall_out, out_out, gate_share,
    up_share,
    heads_in, query_out, key_out, value_out, masks, masks_got, attn_out, middle,
    normed_all, wall, wo, kvp, kvc, acc, total, mixed, send, recv, local,
):
    rows, width = tokens.shape
    dp, b, z = lax.axis_index("dp"), lax.axis_index("blk"), lax.axis_index("ulysses")
    planes = lax.axis_size("ulysses")
    x, y, c = dp % 2, b // 2, b % 2
    base = dp - x
    rank = x * 4 + b
    b_c, b_y = b + 1 - 2 * c, (b + 2) % 4
    b_yc = (b_c + 2) % 4
    pc, py, pyc = (dp, b_c, z), (dp, b_y, z), (dp, b_yc, z)
    other = base + 1 - x
    px, pxc, pxy, pxyc = (other, b, z), (other, b_c, z), (other, b_y, z), (other, b_yc, z)
    pz = (dp, b, z + 1 - 2 * (z % 2))
    left, right = (dp, b, z - 1), (dp, b, z + 1)
    depth = query_hbm.shape[0]
    share = gate_share.shape[1]
    part = out_hbm.shape[0]
    copy = sender(send, recv)

    def block(i):
        return span(i, rows)

    def weight_rows(i):
        return pl.ds(pl.multiple_of(i * depth, 16), depth)

    def out_rows(i):
        return span(i, part)

    heads = ((query_hbm, 2 * HEAD, 0), (key_hbm, HEAD, 2 * HEAD), (value_hbm, HEAD, 3 * HEAD))

    def columns_of(ref, target, size):
        return ref.at[:, pl.ds(pl.multiple_of(target * size, 128), size)]

    own_loads = [
        pltpu.make_async_copy(
            columns_of(ref, b, size), wall.at[weight_rows(rank), pl.ds(to, size)], local.at[i]
        )
        for i, (ref, size, to) in enumerate(heads)
    ]
    own_loads.append(pltpu.make_async_copy(out_hbm, wo.at[out_rows(rank)], local.at[3]))
    table_loads = [
        pltpu.make_async_copy(src, dst, local.at[12 + i])
        for i, (src, dst) in enumerate(
            head_table_copies(
                b, heads_hbm, query_out_hbm, kv_out_hbm, heads_in, query_out, key_out, value_out
            )
        )
    ]
    own_rows = [
        pltpu.make_async_copy(
            columns_of(ref, rank, share), out.at[weight_rows(rank)], local.at[4 + i]
        )
        for i, (ref, out) in enumerate(((gate_hbm, gate_share), (up_hbm, up_share)))
    ]
    for cp in own_loads + table_loads:
        cp.start()

    barrier = pltpu.get_barrier_semaphore()
    for peer in (pc, py, pyc, px, pxc, pxy, pxyc) + tuple(
        (dp, b, (z + d) % planes) for d in range(1, planes)
    ):
        pl.semaphore_signal(barrier, inc=1, device_id=peer, device_id_type=MESH)

    rms_rows(tokens, gains, 0, normed_all.at[block(b)], rows)
    masks[...] = jnp.zeros_like(masks)
    for t in range(4):
        masks[t : t + 1, :] = adapter_mask(ids, t, z, planes, rows)
    masks_out[0] = masks[...]
    pl.semaphore_wait(barrier, 6 + planes)

    stage = []
    for j, (peer, pb) in enumerate(((py, b_y), (pyc, b_yc), (pc, b_c))):
        for i, (ref, size, to) in enumerate(heads):
            stage.append(
                copy(
                    3 + 3 * j + i,
                    columns_of(ref, pb, size),
                    wall.at[weight_rows(rank), pl.ds(to, size)],
                    peer,
                )
            )
    token_copies = [
        copy(0, normed_all.at[block(b)], normed_all.at[block(b)], py),
        copy(1, normed_all.at[block(b)], normed_all.at[block(b)], pc),
        copy(2, normed_all.at[block(b_y)], normed_all.at[block(b_y)], pc),
    ]
    across = [
        copy(12 + i, wall.at[weight_rows(x * 4 + o)], wall.at[weight_rows(x * 4 + o)], px)
        for i, o in enumerate((b, b_c, b_y, b_yc))
    ]
    for cp in stage[:3]:
        cp.start()
    for cp in stage[3:]:
        cp.start()
    token_copies[1].start()
    mask_copy = copy(34, masks, masks_got, px)
    mask_copy.start()
    for cp in own_loads[:3]:
        cp.wait()
    across[0].start()
    lane = lax.broadcasted_iota(jnp.int32, (rows, HEAD // 2), 1).astype(f32)
    inverse = jnp.exp(lane * (-2.0 / HEAD * math.log(rope_base)))

    @pl.loop(0, 4)
    def _(t):
        at = block(t)
        token = (t * planes + z) * rows + lax.broadcasted_iota(jnp.int32, (rows, HEAD // 2), 0)
        position = jnp.where(token >= PROMPT, PROMPT + (token - PROMPT) % CONT, token)
        angle = position.astype(f32) * inverse
        cosine[at, :] = jnp.cos(angle)
        sine[at, :] = jnp.sin(angle)

    for cp in stage[6:]:
        cp.wait_recv()
    across[1].start()
    for cp in stage[:3]:
        cp.wait_recv()
    token_copies[0].start()
    across[2].start()
    for cp in stage[3:6]:
        cp.wait_recv()
    across[3].start()
    token_copies[0].wait_recv()
    token_copies[2].start()
    for cp in table_loads:
        cp.wait()
    mask_copy.wait()
    masks_out[1] = masks_got[...]

    half = part // 2
    rx, ry, rxy = (1 - x) * 4 + b, x * 4 + b_y, (1 - x) * 4 + b_y

    def wo_part(r, h):
        return wo.at[pl.ds(pl.multiple_of(r * part + h * half, 16), half)]

    wo_first = [
        (16, wo_part(rank, 0), px),
        (17, wo_part(rank, 1), py),
        (18, wo_part(rank, 1), px),
        (19, wo_part(rank, 0), py),
        (20, wo.at[out_rows(rank)], pc),
    ]
    wo_next = [
        (21, wo_part(rx, 0), py),
        (22, wo_part(ry, 1), px),
        (23, wo.at[out_rows(rx)], pc),
        (24, wo.at[out_rows(ry)], pc),
        (25, wo.at[out_rows(rxy)], pc),
    ]
    wo_first = [copy(i, ref, ref, peer) for i, ref, peer in wo_first]
    wo_next = [copy(i, ref, ref, peer) for i, ref, peer in wo_next]
    swaps = [
        copy(26 + i, columns_of(ref, x * 4 + b_c, share), out.at[weight_rows(rank)], pc)
        for i, (ref, out) in enumerate(((gate_hbm, gate_share), (up_hbm, up_share)))
    ]
    chips = (
        ((px, rx), (pxc, (1 - x) * 4 + b_c)),
        ((py, ry), (pyc, x * 4 + b_yc)),
        ((pxy, rxy), (pxyc, (1 - x) * 4 + b_yc)),
    )
    got_ranks = (
        (1 - x) * 4 + y * 2 + z % 2, x * 4 + (1 - y) * 2 + z % 2, (1 - x) * 4 + (1 - y) * 2 + z % 2,
    )
    direct, relay, whole = {}, {}, []
    for n, targets in enumerate(chips):
        for i, (ref, out) in enumerate(((gate_hbm, gate_share), (up_hbm, up_share))):
            kind = 2 * n + i
            if kind in (0, 2):
                whole += [
                    copy(63 + kind + j, columns_of(ref, pr, share), out.at[weight_rows(rank)], peer)
                    for j, (peer, pr) in enumerate(targets)
                ]
                continue
            direct[kind] = [
                pltpu.make_async_remote_copy(
                    columns_of(ref, pr, share),
                    out.at[weight_rows(rank)],
                    send.at[51 + 2 * kind + j],
                    recv.at[51 + kind],
                    device_id=peer,
                    device_id_type=MESH,
                )
                for j, (peer, pr) in enumerate(targets)
            ]
            got = out.at[weight_rows(got_ranks[n])]
            relay[kind] = copy(28 + kind, got, got, pz)

    def send_direct(kinds):
        @pl.when(c == z % 2)
        def _():
            for kind in kinds:
                for cp in direct[kind]:
                    cp.start()

    def pass_along(kinds):
        for kind in kinds:
            direct[kind][0].wait_recv()
            relay[kind].start()

    own_loads[3].wait()
    for cp in across:
        cp.wait_recv()
    for cp in wo_first:
        cp.start()
    send_direct((4, 5))
    for cp in swaps + own_rows:
        cp.start()
    token_copies[1].wait_recv()
    token_copies[2].wait_recv()

    outs = [
        pltpu.make_async_copy(normed_all, normed_out, local.at[6]),
        pltpu.make_async_copy(wall, wall_out, local.at[7]),
        pltpu.make_async_copy(wo, out_out, local.at[8]),
        pltpu.make_async_copy(kvp, values_prompt, local.at[9]),
        pltpu.make_async_copy(kvc, values_cont, local.at[10]),
        pltpu.make_async_copy(mixed, mixed_out, local.at[11]),
    ]
    outs[0].start()
    outs[1].start()

    half_head = HEAD // 2

    def turned(pre, at, scale):
        cos, sin = cosine[at, :], sine[at, :]
        first, second = pre[:, :half_head], pre[:, half_head:]
        one, two = first * cos - second * sin, second * cos + first * sin
        if scale != 1.0:
            one, two = one * scale, two * scale
        return jnp.concatenate([one, two], axis=1).astype(bf16)

    def keys_values(p):
        at = pl.ds(2 * p * rows, 2 * rows)
        first = lax.broadcasted_iota(jnp.int32, (2 * rows, 3 * LANES), 0) < rows
        both = [jnp.concatenate([masks[pl.ds(2 * p + k, 1), :]] * 3, axis=1) for k in range(2)]
        mask = jnp.where(first, both[0], both[1])
        low = dot_nt(normed_all[at, :], heads_in[...].reshape(3 * LANES, width))
        narrow[at, :] = (low * mask).astype(bf16)
        pre = dot_nn(normed_all[at, :], wall[:, 2 * HEAD : 3 * HEAD]) + dot_nn(
            narrow[at, LANES : 2 * LANES], flat(key_out[...])
        )
        key = turned(pre, at, 1.0)
        value = (
            dot_nn(normed_all[at, :], wall[:, 3 * HEAD :])
            + dot_nn(narrow[at, 2 * LANES :], flat(value_out[...]))
        ).astype(bf16)
        for k in range(2):
            part_rows = slice(k * rows, (k + 1) * rows)
            if p == 0:
                kvp[z, 0, k] = key[part_rows]
                kvp[z, 1, k] = value[part_rows]
            else:
                kvc[0, k] = key[part_rows]
                kvc[1, k] = value[part_rows]

    keys_values(0)
    def hop(direction, d):
        index = 42 + d if direction > 0 else 45 + d
        zz = z - d * direction
        return copy(index, kvp.at[zz], kvp.at[zz], right if direction > 0 else left)

    def pass_on(direction, d):
        reach = z < planes - 1 if direction > 0 else z > 0

        @pl.when(reach)
        def _():
            hop(direction, d).start()

    pass_on(1, 0)
    pass_on(-1, 0)
    keys_values(1)

    @pl.loop(0, 2)
    def _(p):
        at = span(p, 2 * rows)
        for h in range(2):
            lanes = slice(h * HEAD, (h + 1) * HEAD)
            pre = dot_nn(normed_all[at, :], wall[:, lanes]) + dot_nn(
                narrow[at, :LANES], flat(query_out[:, :, lanes])
            )
            got = turned(pre, at, HEAD ** (-0.5))
            for k in range(2):
                queries[2 * p + k, h * rows : (h + 1) * rows, :] = got[k * rows : (k + 1) * rows]

    send_direct((1, 3))
    acc[...] = jnp.zeros_like(acc)
    total[...] = jnp.zeros_like(total)
    row = lax.broadcasted_iota(jnp.int32, (2 * rows, rows), 0) % rows
    causal = lax.broadcasted_iota(jnp.int32, (2 * rows, rows), 1) <= row

    def step(t, k, v, masked):
        e = jnp.exp(soft_cap * jnp.tanh(dot_nt(queries[t], k) * (1.0 / soft_cap)))
        if masked:
            e = jnp.where(causal, e, 0.0)
        some = e[:, :128]
        for n in range(128, rows, 128):
            some = some + e[:, n : n + 128]
        total[t] += some
        acc[t] += dot_nn(e.astype(bf16), v)

    step(0, kvp[z, 0, 0], kvp[z, 1, 0], True)
    step(1, kvp[z, 0, 0], kvp[z, 1, 0], False)
    step(1, kvp[z, 0, 1], kvp[z, 1, 1], True)

    @pl.loop(2, 4)
    def _(t):
        step(t, kvc[0, t - 2], kvc[1, t - 2], True)
        step(t, kvp[z, 0, 0], kvp[z, 1, 0], False)
        step(t, kvp[z, 0, 1], kvp[z, 1, 1], False)

    wo_first[0].wait_recv()
    wo_next[0].start()
    wo_first[1].wait_recv()
    wo_next[1].start()

    @pl.loop(0, 2 * (planes - 1))
    def _(i):
        d = i // 2 + 1
        direction = 1 - 2 * (i % 2)
        zz = z - d * direction

        @pl.when((zz >= 0) & (zz < planes))
        def _():
            index = 42 + 3 * (i % 2) + d - 1
            here = pltpu.make_async_remote_copy(
                kvp.at[zz], kvp.at[zz], send.at[index], recv.at[index], device_id=left,
                device_id_type=MESH,
            )
            here.wait_recv()

            @pl.when((i % 2 == 0) & (z < planes - 1))
            def _():
                pltpu.make_async_remote_copy(
                    kvp.at[zz], kvp.at[zz], send.at[index + 1], recv.at[index + 1],
                    device_id=right, device_id_type=MESH,
                ).start()

            @pl.when((i % 2 == 1) & (z > 0))
            def _():
                pltpu.make_async_remote_copy(
                    kvp.at[zz], kvp.at[zz], send.at[index + 1], recv.at[index + 1],
                    device_id=left, device_id_type=MESH,
                ).start()

            step(1, kvp[zz, 0, 0], kvp[zz, 1, 0], False)

            @pl.when(zz < z)
            def _():
                step(0, kvp[zz, 0, 0], kvp[zz, 1, 0], False)
                step(1, kvp[zz, 0, 1], kvp[zz, 1, 1], False)

            @pl.loop(2, 4)
            def _(t):
                step(t, kvp[zz, 0, 0], kvp[zz, 1, 0], False)
                step(t, kvp[zz, 0, 1], kvp[zz, 1, 1], False)

    outs[3].start()
    outs[4].start()
    ones = jnp.ones((8, 128), f32)

    @pl.loop(0, 4)
    def _(t):
        whole = jnp.sum(total[t], axis=1, keepdims=True)
        got = (acc[t] / whole).astype(bf16)
        attended[t, :, :HEAD] = got[:rows]
        attended[t, :, HEAD:] = got[rows:]
        sums[t] = lax.dot_general(
            ones, total[t], (((1,), (1,)), ((), ())), precision=lax.Precision.HIGHEST,
            preferred_element_type=f32,
        )

    lanes = pl.ds(pl.multiple_of(b * 2 * HEAD, 128), 2 * HEAD)
    mixes = [
        copy(48 + i, attended.at[o], mixed.at[:, lanes], peer)
        for i, (peer, o) in enumerate(((py, b_y), (pyc, b_yc), (pc, b_c)))
    ]
    for cp in mixes:
        cp.start()
    for cp in whole:
        cp.start()
    mixed[:, lanes] = attended[b]
    pass_along((4, 5))
    pass_along((1, 3))
    wo_first[2].wait_recv()
    wo_next[2].start()
    wo_first[3].wait_recv()
    wo_next[3].start()
    wo_next[0].wait_recv()
    wo_next[1].wait_recv()
    wo_next[4].start()
    wo_first[4].wait_recv()
    for cp in wo_next[2:]:
        cp.wait_recv()
    for cp in mixes:
        cp.wait_recv()
    outs[2].start()
    outs[5].start()
    narrow_mix[...] = (dot_nt(mixed[...], mix_in[...]) * masks[pl.ds(b, 1), :]).astype(bf16)

    @pl.loop(0, width // 384)
    def _(n):
        at = span(n, 384)
        attn_out[:, at] = dot_nn(mixed[...], wo[:, at]) + dot_nn(narrow_mix[...], mix_out[:, at])

    rms_rows(attn_out, gains, 1, middle, rows, add=tokens)
    rms_rows(middle, gains, 2, normed_feed, rows)
    attn_out_out[...] = attn_out[...].astype(bf16)
    middle_out[...] = middle[...].astype(bf16)

    for cp in swaps + whole:
        cp.wait()
    for cp in relay.values():
        cp.wait()

    @pl.when(c == z % 2)
    def _():
        for pair in direct.values():
            for cp in pair:
                cp.wait_send()

    for cp in own_rows + outs:
        cp.wait()
    for cp in stage + token_copies + across + wo_first + wo_next + mixes:
        cp.wait_send()

    @pl.loop(0, 2 * (planes - 1))
    def _(i):
        d = i // 2
        direction = 1 - 2 * (i % 2)
        zz = z - d * direction
        onward = z + direction

        @pl.when((zz >= 0) & (zz < planes) & (onward >= 0) & (onward < planes))
        def _():
            index = 42 + 3 * (i % 2) + d
            pltpu.make_async_remote_copy(
                kvp.at[zz], kvp.at[zz], send.at[index], recv.at[index], device_id=left,
                device_id_type=MESH,
            ).wait_send()


def attention_forward(tokens, gains, ids, mix_in, mix_out, tables, weights, share):
    rows, width = tokens.shape
    planes = lax.axis_size("ulysses")
    return pl.pallas_call(
        attention_forward_kernel,
        out_shape=(
            shape((4, 2 * rows, HEAD), bf16),
            shape((planes, 2, 2, rows, HEAD), bf16),
            shape((2, 2, rows, HEAD), bf16),
            shape((4, rows, 2 * HEAD), bf16),
            shape((4, 8, 2 * rows), f32),
            shape((4 * rows, 3 * LANES), bf16),
            shape((rows, 8 * HEAD), bf16),
            shape((rows, LANES), bf16),
            shape((rows, width), bf16),
            shape((rows, width), bf16),
            shape((rows, width), bf16),
            shape((4 * rows, HEAD // 2), f32),
            shape((4 * rows, HEAD // 2), f32),
            shape((2, 16, LANES), f32),
            shape((4 * rows, width), bf16),
            shape((width, 4 * HEAD), bf16),
            shape((8 * HEAD, width), bf16),
            shape((width, share), bf16),
            shape((width, share), bf16),
        ),
        in_specs=[VM, VM, pl.BlockSpec(memory_space=pltpu.SMEM), VM, VM] + [ANY] * 9,
        out_specs=(VM, ANY, ANY, VM, VM, VM, ANY) + (VM,) * 7 + (ANY,) * 5,
        scratch_shapes=head_table_scratch(width)
        + [
            pltpu.VMEM((16, LANES), f32),
            pltpu.VMEM((16, LANES), f32),
            pltpu.VMEM((rows, width), f32),
            pltpu.VMEM((rows, width), f32),
            pltpu.VMEM((4 * rows, width), bf16),
            pltpu.VMEM((width, 4 * HEAD), bf16),
            pltpu.VMEM((8 * HEAD, width), bf16),
            pltpu.VMEM((planes, 2, 2, rows, HEAD), bf16),
            pltpu.VMEM((2, 2, rows, HEAD), bf16),
            pltpu.VMEM((4, 2 * rows, HEAD), f32),
            pltpu.VMEM((4, 2 * rows, 128), f32),
            pltpu.VMEM((rows, 8 * HEAD), bf16),
            pltpu.SemaphoreType.DMA((67,)),
            pltpu.SemaphoreType.DMA((67,)),
            pltpu.SemaphoreType.DMA((18,)),
        ],
        compiler_params=pltpu.CompilerParams(
            collective_id=3, has_side_effects=True, vmem_limit_bytes=62 << 20
        ),
        name="attention_forward",
    )(tokens, gains, ids, mix_in, mix_out, *tables, *weights)


class Places:
    def __init__(self):
        dp, b, z = lax.axis_index("dp"), lax.axis_index("blk"), lax.axis_index("ulysses")
        self.b, self.z, self.planes = b, z, lax.axis_size("ulysses")
        x, c = dp % 2, b % 2
        self.x, self.y, self.c = x, b // 2, c
        self.b_c, self.b_y = b + 1 - 2 * c, (b + 2) % 4
        self.b_yc = (self.b_c + 2) % 4
        other = dp + 1 - 2 * x
        self.dp, self.other = dp, other
        self.pc, self.py, self.pyc = (dp, self.b_c, z), (dp, self.b_y, z), (dp, self.b_yc, z)
        self.px = (other, b, z)
        self.plane = (
            self.pc, self.py, self.pyc, self.px,
            (other, self.b_c, z), (other, self.b_y, z), (other, self.b_yc, z),
        )
        self.rank = x * 4 + b
        self.near = (x * 4 + b, (1 - x) * 4 + b, (1 - x) * 4 + self.b_y, x * 4 + self.b_y)
        self.far = (x * 4 + self.b_c, (1 - x) * 4 + self.b_c, (1 - x) * 4 + self.b_yc, x * 4 + self.b_yc)

    def along(self, d):
        return (self.z + d) % self.planes

    def up(self, d):
        return (self.dp, self.b, self.along(d))


class TableSum:
    COUNT = 6

    def __init__(self, place, copy, first, source, arrived, piece, target, local):
        self.place, self.source, self.arrived, self.piece = place, source, arrived, piece
        n = place.planes
        self.q = piece.shape[0]
        self.out = [
            copy(first + d - 1, source.at[span(place.along(d), self.q)], arrived.at[d - 1], place.up(d))
            for d in range(1, n)
        ]
        self.own = pltpu.make_async_copy(piece, target(place.z), local)
        self.back = [
            copy(first + 2 + d, piece, target(place.z), place.up(d)) for d in range(1, n)
        ]

    def scatter(self):
        for c in self.out:
            c.start()

    def gather(self):
        for c in self.out:
            c.wait_recv()
        got = self.source[span(self.place.z, self.q), :].astype(f32)
        for i in range(self.place.planes - 1):
            got = got + self.arrived[i].astype(f32)
        self.piece[...] = got.astype(bf16)
        self.own.start()
        for c in self.back:
            c.start()

    def ready(self):
        for c in self.back:
            c.wait_recv()
        self.own.wait()

    def finish(self):
        self.ready()
        self.close()

    def close(self):
        for c in self.out + self.back:
            c.wait_send()


class PlaneSpread:
    COUNT = 10

    def __init__(self, place, copy, first, own, gathered):
        half = place.planes // 2
        parts = (pl.ds(0, half), pl.ds(half, half))
        mine, rx, rxy, ry = place.near
        px, py, pc = place.px, place.py, place.pc

        def same(i, ref, peer):
            return copy(first + i, ref, ref, peer)

        def send(i, part, peer):
            return copy(first + i, own.at[part], gathered.at[mine, part], peer)

        self.first = [
            send(0, parts[0], px),
            send(1, parts[1], py),
            send(2, parts[1], px),
            send(3, parts[0], py),
            copy(first + 4, own, gathered.at[mine], pc),
        ]
        self.next = [
            same(5, gathered.at[rx, parts[0]], py),
            same(6, gathered.at[ry, parts[1]], px),
            same(7, gathered.at[rx], pc),
            same(8, gathered.at[ry], pc),
            same(9, gathered.at[rxy], pc),
        ]

    def plane(self):
        for c in self.first:
            c.start()

    def forward(self):
        for i in range(4):
            self.first[i].wait_recv()
            self.next[i].start()

    def corner(self):
        self.next[0].wait_recv()
        self.next[1].wait_recv()
        self.next[4].start()

    def finish(self):
        self.first[4].wait_recv()
        for c in self.next[2:]:
            c.wait_recv()
        for c in self.first + self.next:
            c.wait_send()


class TableSpread:
    COUNT = TableSum.COUNT + PlaneSpread.COUNT

    def __init__(self, place, copy, first, source, arrived, piece, gathered, local):
        own = gathered.at[place.rank]
        self.sum = TableSum(
            place, copy, first, source, arrived, piece, lambda z: gathered.at[place.rank, z], local
        )
        self.spread = PlaneSpread(place, copy, first + TableSum.COUNT, own, gathered)
        self.scatter, self.gather = self.sum.scatter, self.sum.gather
        self.forward, self.corner = self.spread.forward, self.spread.corner

    def plane(self):
        self.sum.ready()
        self.spread.plane()

    def finish(self):
        self.sum.close()
        self.spread.finish()


class TableReduce:
    COUNT = 10

    def __init__(self, place, copy, first, table, part, from_core, from_x, from_y, diag, total, local):
        self.part, self.from_core, self.from_x, self.from_y = part, from_core, from_x, from_y
        self.diag, self.total = diag, total
        m = total.shape[0]
        self.m, self.h = m, m // 2
        h0, h1 = pl.ds(0, self.h), pl.ds(self.h, self.h)
        self.h0, self.h1 = h0, h1
        self.core = [
            copy(first + i, table.at[place.far[i]], from_core.at[i], place.pc) for i in range(4)
        ]
        self.load = [
            pltpu.make_async_copy(table.at[place.near[i]], part.at[i], local(i)) for i in range(4)
        ]
        self.d = [
            copy(first + 4, part.at[2, h0], diag.at[h0], place.px),
            copy(first + 5, part.at[2, h1], diag.at[h1], place.py),
        ]
        self.e = [
            copy(first + 6, part.at[1, h0], from_x.at[h0], place.px),
            copy(first + 7, part.at[3, h1], from_y.at[h1], place.py),
            copy(first + 8, part.at[1, h1], from_x.at[h1], place.px),
            copy(first + 9, part.at[3, h0], from_y.at[h0], place.py),
        ]

    def begin(self):
        for c in self.core + self.load:
            c.start()

    def merge(self):
        for i in (2, 1, 3, 0):
            self.load[i].wait()
            self.core[i].wait_recv()
            add_into(self.part.at[i], self.from_core.at[i], self.m, 16)
            if i == 2:
                self.d[0].start()
                self.d[1].start()
        self.e[0].start()
        self.e[1].start()

    def corner(self):
        self.d[0].wait_recv()
        add_into(self.part.at[3, self.h0], self.diag.at[self.h0], self.h, 16)
        self.e[3].start()
        self.d[1].wait_recv()
        add_into(self.part.at[1, self.h1], self.diag.at[self.h1], self.h, 16)
        self.e[2].start()

    def finish(self):
        for e in self.e:
            e.wait_recv()

        @pl.loop(0, self.m // 16)
        def _(i):
            at = span(i, 16)
            self.total[at, :] = (
                self.part[0, at, :].astype(f32)
                + self.from_x[at, :].astype(f32)
                + self.from_y[at, :].astype(f32)
            ).astype(bf16)

        for c in self.core + self.d + self.e:
            c.wait_send()


def attention_backward_kernel(
    middle, attn_out, cotangent, gains, masks, mixed, narrow_mix, mix_in, mix_out,
    queries, kvp, kvc, attended, sums, narrow, cosine, sine,
    grad_feed_hbm, tokens_hbm, heads_hbm, query_out_hbm, kv_out_hbm, out_hbm, normed_hbm, wall_hbm, feed_hbm, feed_share,
    tokens_grad, g_feed_table, g_feed_share, g_head_table, g_head_share,
    heads_in, query_out, key_out, value_out, wo, wall, grad_attn, grad_mixed,
    g, delta, inv, dq, kv_own, kv_far, kv_send, kv_got, grad_pre, back,
    from_core, from_y,
    feed_table, a_part, a_core, a_x, a_y, a_diag, a_total, a_in, a_piece,
    h_table, h_part, h_core, h_x, h_y, h_diag, h_total, h_in, h_piece,
    o_table, o_got, o_total, o_in, o_piece,
    send, recv, local,
):
    rows, width = tokens_grad.shape
    place = Places()
    b, z, planes = place.b, place.z, place.planes
    copy = sender(send, recv)
    normed_all = wo.at[pl.ds(0, 4 * rows)]
    part = [wo.at[pl.ds((4 + i) * rows, rows)] for i in range(4)]
    own_share = pltpu.make_async_copy(feed_share, g_feed_share.at[place.rank], local.at[0])
    loads = [
        pltpu.make_async_copy(src, dst, local.at[14 + i])
        for i, (src, dst) in enumerate(
            [(out_hbm, wo)]
            + head_table_copies(
                b, heads_hbm, query_out_hbm, kv_out_hbm, heads_in, query_out, key_out, value_out
            )
            + [(wall_hbm, wall), (feed_hbm, feed_table.at[:, pl.ds(0, 3 * RANK)])]
        )
    ]
    grad_feed = from_y
    bring_feed = pltpu.make_async_copy(grad_feed_hbm, grad_feed, local.at[24])
    bring_feed.start()
    late = pltpu.make_async_copy(normed_hbm, normed_all, local.at[1])
    for c in loads:
        c.start()
    own_share.start()
    barrier = pltpu.get_barrier_semaphore()
    peers = list(place.plane) + [place.up(d) for d in range(1, planes)]
    for peer in peers:
        pl.semaphore_signal(barrier, inc=1, device_id=peer, device_id_type=MESH)
    pl.semaphore_wait(barrier, len(peers))

    swaps = []
    for j, (peer, pb) in enumerate(
        ((place.py, place.b_y), (place.pyc, place.b_yc), (place.pc, place.b_c))
    ):
        for h in range(2):
            lanes = pl.ds(pl.multiple_of(pb * 2 * HEAD + h * HEAD, 128), HEAD)
            swaps.append(
                copy(
                    2 * j + h,
                    grad_mixed.at[:, lanes],
                    g.at[b, pl.ds(h * rows, rows)],
                    peer,
                )
            )
    at = 12
    feed_reduce = TableReduce(
        place, copy, at, feed_table, a_part, a_core, a_x, a_y, a_diag, a_total,
        lambda i: local.at[2 + i],
    )
    at += TableReduce.COUNT
    feed_spread = TableSpread(place, copy, at, a_total, a_in, a_piece, g_feed_table, local.at[6])
    at += TableSpread.COUNT
    kv_second = at
    at += 3
    share_spread = PlaneSpread(place, copy, at, feed_share, g_feed_share)
    at += PlaneSpread.COUNT
    head_reduce = TableReduce(
        place, copy, at, h_table, h_part, h_core, h_x, h_y, h_diag, h_total,
        lambda i: local.at[8 + i],
    )
    at += TableReduce.COUNT
    head_spread = TableSpread(place, copy, at, h_total, h_in, h_piece, g_head_table, local.at[12])
    at += TableSpread.COUNT
    out_spread = TableSpread(place, copy, at, o_total, o_in, o_piece, g_head_share, local.at[13])
    at += TableSpread.COUNT
    lanes_half = o_total.shape[0]
    out_swap = copy(
        at, o_table.at[span(1 - place.x, lanes_half)], o_got, place.px
    )

    bring_feed.wait()

    @pl.loop(0, rows // 32)
    def _(i):
        at = span(i, 32)
        grad = cotangent[at, :].astype(f32) + norm_grad(
            middle[at, :].astype(f32), gains[2:3, :], grad_feed[at, :].astype(f32)
        )
        tokens_grad[at, :] = grad
        grad_attn[at, :] = norm_grad(attn_out[at, :].astype(f32), gains[1:2, :], grad).astype(bf16)

    back_mix = (dot_nt(grad_attn[...], mix_out[...]) * masks[0, pl.ds(b, 1), :]).astype(bf16)
    loads[0].wait()
    for j, pb in enumerate((place.b_y, place.b_yc, place.b_c, b)):

        @pl.loop(0, 2)
        def _(h):
            at = span(pb * 2 + h, HEAD)
            grad_mixed[:, at] = (
                dot_nt(grad_attn[...], wo[at, :]) + dot_nn(back_mix, mix_in[:, at])
            ).astype(bf16)

        if j < 3:
            for c in swaps[2 * j : 2 * j + 2]:
                c.start()
    late.start()
    for c in loads[1:]:
        c.wait()
    for n in range(8):
        lanes = slice(n * HEAD, (n + 1) * HEAD)
        got = dot_tn(back_mix, mixed[:, lanes]).astype(bf16)
        for a in range(ADAPTERS):
            h_table[a, 3 * RANK :, lanes] = got[a * RANK : (a + 1) * RANK]
    h_table[:, 3 * RANK :, 8 * HEAD :] = jnp.zeros((ADAPTERS, RANK, width - 8 * HEAD), bf16)

    @pl.loop(0, width // 256)
    def _(n):
        at = span(n, 256)
        got = dot_tn(narrow_mix[...], grad_attn[:, at]).astype(bf16)
        for a in range(ADAPTERS):
            feed_table[a, 3 * RANK :, at] = got[a * RANK : (a + 1) * RANK]

    tokens = grad_attn
    bring_tokens = pltpu.make_async_copy(tokens_hbm, tokens, local.at[23])
    bring_tokens.start()
    feed_reduce.begin()
    for h in range(2):
        lanes = pl.ds(pl.multiple_of(b * 2 * HEAD + h * HEAD, 128), HEAD)
        g[b, h * rows : (h + 1) * rows, :] = grad_mixed[:, lanes]
    for c in swaps:
        c.wait()
    share_spread.plane()

    ones = jnp.ones((8, HEAD), f32)

    @pl.loop(0, 4)
    def _(t):
        for h in range(2):
            at_h = slice(h * rows, (h + 1) * rows)
            lanes = slice(h * HEAD, (h + 1) * HEAD)
            product = g[t, at_h, :].astype(f32) * attended[t, :, lanes].astype(f32)
            delta[t, :, at_h] = lax.dot_general(
                ones, product, (((1,), (1,)), ((), ())), precision=lax.Precision.HIGHEST,
                preferred_element_type=f32,
            )
        inv[t] = 1.0 / sums[t]

    query = lax.broadcasted_iota(jnp.int32, (rows, 2 * rows), 1) % rows
    causal = lax.broadcasted_iota(jnp.int32, (rows, 2 * rows), 0) <= query

    def step(t, k, v, total, slot, masked):
        q, gt = queries[t], g[t]
        th = jnp.tanh(dot_nt(k, q) * (1.0 / soft_cap))
        p = jnp.exp(soft_cap * th) * inv[t, 0:1, :]
        if masked:
            p = jnp.where(causal, p, 0.0)
        total[1, slot] += dot_nn(p.astype(bf16), gt)
        ds = (p * (dot_nt(v, gt) - delta[t, 0:1, :]) * (1.0 - th * th)).astype(bf16)
        total[0, slot] += dot_nn(ds, q)
        dq[t] += dot_tn(ds, k)

    dq[...] = jnp.zeros_like(dq)
    kv_own[...] = jnp.zeros_like(kv_own)

    def kv_copy(d, n):
        index = 6 + d - 1 if n == 0 else kv_second + d - 1
        return copy(index, kv_send.at[d - 1, :, n], kv_got.at[d - 1, :, n], place.up(d))

    @pl.loop(1, planes)
    def _(d):
        zz = (z + d) % planes
        kv_far[...] = jnp.zeros_like(kv_far)
        def ship(n):
            for kind in range(2):
                kv_send[d - 1, kind, n] = kv_far[kind, n].astype(bf16)
            for k in range(1, planes):

                @pl.when(d == k)
                def _(k=k):
                    kv_copy(k, n).start()

        step(1, kvp[zz, 0, 0], kvp[zz, 1, 0], kv_far, 0, False)

        @pl.when(zz < z)
        def _():
            step(0, kvp[zz, 0, 0], kvp[zz, 1, 0], kv_far, 0, False)
            step(1, kvp[zz, 0, 1], kvp[zz, 1, 1], kv_far, 1, False)

        @pl.loop(2, 4)
        def _(t):
            step(t, kvp[zz, 0, 0], kvp[zz, 1, 0], kv_far, 0, False)

        ship(0)

        @pl.loop(2, 4)
        def _(t):
            step(t, kvp[zz, 0, 1], kvp[zz, 1, 1], kv_far, 1, False)

        ship(1)
        for k in range(1, planes):

            @pl.when(d == k)
            def _(k=k):
                if k == 1:
                    feed_reduce.merge()
                if k == 2:
                    feed_reduce.corner()
                    share_spread.forward()
                if k == 3:
                    share_spread.corner()

    feed_reduce.finish()
    step(0, kvp[z, 0, 0], kvp[z, 1, 0], kv_own, 0, True)
    step(1, kvp[z, 0, 0], kvp[z, 1, 0], kv_own, 0, False)
    step(1, kvp[z, 0, 1], kvp[z, 1, 1], kv_own, 1, True)

    @pl.loop(2, 4)
    def _(t):
        step(t, kvc[0, t - 2], kvc[1, t - 2], kv_own, t, True)
        step(t, kvp[z, 0, 0], kvp[z, 1, 0], kv_own, 0, False)
        step(t, kvp[z, 0, 1], kvp[z, 1, 1], kv_own, 1, False)

    late.wait()
    for d in range(1, planes):
        for n in range(2):
            kv_copy(d, n).wait_recv()
        kv_own[:, 0:2] += kv_got[d - 1].astype(f32)
    half_head = HEAD // 2

    @pl.loop(0, 4)
    def _(t):
        at = span(t, rows)
        cos, sin = cosine[at, :], sine[at, :]
        mask = masks[0, pl.ds(t, 1), :]

        def turned(pre, scale):
            first, second = pre[:, :half_head], pre[:, half_head:]
            one, two = first * cos + second * sin, second * cos - first * sin
            if scale != 1.0:
                one, two = one * scale, two * scale
            return jnp.concatenate([one, two], axis=1).astype(bf16)

        for h in range(2):
            grad_pre[at, h * HEAD : (h + 1) * HEAD] = turned(
                dq[t, h * rows : (h + 1) * rows, :], HEAD ** (-0.5)
            )
        grad_pre[at, 2 * HEAD : 3 * HEAD] = turned(kv_own[0, t], 1.0)
        grad_pre[at, 3 * HEAD :] = kv_own[1, t].astype(bf16)
        for i, (lanes, table) in enumerate(
            (
                (slice(0, 2 * HEAD), query_out),
                (slice(2 * HEAD, 3 * HEAD), key_out),
                (slice(3 * HEAD, 4 * HEAD), value_out),
            )
        ):
            back[at, i * LANES : (i + 1) * LANES] = (
                dot_nt(grad_pre[at, lanes], flat(table[...])) * mask
            ).astype(bf16)

    for i, lanes in enumerate(
        (slice(0, 2 * HEAD), slice(2 * HEAD, 3 * HEAD), slice(3 * HEAD, 4 * HEAD))
    ):
        o_table[:, lanes] = dot_tn(
            narrow[:, i * LANES : (i + 1) * LANES], grad_pre[:, lanes]
        ).astype(bf16)
    out_swap.start()

    @pl.loop(0, width // 256)
    def _(n):
        at = span(n, 256)
        got = dot_tn(back[...], normed_all[:, at]).astype(bf16)
        for i in range(3):
            for a in range(ADAPTERS):
                first = i * LANES + a * RANK
                h_table[a, i * RANK : (i + 1) * RANK, at] = got[first : first + RANK]

    head_reduce.begin()
    feed_spread.scatter()

    def project(slot, target):
        at_rows = span(target, rows)

        @pl.loop(0, width // 256)
        def _(n):
            at = span(n, 256)
            part[slot][:, at] = (
                dot_nt(grad_pre[at_rows, :], wall[at, :])
                + dot_nn(back[at_rows, :], heads_in[:, :, :, at].reshape(3 * LANES, 256))
            ).astype(bf16)

    to_core = [copy(9 + i, part[i], from_core.at[i], place.pc) for i in range(2)]
    to_y = copy(11, part[2], from_y, place.py)
    project(0, place.b_yc)
    to_core[0].start()
    head_reduce.merge()
    project(2, place.b_y)
    head_reduce.corner()
    to_core[0].wait_recv()
    add_into(part[2], from_core.at[0], rows)
    to_y.start()
    out_swap.wait_recv()

    @pl.loop(0, lanes_half // 16)
    def _(i):
        at = span(i, 16)
        mine = pl.ds(pl.multiple_of(place.x * lanes_half + i * 16, 16), 16)
        o_total[at, :] = (o_table[mine, :].astype(f32) + o_got[at, :].astype(f32)).astype(bf16)

    feed_spread.gather()
    out_spread.scatter()
    head_reduce.finish()
    head_spread.scatter()
    project(1, place.b_c)
    to_core[1].start()
    feed_spread.plane()
    head_spread.gather()
    out_spread.gather()
    project(3, b)
    head_spread.plane()
    out_spread.plane()
    feed_spread.forward()
    head_spread.forward()
    out_spread.forward()
    to_core[1].wait_recv()
    feed_spread.corner()
    head_spread.corner()
    out_spread.corner()
    to_y.wait_recv()
    bring_tokens.wait()

    @pl.loop(0, rows // 32)
    def _(i):
        at = span(i, 32)
        grad = (
            part[3][at, :].astype(f32)
            + from_core[1, at, :].astype(f32)
            + from_y[at, :].astype(f32)
        )
        tokens_grad[at, :] += norm_grad(tokens[at, :].astype(f32), gains[0:1, :], grad)

    for spread in (share_spread, feed_spread, out_spread, head_spread):
        spread.finish()
    own_share.wait()
    out_swap.wait_send()
    to_y.wait_send()
    for c in to_core:
        c.wait_send()
    for d in range(1, planes):
        for n in range(2):
            kv_copy(d, n).wait_send()


def attention_backward(rows_in, kept, grad_feed, tokens, tables, weights, feed_table, feed_share):
    rows, width = rows_in[0].shape
    planes = lax.axis_size("ulysses")
    m = 4 * RANK
    hm = 4 * RANK
    ow = 4 * HEAD
    om = LANES // 2
    count = 12 + 2 * TableReduce.COUNT + 3 * TableSpread.COUNT + PlaneSpread.COUNT + 4

    def reduce_scratch(m):
        return [
            pltpu.VMEM((ADAPTERS, m, width), bf16),
            pltpu.VMEM((4, m, width), bf16),
            pltpu.VMEM((4, m, width), bf16),
            pltpu.VMEM((m, width), bf16),
            pltpu.VMEM((m, width), bf16),
            pltpu.VMEM((m, width), bf16),
            pltpu.VMEM((m, width), bf16),
        ]

    def spread_scratch(m, w):
        return [
            pltpu.VMEM((planes - 1, m // planes, w), bf16),
            pltpu.VMEM((m // planes, w), bf16),
        ]

    return pl.pallas_call(
        attention_backward_kernel,
        out_shape=(
            shape((rows, width), f32),
            shape((8, planes, m // planes, width), bf16),
            shape((8,) + feed_share.shape, bf16),
            shape((8, planes, hm // planes, width), bf16),
            shape((8, planes, om // planes, ow), bf16),
        ),
        in_specs=[VM] * 17 + [ANY] * 10,
        out_specs=(VM, ANY, ANY, ANY, ANY),
        scratch_shapes=head_table_scratch(width)
        + [
            pltpu.VMEM((8 * HEAD, width), bf16),
            pltpu.VMEM((width, 4 * HEAD), bf16),
            pltpu.VMEM((rows, width), bf16),
            pltpu.VMEM((rows, 8 * HEAD), bf16),
            pltpu.VMEM((4, 2 * rows, HEAD), bf16),
            pltpu.VMEM((4, 8, 2 * rows), f32),
            pltpu.VMEM((4, 8, 2 * rows), f32),
            pltpu.VMEM((4, 2 * rows, HEAD), f32),
            pltpu.VMEM((2, 4, rows, HEAD), f32),
            pltpu.VMEM((2, 2, rows, HEAD), f32),
            pltpu.VMEM((planes - 1, 2, 2, rows, HEAD), bf16),
            pltpu.VMEM((planes - 1, 2, 2, rows, HEAD), bf16),
            pltpu.VMEM((4 * rows, 4 * HEAD), bf16),
            pltpu.VMEM((4 * rows, 3 * LANES), bf16),
            pltpu.VMEM((2, rows, width), bf16),
            pltpu.VMEM((rows, width), bf16),
        ]
        + reduce_scratch(m)
        + spread_scratch(m, width)
        + reduce_scratch(hm)
        + spread_scratch(hm, width)
        + [
            pltpu.VMEM((LANES, ow), bf16),
            pltpu.VMEM((om, ow), bf16),
            pltpu.VMEM((om, ow), bf16),
        ]
        + spread_scratch(om, ow)
        + [
            pltpu.SemaphoreType.DMA((count,)),
            pltpu.SemaphoreType.DMA((count,)),
            pltpu.SemaphoreType.DMA((25,)),
        ],
        compiler_params=pltpu.CompilerParams(
            collective_id=4, has_side_effects=True, vmem_limit_bytes=63 << 20
        ),
        name="attention_backward",
    )(*rows_in, *kept, grad_feed, tokens, *tables, *weights, feed_table, feed_share)


def lay_out_kernel(
    feed_rows, feed_columns, head_rows, head_columns,
    heads_in, query_out, kv_out, t_mix_in, t_mix_out, feed_in, feed_out, t_down_in, t_down_out,
):
    rows = feed_rows[0]
    feed_in[0, 0] = rows[0].astype(f32)
    feed_in[0, 1] = rows[1].astype(f32)
    t_down_out[0] = rows[2].astype(f32)
    t_mix_out[0] = rows[3].astype(f32)
    rows = head_rows[0]
    for i in range(3):
        heads_in[0, i] = rows[i].astype(f32)
    t_mix_in[0] = rows[3, :, : t_mix_in.shape[2]].astype(f32)
    share = feed_out.shape[3]
    table = feed_columns[0].reshape(3, ADAPTERS, RANK, share)
    for a in range(ADAPTERS):
        feed_out[a, 0] = table[0, a].astype(f32)
        feed_out[a, 1] = table[1, a].astype(f32)
        t_down_in[a] = table[2, a].astype(f32)
    for a in range(head_columns.shape[1]):
        got = head_columns[0, a].astype(f32)
        query_out[a] = got[:, : 2 * HEAD]
        kv_out[a, 0] = got[:, 2 * HEAD : 3 * HEAD]
        kv_out[a, 1] = got[:, 3 * HEAD :]


def lay_out(feed_rows, feed_columns, head_rows, head_columns):
    planes, _, width = feed_rows.shape[1:]
    share = feed_columns.shape[3]
    ff = 8 * share

    def whole(array):
        return pl.BlockSpec((1,) + array.shape[1:], lambda r: (r, 0, 0, 0))

    return pl.pallas_call(
        lay_out_kernel,
        grid=(8,),
        out_shape=(
            shape((ADAPTERS, 3, RANK, width), f32),
            shape((ADAPTERS, RANK, 8 * HEAD), f32),
            shape((ADAPTERS, 2, RANK, 4 * HEAD), f32),
            shape((ADAPTERS, RANK, 8 * HEAD), f32),
            shape((ADAPTERS, RANK, width), f32),
            shape((ADAPTERS, 2, RANK, width), f32),
            shape((ADAPTERS, 2, RANK, ff), f32),
            shape((ADAPTERS, RANK, ff), f32),
            shape((ADAPTERS, RANK, width), f32),
        ),
        in_specs=[whole(x) for x in (feed_rows, feed_columns, head_rows, head_columns)],
        out_specs=(
            pl.BlockSpec((1, 3, RANK, width), lambda r: (r, 0, 0, 0)),
            pl.BlockSpec((planes, RANK, 2 * HEAD), lambda r: (r // 4, 0, r % 4)),
            pl.BlockSpec((planes, 2, RANK, HEAD), lambda r: (r // 4, 0, 0, r % 4)),
            pl.BlockSpec((1, RANK, 8 * HEAD), lambda r: (r, 0, 0)),
            pl.BlockSpec((1, RANK, width), lambda r: (r, 0, 0)),
            pl.BlockSpec((1, 2, RANK, width), lambda r: (r, 0, 0, 0)),
            pl.BlockSpec((ADAPTERS, 2, RANK, share), lambda r: (0, 0, 0, r)),
            pl.BlockSpec((ADAPTERS, RANK, share), lambda r: (0, 0, r)),
            pl.BlockSpec((1, RANK, width), lambda r: (r, 0, 0)),
        ),
        compiler_params=pltpu.CompilerParams(vmem_limit_bytes=62 << 20),
        name="lay_out",
    )(feed_rows, feed_columns, head_rows, head_columns)


def shards(
    tokens,
    query_weight,
    key_projection,
    value_projection,
    out_weight,
    gate_weight,
    up_weight,
    down_weight,
    attn_in_gain,
    attn_out_gain,
    feed_in_gain,
    feed_out_gain,
    adapt_heads_in,
    adapt_query_out,
    adapter_key_value_second,
    adapt_mix_in,
    adapt_mix_out,
    adapt_feed_in,
    adapt_feed_out,
    adapt_down_in,
    adapt_down_out,
    adapter_ids,
    cotangent,
):
    width = tokens.shape[1]
    blk_n = lax.axis_size("blk")
    dp_n = lax.axis_size("dp")
    rank = lax.axis_index("dp") % 2 * blk_n + lax.axis_index("blk")
    ff = gate_weight.shape[1]
    share = ff // (2 * blk_n)
    weights = (
        query_weight, key_projection, value_projection, out_weight, gate_weight, up_weight,
        down_weight,
    )
    if dp_n > 2:
        weights = tuple(
            lax.dynamic_slice_in_dim(
                lax.all_gather(weight, PLANE, axis=0, tiled=True),
                rank * (weight.shape[0] * dp_n // 2),
                weight.shape[0] * dp_n // 2,
            )
            for weight in weights
        )
    down_rows = weights[6]
    gains = jnp.concatenate([attn_in_gain, attn_out_gain, feed_in_gain, feed_out_gain]).reshape(4, -1)
    mix_in, mix_out, down_out = flat(adapt_mix_in), flat(adapt_mix_out), flat(adapt_down_out)
    head_tables = (adapt_heads_in, adapt_query_out, adapter_key_value_second)
    feed_tables = (adapt_feed_in, adapt_feed_out, adapt_down_in)
    (
        queries, kvp, kvc, attended, exp_sum, narrow_heads, mixed, narrow_mix, attn_out, middle,
        normed_feed, cosine, sine, masks, normed_all, head_weight, out_full, gate_share, up_share,
    ) = attention_forward(
        tokens, gains, adapter_ids, mix_in, mix_out, head_tables, weights[:6], share
    )
    layer_out, grad_branch, narrow_feed, feed_all, gate_up = feed_forward(
        normed_feed, middle, cotangent, gains, masks, down_out, feed_tables, gate_share, up_share,
        down_rows,
    )
    grad_feed, feed_table, share_sum = feed_backward(
        grad_branch, masks, down_out, narrow_feed, feed_tables, gate_share, up_share, down_rows,
        gate_up, feed_all,
    )
    tokens_grad, feed_rows, feed_columns, head_rows, head_columns = attention_backward(
        (
            middle, attn_out, cotangent, gains, masks, mixed, narrow_mix, mix_in, mix_out,
        ),
        (queries, kvp, kvc, attended, exp_sum, narrow_heads, cosine, sine),
        grad_feed,
        tokens,
        head_tables,
        (out_full, normed_all, head_weight),
        feed_table,
        share_sum,
    )

    summed = lay_out(feed_rows, feed_columns, head_rows, head_columns)
    if dp_n > 2:
        summed = tuple(lax.psum(table * 0.5, "dp") for table in summed)
    return (layer_out, tokens_grad) + summed


def solution(mesh):
    sharded = P(EVERY, None)
    rowwise = P(PLANE, None)
    placed = (
        (sharded,) + (rowwise,) * 7 + (P(),) * 13 + (P("dp", None), sharded)
    )
    return jax.shard_map(
        shards,
        mesh=mesh,
        in_specs=placed,
        out_specs=(sharded, sharded) + (P(),) * 9,
        check_vma=False,
    )
```
